128 devices in a mesh: dp: 8 (over y, z_hi), seq: 2 (over core), tensor: 8 (over z_lo, x).
Axes of the slice: x: 4, y: 4, z: 4 (z_hi: 2, z_lo: 2; z = z_hi * 2 + z_lo), core: 2. Of those that a mesh axis runs over, the one named last changes fastest.
Arguments:
- inputs: bfloat16 [24, 512, 1152], P('dp', 'seq'), may hold values from -6 to 6
- picture_ids: int32 [24, 512], P('dp', 'seq'), may hold values from -1 to 3, as said below
- cotangent: bfloat16 [24, 512, 1152], P('dp', 'seq'), may hold values from -6 to 6
- norm_gain: float32 [2, 2, 1152], replicated, may hold values from 0.5 to 1.5
- norm_bias: float32 [2, 2, 1152], replicated, may hold values from -1.75 to 1.75
- w_qkv: bfloat16 [2, 3, 1152, 1152], P(None, None, None, 'tensor'), may hold values from -0.1875 to 0.1875
- q_bias: float32 [2, 1152], P(None, 'tensor'), may hold values from -1.75 to 1.75
- v_bias: float32 [2, 1152], P(None, 'tensor'), may hold values from -0.3125 to 0.3125
- w_out: bfloat16 [2, 1152, 1152], P(None, 'tensor'), may hold values from -3 to 3
- out_bias: float32 [2, 1152], replicated, may hold values from -1.75 to 1.75
- w_up: bfloat16 [2, 1152, 4304], P(None, None, 'tensor'), may hold values from -0.1875 to 0.1875
- up_bias: float32 [2, 4304], P(None, 'tensor'), may hold values from -3 to 3
- w_down: bfloat16 [2, 4304, 1152], P(None, 'tensor'), may hold values from -0.125 to 0.125
- down_bias: float32 [2, 1152], replicated, may hold values from -1.75 to 1.75
Outputs:
- outputs: bfloat16 [24, 512, 1152], P('dp', 'seq')
- input_grad: float32 [24, 512, 1152], P('dp', 'seq')
- norm_gain_grad: float32 [2, 2, 1152], replicated
- norm_bias_grad: float32 [2, 2, 1152], replicated
- w_qkv_grad: float32 [2, 3, 1152, 1152], P(None, None, None, 'tensor')
- q_bias_grad: float32 [2, 1152], P(None, 'tensor')
- v_bias_grad: float32 [2, 1152], P(None, 'tensor')
- w_out_grad: float32 [2, 1152, 1152], P(None, 'tensor')
- out_bias_grad: float32 [2, 1152], replicated
- w_up_grad: float32 [2, 1152, 4304], P(None, None, 'tensor')
- up_bias_grad: float32 [2, 4304], P(None, 'tensor')
- w_down_grad: float32 [2, 4304, 1152], P(None, 'tensor')
- down_bias_grad: float32 [2, 1152], replicated
The draws below stay inside these ranges and needn't reach their ends.
Inputs may be any that keep to these rules, and one draw needn't show every extreme that they name: `picture_ids`: in each row the slots hold pictures numbered 0, 1, 2, 3 in this order, each a run of consecutive slots, followed by 1 to 64 pad slots of -1; picture 2 covers the slots 512 // 4 to 383 and more.
All inputs are finite; a program needn't handle non-finite values.
Results may differ from the reference program's by a relative error of at most 0.025.
Values may be sent and summed in bfloat16 or wider, within the bound.
No kernel may reach another device: no remote copies, remote signals or barrier semaphores. Data moves between devices by JAX's collectives and lax.ppermute only.
A program may use at most 192 MiB of HBM per device.

```python
import jax
import jax.numpy as jnp
from jax import lax

D = 1152
HEADS = 16
HEAD_DIM = 72
FF = 4304
TOK_DEV = 256
LAYERS = 2
ROW = 512
ROWS = 24
N_TENSOR = 8


def draw_picture_ids(key, part):
    key = jax.random.fold_in(key, 11)
    first_key, second_key, third_key, pad_key = jax.random.split(key, 4)
    eighth = ROW // 8
    first_cut = jax.random.randint(first_key, (ROWS, 1), 1, eighth + 1)
    second_cut = jax.random.randint(second_key, (ROWS, 1), eighth + 1, ROW // 4 + 1)
    third_cut = jax.random.randint(third_key, (ROWS, 1), 3 * ROW // 4, 7 * ROW // 8)
    pad_count = jax.random.randint(pad_key, (ROWS, 1), 1, eighth + 1)
    place = jnp.arange(ROW, dtype=jnp.int32)[None, :]
    numbers = (place >= first_cut).astype(jnp.int32) + (place >= second_cut).astype(jnp.int32) + (place >= third_cut).astype(jnp.int32)
    return jnp.where(place >= ROW - pad_count, -1, numbers).astype(jnp.int32)


def level_of(own_key, shape, cuts, least, high):
    level = 1.0
    for dim, shards_of in cuts:
        steps = jax.random.uniform(jax.random.fold_in(jax.random.fold_in(own_key, 6), dim), (shards_of,), jnp.float32, least / len(cuts), high / len(cuts))
        level = level * jnp.repeat(jnp.exp(steps), shape[dim] // shards_of).reshape((-1,) + (1,) * (len(shape) - 1 - dim))
    return level


def scatter_about(own_key, dims, spread, reach, pieces=(), kind=jnp.bfloat16):
    gain = level_of(own_key, dims, pieces, -0.22, 0.18) if pieces else 1.0
    values = jax.random.normal(own_key, dims, jnp.float32) * spread * gain
    return jnp.minimum(jnp.maximum(values, -reach), reach).astype(kind)


def setup_inputs(seed: int = 0) -> dict:
    keys = jax.random.split(jax.random.key(seed), 15)
    inputs = scatter_about(keys[0], (ROWS, ROW, D), 1.0, 6.0, ((0, 8), (1, 2)))
    picture_ids = draw_picture_ids(jax.random.fold_in(keys[14], 71), 0)
    cotangent = scatter_about(keys[2], (ROWS, ROW, D), 1.0, 6.0, ((0, 8), (1, 2)))
    norm_gain = jnp.clip(1.0 + 0.1 * jax.random.normal(keys[3], (LAYERS, 2, D), jnp.float32), 0.5, 1.5)
    norm_bias = scatter_about(keys[4], (LAYERS, 2, D), 0.3, 1.75, (), jnp.float32)
    w_qkv = scatter_about(keys[5], (LAYERS, 3, D, D), D ** -0.5, 0.1875, ((3, 8),))
    q_bias = scatter_about(keys[6], (LAYERS, D), 0.3, 1.75, ((1, 8),), jnp.float32)
    v_bias = scatter_about(keys[7], (LAYERS, D), 0.05, 0.3125, ((1, 8),), jnp.float32)
    w_out = scatter_about(keys[8], (LAYERS, D, D), (max(D // TOK_DEV, 1)) ** -0.5, 3.0, ((1, 8),))
    out_bias = scatter_about(keys[9], (LAYERS, D), 0.3, 1.75, (), jnp.float32)
    w_up = scatter_about(keys[10], (LAYERS, D, FF), D ** -0.5, 0.1875, ((2, 8),))
    up_bias = scatter_about(keys[11], (LAYERS, FF), 0.5, 3.0, ((1, 8),), jnp.float32)
    w_down = scatter_about(keys[12], (LAYERS, FF, D), (FF // 2) ** -0.5, 0.125, ((1, 8),))
    down_bias = scatter_about(keys[13], (LAYERS, D), 0.3, 1.75, (), jnp.float32)
    return dict(inputs=inputs, picture_ids=picture_ids, cotangent=cotangent, norm_gain=norm_gain, norm_bias=norm_bias, w_qkv=w_qkv, q_bias=q_bias, v_bias=v_bias, w_out=w_out, out_bias=out_bias, w_up=w_up, up_bias=up_bias, w_down=w_down, down_bias=down_bias)


@jax.custom_vjp
def low(v):
    return lax.optimization_barrier(v.astype(jnp.bfloat16)).astype(jnp.float32)

@jax.custom_vjp
def low_back(v):
    return v

def low_keep(v):
    return (low(v), None)

def low_pass(kept, grad):
    return (grad,)

def back_keep(v):
    return (v, None)

def back_low(kept, grad):
    return (low(grad),)
low.defvjp(low_keep, low_pass)
low_back.defvjp(back_keep, back_low)
highest = lax.Precision.HIGHEST
norm_eps = 1e-06
gelu_coef = 0.7978845608028654

def normalize(stream, weight_gain, weight_shift):
    row_mean = lax.optimization_barrier(jnp.mean(stream, axis=-1, keepdims=True))
    centred = stream - row_mean
    row_var = lax.optimization_barrier(jnp.mean(centred * centred, axis=-1, keepdims=True))
    return centred * lax.rsqrt(row_var + norm_eps) * weight_gain + weight_shift

def gelu_tanh(stream):
    return 0.5 * stream * (1.0 + jnp.tanh(gelu_coef * (stream + 0.044715 * stream * stream * stream)))

def group_sum(left, right):
    groups = N_TENSOR
    parts = jnp.einsum('tgc,gcd->gtd', left.reshape(left.shape[0], groups, -1), right.reshape(groups, -1, right.shape[1]), precision=highest)
    return lax.optimization_barrier(jnp.sum(low(parts), axis=0))

def encoder_layer(stream, slot_ids, params):
    gains, shifts, w_qkv, q_bias, v_bias, w_out, out_bias, w_up, up_bias, w_down, down_bias = params
    normed = low(normalize(stream, gains[0], shifts[0]))
    query = low(low_back(jnp.dot(normed, w_qkv[0], precision=highest) + q_bias))
    key_proj = low(low_back(jnp.dot(normed, w_qkv[1], precision=highest)))
    value_proj = low(low_back(jnp.dot(normed, w_qkv[2], precision=highest) + v_bias))
    query_heads = query.reshape(ROW, HEADS, HEAD_DIM)
    key_heads = key_proj.reshape(ROW, HEADS, HEAD_DIM)
    value_heads = value_proj.reshape(ROW, HEADS, HEAD_DIM)
    raw_scores = jnp.einsum('qhd,khd->hqk', query_heads, key_heads, precision=highest)
    allowed = (slot_ids[None, :] >= 0) & ((slot_ids[:, None] == slot_ids[None, :]) | (slot_ids[:, None] < 0))
    scores = jnp.where(allowed[None], low_back(raw_scores) * HEAD_DIM ** (-0.5), -1e+30)
    probs = low(jax.nn.softmax(scores, axis=-1))
    mixed_heads = jnp.einsum('hqk,khd->qhd', probs, value_heads, precision=highest)
    mixed = low(low_back(mixed_heads.reshape(ROW, D)))
    after_attn = stream + low_back(group_sum(mixed, w_out)) + out_bias
    normed_two = low(normalize(after_attn, gains[1], shifts[1]))
    up_proj = low_back(jnp.dot(normed_two, w_up, precision=highest) + up_bias)
    activated = low(gelu_tanh(up_proj))
    return after_attn + low_back(group_sum(activated, w_down)) + down_bias

def reference(inputs, picture_ids, cotangent, norm_gain, norm_bias, w_qkv, q_bias, v_bias, w_out, out_bias, w_up, up_bias, w_down, down_bias):
    weights = (norm_gain, norm_bias, w_qkv.astype(jnp.float32), q_bias, v_bias, w_out.astype(jnp.float32), out_bias, w_up.astype(jnp.float32), up_bias, w_down.astype(jnp.float32), down_bias)
    layers = norm_gain.shape[0]

    def forward(stream_all, weight_set):

        def one_row(row_pair):
            stream, slot_ids = row_pair
            for layer_index in range(layers):
                stream = encoder_layer(stream, slot_ids, tuple((item[layer_index] for item in weight_set)))
            return stream
        return lax.map(jax.checkpoint(one_row), (stream_all, picture_ids))
    result, pullback = jax.vjp(forward, inputs.astype(jnp.float32), weights)
    seed_grad = cotangent.astype(jnp.float32) * (picture_ids >= 0)[..., None].astype(jnp.float32)
    input_grad, weight_grads = pullback(seed_grad)
    return (result.astype(jnp.bfloat16), input_grad, weight_grads[0], weight_grads[1], weight_grads[2], weight_grads[3], weight_grads[4], weight_grads[5], weight_grads[6], weight_grads[7], weight_grads[8], weight_grads[9], weight_grads[10])
```

```python
import functools

import jax
import jax.numpy as jnp
from jax import lax
from jax.experimental import pallas as pl
from jax.experimental.pallas import tpu as pltpu
from jax.sharding import Mesh
from jax.sharding import PartitionSpec as P

HEAD_DIM = 72
SCALE = HEAD_DIM**-0.5
D = 1152
CW = 144
FW = 538
FP = 576
NA = 256
NB = 128
NT = NA + NB
CA = NA // 4
CB = NB // 4
EXTRA = 8
norm_eps = 1e-06
gelu_coef = 0.7978845608028654
bf16 = jnp.bfloat16
f32 = jnp.float32
SIZES = {"y": 4, "x": 4, "c": 2, "zl": 2, ("zh", "zl"): 4}
Z = ("zh", "zl")
VMEM_LIMIT = 50 * 1024 * 1024


def shift(value, axis, by):
    n = SIZES[axis]
    return lax.ppermute(value, axis, [(i, (i + by) % n) for i in range(n)])


def dot(a, b):
    return lax.dot_general(a, b, (((1,), (0,)), ((), ())), preferred_element_type=f32)


def dot_nt(a, b):
    return lax.dot_general(a, b, (((1,), (1,)), ((), ())), preferred_element_type=f32)


def dot_tn(a, b):
    return lax.dot_general(a, b, (((0,), (0,)), ((), ())), preferred_element_type=f32)


def after(value, anchor):
    return lax.optimization_barrier((value, anchor))[0]


def shaped(shape, dtype):
    return jax.ShapeDtypeStruct(shape, dtype)


CHUNK = CA + CB
SENDS = [shaped((CHUNK, D), bf16)] * 3 + [shaped((CHUNK, D), f32)]


def call(kernel, outs, *args, pos=None):
    specs = [pl.BlockSpec(memory_space=pltpu.VMEM)] * len(args)
    if pos is not None:
        specs = [pl.BlockSpec(memory_space=pltpu.SMEM)] + specs
        args = (pos, *args)
    return pl.pallas_call(
        kernel,
        out_shape=outs,
        in_specs=specs,
        out_specs=[pl.BlockSpec(memory_space=pltpu.VMEM)] * len(outs),
        compiler_params=pltpu.CompilerParams(vmem_limit_bytes=VMEM_LIMIT),
    )(*args)


def whole(chunks):
    if len(chunks) == 1:
        return chunks[0][...]
    return jnp.concatenate([r[:CA] for r in chunks] + [r[CA:] for r in chunks], axis=0)


def put_sends(total, outs):
    for k in range(4):
        ref = outs[k - 1]
        ref[:CA] = total[CA * k : CA * (k + 1)].astype(ref.dtype)
        ref[CA:] = total[NA + CB * k : NA + CB * (k + 1)].astype(ref.dtype)


def ids_kernel(pos, near, far, qid_a, kid_a, qid_b, kid_b):
    first = pos[0] == 0
    x = pos[1]

    def turned(row, n):
        rows = jnp.broadcast_to(row, (8, n))
        return pltpu.roll(rows, (n - x * (n // 4)) % n, axis=1)

    def half(ref):
        return turned(jnp.where(first, ref[0:1], ref[1:2]), NA)

    def quarter(ref, own):
        low, high = ref[2:3, :NB], ref[2:3, NB:]
        return turned(jnp.where(first == own, low, high), NB)

    a, b = half(near), quarter(near, True)
    qid_a[...] = a.astype(f32).T.astype(jnp.int32)
    qid_b[...] = b.astype(f32).T.astype(jnp.int32)
    kid_a[...] = jnp.concatenate([a, half(far)], axis=1)
    kid_b[...] = jnp.concatenate(
        [b, quarter(far, True), quarter(near, False), quarter(far, False)], axis=1
    )


def arrange_ids(pos, near, far):
    i32 = jnp.int32
    outs = [shaped((NA, 8), i32), shaped((8, 2 * NA), i32)]
    outs += [shaped((NB, 8), i32), shaped((8, 4 * NB), i32)]
    return call(ids_kernel, outs, near, far, pos=pos)


def arranged(pos, ref):
    zl, x = pos[0], pos[1]
    rows, quarters = [], []
    for k in range(4):
        a = lax.rem(x + k, 4)
        rows.append(ref[zl, pl.ds(pl.multiple_of(a * CA, CA), CA)])
        quarters.append(ref[2, pl.ds(pl.multiple_of(zl * NB + a * CB, CB), CB)])
    return jnp.concatenate(rows + quarters, axis=0)


def first_kernel(pos, inputs, gain, bias, normed, stream):
    v = arranged(pos, inputs).astype(f32)
    stream[:CA] = v[:CA]
    stream[CA:] = v[NA : NA + CB]
    mean = jnp.mean(v, axis=-1, keepdims=True)
    centred = v - mean
    var = jnp.mean(centred * centred, axis=-1, keepdims=True)
    out = centred * lax.rsqrt(var + norm_eps) * gain[0, 0:1] + bias[0, 0:1]
    normed[...] = out.astype(bf16)


def cotangent_kernel(pos, cotangent, qid_a, qid_b, low, grad, total):
    live = jnp.concatenate([qid_a[...], qid_b[...]], axis=0)[:, :1] >= 0
    v = jnp.where(live, arranged(pos, cotangent).astype(f32), 0.0)
    low[...] = v.astype(bf16)
    own = jnp.concatenate([v[:CA], v[NA : NA + CB]], axis=0)
    grad[...] = own
    total[...] = jnp.sum(own, axis=0, keepdims=True)


def place_kernel(pos, *refs):
    out = refs[8]
    for dz in range(2):
        zl = pos[0] if dz == 0 else 1 - pos[0]
        for k in range(4):
            a = lax.rem(pos[1] + k, 4)
            chunk = refs[dz * 4 + k]
            out[zl, pl.ds(pl.multiple_of(a * CA, CA), CA)] = chunk[:CA].astype(out.dtype)
            out[2, pl.ds(pl.multiple_of(zl * NB + a * CB, CB), CB)] = chunk[CA:].astype(out.dtype)


def placed_rows(pos, slots, dtype):
    return call(place_kernel, [shaped((3, NA, D), dtype)], *slots, pos=pos)[0]


def norm_kernel(layer, at, stream, own, r1, r2, r3, extra, gain, bias, x_out, n_out):
    x = stream[...] + (own[...] + r1[...].astype(f32) + r2[...].astype(f32) + r3[...].astype(f32))
    x = x + extra[layer : layer + 1]
    x_out[...] = x
    mean = jnp.mean(x, axis=-1, keepdims=True)
    centred = x - mean
    var = jnp.mean(centred * centred, axis=-1, keepdims=True)
    g, b = (ref[at[0], at[1] : at[1] + 1] for ref in (gain, bias))
    n_out[...] = (centred * lax.rsqrt(var + norm_eps) * g + b).astype(bf16)


def norm_step(layer, at, stream, got, extra, gain, bias):
    return call(
        functools.partial(norm_kernel, layer, at),
        [shaped((CHUNK, D), f32), shaped((CHUNK, D), bf16)],
        stream, *got, extra, gain, bias,
    )


def result_kernel(layer, stream, own, r1, r2, r3, extra, out):
    x = stream[...] + (own[...] + r1[...].astype(f32) + r2[...].astype(f32) + r3[...].astype(f32))
    out[...] = (x + extra[layer : layer + 1]).astype(bf16)


def norm_back_kernel(at, x_ref, own, r1, r2, r3, grad_ref, gain, out, low, sums):
    x = x_ref[...]
    d = own[...] + r1[...].astype(f32) + r2[...].astype(f32) + r3[...].astype(f32)
    mean = jnp.mean(x, axis=-1, keepdims=True)
    centred = x - mean
    var = jnp.mean(centred * centred, axis=-1, keepdims=True)
    r = lax.rsqrt(var + norm_eps)
    xh = centred * r
    e = d * gain[at[0], at[1] : at[1] + 1]
    inner = e - jnp.mean(e, axis=-1, keepdims=True)
    inner = inner - xh * jnp.mean(e * xh, axis=-1, keepdims=True)
    grad = grad_ref[...] + r * inner
    out[...] = grad
    low[...] = grad.astype(bf16)
    sums[0:1] = jnp.sum(d * xh, axis=0, keepdims=True)
    sums[1:2] = jnp.sum(d, axis=0, keepdims=True)
    sums[2:3] = jnp.sum(grad, axis=0, keepdims=True)


def norm_back(at, x, got, grad, gain):
    return call(
        functools.partial(norm_back_kernel, at),
        [shaped((CHUNK, D), f32), shaped((CHUNK, D), bf16), shaped((3, D), f32)],
        x, *got, grad, gain,
    )


def qkv_kernel(layer, n, *refs):
    chunks, (w0, wa, wb, qb0, qb1, vb0, vb1) = refs[:n], refs[n : n + 7]
    q_out, kv_out, part_out = refs[n + 7 : n + 10]
    nt = whole(chunks)
    if n > 1:
        refs[n + 10][...] = nt
    w1 = jnp.concatenate([wa[...], wb[...]], axis=0)
    for g, w, qb, vb in ((0, w0[...], qb0, vb0), (1, w1, qb1, vb1)):
        q_out[g] = (dot_nt(nt, w[:CW]) + qb[layer : layer + 1]).astype(bf16)
        key = dot_nt(w[CW : 2 * CW], nt).astype(bf16)
        value = (dot_nt(nt, w[2 * CW :]) + vb[layer : layer + 1]).T.astype(bf16)
        kv_out[g, 0] = key
        kv_out[g, 1] = value
        part_out[1 - g, 0] = key[:, NA:]
        part_out[1 - g, 1] = value[:, NA:]


def project(layer, chunks, own, far, biases):
    n = len(chunks)
    outs = [shaped((2, NT, CW), bf16), shaped((2, 2, CW, NT), bf16), shaped((2, 2, CW, NB), bf16)]
    if n > 1:
        outs.append(shaped((NT, D), bf16))
    got = call(functools.partial(qkv_kernel, layer, n), outs, *chunks, own, *far, *biases)
    return (*got[:3], got[3] if n > 1 else chunks[0])


def lane_mask(head):
    lane = lax.broadcasted_iota(jnp.int32, (1, CW), 1)
    return (lane < HEAD_DIM) if head == 0 else (lane >= HEAD_DIM)


def row_mask(head):
    place = lax.broadcasted_iota(jnp.int32, (CW, 1), 0)
    return (place < HEAD_DIM) if head == 0 else (place >= HEAD_DIM)


def masked(mask, value):
    return jnp.where(mask, value.astype(f32), 0.0).astype(bf16)


def probabilities(qm, keys, allowed):
    scores = jnp.where(allowed, dot(qm, keys) * SCALE, -1e30)
    expanded = jnp.exp(scores - jnp.max(scores, axis=-1, keepdims=True))
    return expanded / jnp.sum(expanded, axis=-1, keepdims=True)


def slot_mask(qid, kid):
    return (kid >= 0) & ((qid == kid) | (qid < 0))


def attend_kernel(first, count, blocks, *refs):
    n = len(blocks)
    q, kvs, (qid, kid, wo0, wo1) = refs[0], refs[1 : 1 + n], refs[1 + n : 5 + n]
    rest = refs[5 + n :]
    allowed = slot_mask(qid[:, :1], kid[:1])
    mixed_out = rest[0] if first == 0 else rest[1]
    total = None
    for g, wo in ((0, wo0), (1, wo1)):
        keys = jnp.concatenate([r[g, 0, :, b : b + m] for r, (b, m) in zip(kvs, blocks)], axis=1)
        values = jnp.concatenate([r[g, 1, :, b : b + m] for r, (b, m) in zip(kvs, blocks)], axis=1)
        query = q[g, first : first + count]
        mixed = None
        for head in range(2):
            mask = lane_mask(head)
            probs = probabilities(masked(mask, query), keys, allowed).astype(bf16)
            got = dot_nt(probs, values)
            mixed = got if head == 0 else jnp.where(mask, got, mixed)
        mixed = mixed.astype(bf16)
        mixed_out[g] = mixed
        part = dot(mixed, wo[...])
        total = part if total is None else total + part
    if first == 0:
        rest[1][...] = total
    else:
        put_sends(jnp.concatenate([rest[0][...], total], axis=0), rest[2:])


def attend_row(q, kvs, blocks, qid, kid, wo):
    return call(
        functools.partial(attend_kernel, 0, NA, blocks),
        [shaped((2, NA, CW), bf16), shaped((NA, D), f32)],
        q, *kvs, qid, kid, *wo,
    )


def attend_quarter(q, kvs, blocks, qid, kid, wo, total):
    return call(
        functools.partial(attend_kernel, NA, NB, blocks),
        [shaped((2, NB, CW), bf16), *SENDS],
        q, *kvs, qid, kid, *wo, total,
    )


def attend_back_kernel(
    c0, c1, c2, c3, q, kv, kvo, kvz, kvd, qid_a, kid_a, qid_b, kid_b, wo0, wo1,
    mid_out, dq_out, own_out, far_out, z_out,
):
    allowed_a = slot_mask(qid_a[:, :1], kid_a[:1])
    allowed_b = slot_mask(qid_b[:, :1], kid_b[:1])
    mid = whole((c0, c1, c2, c3))
    mid_out[...] = mid
    for g, wo in ((0, wo0), (1, wo1)):
        d_mixed = dot_nt(mid, wo[...]).astype(bf16)
        d_mixed_t = dot_nt(wo[...], mid).astype(bf16)
        query = q[g]
        query_t = query.astype(f32).T.astype(bf16)
        for part in range(2):
            if part == 0:
                allowed, lo, hi = allowed_a, 0, NA
                keys = jnp.concatenate([kv[g, 0, :, :NA], kvo[g, 0, :, :NA]], axis=1)
                values = jnp.concatenate([kv[g, 1, :, :NA], kvo[g, 1, :, :NA]], axis=1)
            else:
                allowed, lo, hi = allowed_b, NA, NT
                keys = jnp.concatenate(
                    [kv[g, 0, :, NA:], kvo[g, 0, :, NA:], kvz[g, 0], kvd[g, 0]], axis=1
                )
                values = jnp.concatenate(
                    [kv[g, 1, :, NA:], kvo[g, 1, :, NA:], kvz[g, 1], kvd[g, 1]], axis=1
                )
            dq, dk, dv = None, None, None
            for head in range(2):
                mask, rmask = lane_mask(head), row_mask(head)
                probs = probabilities(masked(mask, query[lo:hi]), keys, allowed)
                d_probs = dot(masked(mask, d_mixed[lo:hi]), values)
                inner = jnp.sum(d_probs * probs, axis=-1, keepdims=True)
                d_raw = (SCALE * probs * (d_probs - inner)).astype(bf16)
                got_q = dot_nt(keys, d_raw)
                got_k = dot(query_t[:, lo:hi], d_raw)
                got_v = dot(d_mixed_t[:, lo:hi], probs.astype(bf16))
                if head == 0:
                    dq, dk, dv = got_q, got_k, got_v
                else:
                    dq = jnp.where(rmask, got_q, dq)
                    dk = jnp.where(rmask, got_k, dk)
                    dv = jnp.where(rmask, got_v, dv)
            dq_out[g, :, lo:hi] = dq.astype(bf16)
            n = hi - lo
            for j, grad in ((0, dk), (1, dv)):
                own_out[g, j, :, lo:hi] = grad[:, :n]
                far_out[g, j, :, lo:hi] = grad[:, n : 2 * n].astype(bf16)
                if part == 1:
                    z_out[1 - g, j] = grad[:, 2 * n : 3 * n]
                    far_out[1 - g, j, :, NT:] = grad[:, 3 * n :].astype(bf16)


def attend_back(chunks, q, kv, kvo, kvz, kvd, ids, wo):
    return call(
        attend_back_kernel,
        [
            shaped((NT, D), bf16),
            shaped((2, CW, NT), bf16),
            shaped((2, 2, CW, NT), f32),
            shaped((2, 2, CW, NT + NB), bf16),
            shaped((2, 2, CW, NB), f32),
        ],
        *chunks, q, kv, kvo, kvz, kvd, *ids, *wo,
    )


def project_back_kernel(dq, own, far, dz, w0, wa, wb, stack_out, sums, *sends):
    total = None
    w1 = jnp.concatenate([wa[...], wb[...]], axis=0)
    for g, w in ((0, w0[...]), (1, w1)):
        stack_out[g, 0] = dq[g]
        sums[g, 0] = jnp.sum(dq[g].astype(f32), axis=-1, keepdims=True)
        for j in range(2):
            grad = own[g, j] + far[g, j, :, :NT].astype(f32)
            low = jnp.concatenate(
                [grad[:, :NA], grad[:, NA:] + dz[g, j].astype(f32)], axis=1
            ).astype(bf16)
            stack_out[g, 1 + j] = low
            if j == 1:
                sums[g, 1] = jnp.sum(low.astype(f32), axis=-1, keepdims=True)
        for j in range(3):
            part = dot_tn(stack_out[g, j], w[CW * j : CW * (j + 1)])
            total = part if total is None else total + part
    put_sends(total, sends)


def project_back(dq, own, far, dz, w0, w1):
    return call(
        project_back_kernel,
        [shaped((2, 3, CW, NT), bf16), shaped((2, 2, CW, 1), f32), *SENDS],
        dq, own, far, dz, w0, *w1,
    )


def mlp_kernel(layer, c0, c1, c2, c3, wu0, wu1, ub0, ub1, wd0, wd1, nt_out, up_out, act_out, *sends):
    nt = whole((c0, c1, c2, c3))
    nt_out[...] = nt
    total = None
    for g, wu, ub, wd in ((0, wu0, ub0, wd0), (1, wu1, ub1, wd1)):
        u = dot_nt(nt, wu[...]) + ub[layer : layer + 1]
        up_out[g] = u
        act = (0.5 * u * (1.0 + jnp.tanh(gelu_coef * (u + 0.044715 * u * u * u)))).astype(bf16)
        act_out[g] = act
        part = dot(act, wd[...])
        total = part if total is None else total + part
    put_sends(total, sends)


def mlp(layer, chunks, own, oth, ub0, ub1):
    return call(
        functools.partial(mlp_kernel, layer),
        [
            shaped((NT, D), bf16),
            shaped((2, NT, FP), f32),
            shaped((2, NT, FP), bf16),
            *SENDS,
        ],
        *chunks, own[2], oth[2], ub0, ub1, own[3], oth[3],
    )


def mlp_back_kernel(n, *refs):
    chunks, (up, wu0, wu1, wd0, wd1) = refs[:n], refs[n : n + 5]
    d_up_out, sums = refs[n + 5 : n + 7]
    sends = refs[n + 7 : n + 11]
    low = whole(chunks)
    if n > 1:
        refs[n + 11][...] = low
    total = None
    for g, wu, wd in ((0, wu0, wd0), (1, wu1, wd1)):
        d_act = dot_nt(low, wd[...])
        u = up[g]
        t = jnp.tanh(gelu_coef * (u + 0.044715 * u * u * u))
        slope = 0.5 * (1.0 + t) + 0.5 * u * (1.0 - t * t) * (
            gelu_coef * (1.0 + 3 * 0.044715 * u * u)
        )
        d_up = (d_act * slope).astype(bf16)
        d_up_out[g] = d_up
        sums[g] = jnp.sum(d_up.astype(f32), axis=0, keepdims=True)
        part = dot(d_up, wu[...])
        total = part if total is None else total + part
    put_sends(total, sends)


def mlp_back(chunks, up, own, oth):
    n = len(chunks)
    outs = [shaped((2, NT, FP), bf16), shaped((2, 1, FP), f32), *SENDS]
    if n > 1:
        outs.append(shaped((NT, D), bf16))
    got = call(
        functools.partial(mlp_back_kernel, n), outs, *chunks, up, own[2], oth[2], own[3], oth[3]
    )
    return got[0], got[1], got[2:6], (got[6] if n > 1 else chunks[0])


def mlp_weights_kernel(pos, d_up, act, nt, low, keep_out, sent_out):
    first = pos[2] == 0
    for j, (a, b) in enumerate(((d_up, nt), (act, low))):
        for out, g in ((keep_out, 0), (sent_out, 1)):
            picked = jnp.where(first, a[g], a[1 - g])
            out[j] = dot_tn(picked, b[...]).astype(bf16)


def attend_weights_kernel(
    pos, stacked, mixed_a, mixed_b, normed, mid, wide, near, beside, keep_out, sent_out
):
    first = pos[2] == 0
    for out, g in ((keep_out, 0), (sent_out, 1)):
        for j in range(3):
            picked = jnp.where(first, stacked[g, j], stacked[1 - g, j])
            out[j, :CW] = dot(picked, normed[...]).astype(bf16)
        mixed = [jnp.concatenate([mixed_a[i], mixed_b[i]], axis=0) for i in (g, 1 - g)]
        out[3, :CW] = dot_tn(jnp.where(first, mixed[0], mixed[1]), mid[...]).astype(bf16)
        extra = (near, beside) if g == 0 else (beside, near)
        extra = jnp.where(first, extra[0][...], extra[1][...])
        if g == 0:
            extra = extra + wide[...]
        out[:, CW:] = extra.astype(bf16)


def plain_weights_kernel(pos, stacked, mixed_a, mixed_b, normed, mid, keep_out, sent_out):
    first = pos[2] == 0
    for out, g in ((keep_out, 0), (sent_out, 1)):
        for j in range(3):
            picked = jnp.where(first, stacked[g, j], stacked[1 - g, j])
            out[j] = dot(picked, normed[...]).astype(bf16)
        mixed = [jnp.concatenate([mixed_a[i], mixed_b[i]], axis=0) for i in (g, 1 - g)]
        out[3] = dot_tn(jnp.where(first, mixed[0], mixed[1]), mid[...]).astype(bf16)


def mlp_final_kernel(pos, full0, other0, full1, other1, up, down):
    first = pos[2] == 0
    for layer, (full, other) in enumerate(((full0, other0), (full1, other1))):
        for j, out in enumerate((up, down)):
            got = jnp.where(first, full[j], other[j])
            out[:, layer, :] = got[:FW].astype(f32)


def mlp_final(pos, sums):
    args = [part for total in sums for part in total]
    return call(mlp_final_kernel, [shaped((FW, 2, D), f32)] * 2, *args, pos=pos)


def attend_final_kernel(pos, full0, other0, full1, other1, qkv, out, wide, narrow):
    first = pos[2] == 0
    for layer, (full, other) in enumerate(((full0, other0), (full1, other1))):
        got = jnp.where(first, full[...], other[...]).astype(f32)
        for j in range(3):
            qkv[layer, j] = got[j, :CW]
        out[layer] = got[3, :CW]
        if layer == 0:
            narrow[...] = got[:, CW:]
            wide[...] = got[:, CW:].astype(bf16)


def attend_final(pos, sums):
    args = [part for total in sums for part in total]
    outs = [shaped((2, 3, CW, D), f32), shaped((2, CW, D), f32)]
    outs += [shaped((4, EXTRA, D), bf16), shaped((4, EXTRA, D), f32)]
    return call(attend_final_kernel, outs, *args, pos=pos)


def gather_x(chunk):
    return [chunk] + [shift(chunk, "x", -k) for k in (1, 2, 3)]


def scatter_x(sends):
    return [sends[3]] + [shift(sends[k - 1], "x", k) for k in (1, 2, 3)]


def rolled(blocks, by):
    return lax.dynamic_slice_in_dim(jnp.concatenate([blocks, blocks], axis=0), by, 4, axis=0)


def pieces_of(value, index):
    return [
        lax.dynamic_index_in_dim(value, (index + k) % 4, 0, keepdims=False) for k in range(4)
    ]


def scatter_ring(pieces, axis):
    return [pieces[0]] + [shift(pieces[k], axis, k) for k in (1, 2, 3)]


def gather_ring(piece, axis, some):
    got = [piece]
    for k in (1, 2, 3):
        if not some:
            got.append(shift(piece, axis, -k))
        elif axis == "y":
            pairs = [
                (((y + k) % 4) * 4 + e, y * 4 + e) for y in range(4) for e in (0, 3)
            ]
            got.append(lax.ppermute(piece, ("y", "c", "zl"), pairs))
        else:
            pairs = []
            for z in range(4):
                c = z % 2
                src = (z + k) % 4
                pairs.append(
                    ((src // 2) * 4 + c * 2 + src % 2, (z // 2) * 4 + c * 2 + z % 2)
                )
            got.append(lax.ppermute(piece, ("zh", "c", "zl"), pairs))
    return got


def total_of(parts):
    return sum(part.astype(f32) for part in parts).astype(bf16)


class WeightSum:
    def __init__(self, kept, sent, where, y_first, direct):
        y, z = where
        self.one, self.two = (("y", y), (Z, z)) if y_first else ((Z, z), ("y", y))
        self.shape = kept.shape
        self.rows = kept.shape[0] * kept.shape[1] // 4
        self.direct = direct
        self.pending = (kept, shift(sent, "c", 1))
        self.step = 0

    def advance(self, anchor, late=None):
        pending = self.pending if anchor is None else after(self.pending, anchor)
        step, self.step = self.step, self.step + 1
        r = self.rows
        if step == 0:
            both = total_of(pending if late is None else (*pending, late)).reshape(4, r, D)
            feed = pieces_of(both, self.one[1])
            self.pending = scatter_ring(feed, self.one[0])
        elif step == 1 and self.direct:
            feed = total_of(pending)
            self.pending = [feed] + [shift(feed, self.two[0], k) for k in (1, 2, 3)]
            self.step += 1
        elif step == 1:
            piece = total_of(pending).reshape(4, r // 4, D)
            feed = pieces_of(piece, self.two[1])
            self.pending = scatter_ring(feed, self.two[0])
        elif step == 2:
            feed = total_of(pending)
            self.pending = gather_ring(feed, self.two[0], self.two[0] == Z)
        elif step == 3:
            if self.direct:
                feed = total_of(pending)
            else:
                feed = rolled(jnp.stack(pending), (4 - self.two[1]) % 4).reshape(r, D)
            self.pending = gather_ring(feed, self.one[0], True)
        else:
            feed = rolled(jnp.stack(pending), (4 - self.one[1]) % 4).reshape(self.shape)
            self.pending = (feed, shift(feed, "c", 1))
        return feed

    def finish(self):
        while self.step < 5:
            self.advance(None)
        return self.pending


def local(
    inputs,
    picture_ids,
    cotangent,
    norm_gain,
    norm_bias,
    w_qkv,
    q_bias,
    v_bias,
    w_out,
    out_bias,
    w_up,
    up_bias,
    w_down,
    down_bias,
):
    layers = w_qkv.shape[0]
    zl, c, x, y = (lax.axis_index(name) for name in ("zl", "c", "x", "y"))
    z = lax.axis_index("zh") * 2 + zl
    where = (y, z)
    pos = jnp.stack([zl, x, jnp.where(zl == c, 0, 1)]).astype(jnp.int32)

    wq_t = jnp.swapaxes(w_qkv, 2, 3).reshape(layers, 3 * CW, D)
    half = 3 * CW // 2

    def far_projection(own):
        return shift(own[:half], Z, 1), shift(own[half:], Z, -1)

    wq = [(wq_t[0], far_projection(wq_t[0]))]
    up_bias = jnp.pad(up_bias, ((0, 0), (0, FP - FW)))
    qb_far, vb_far, ids_far = shift(q_bias, "zl", 1), shift(v_bias, "zl", 1), shift(picture_ids, "c", 1)
    biases = (q_bias, qb_far, v_bias, vb_far)
    normed, stream = call(
        first_kernel, [shaped((NT, D), bf16), shaped((CHUNK, D), f32)],
        inputs, norm_gain, norm_bias, pos=pos,
    )

    w_out, w_up, w_down, up_bias = after((w_out, w_up, w_down, up_bias), normed)
    ub_far = shift(up_bias, "zl", 1)
    pad = ((0, FP - FW), (0, 0))
    rest = [
        (w_out[layer], jnp.pad(w_up[layer].T, pad), jnp.pad(w_down[layer], pad))
        for layer in range(layers)
    ]
    far_out = [shift(rest[0][0], Z, 1)]
    far_mlp = []
    ids = arrange_ids(pos, picture_ids, ids_far)

    chunks = [normed]
    kept = []
    weights = []
    for layer in range(layers):
        q, kv, part, normed = project(layer, chunks, *wq[layer], biases)
        kvo = shift(kv, "c", 1)
        kvz = shift(part, "zl", 1)
        kvd = shift(kvz, "c", 1)
        wo = (rest[layer][0], far_out[layer])
        mixed_a, total_a = attend_row(q, (kv, kvo), ((0, NA), (0, NA)), ids[0], ids[1], wo)
        up_sent, down_sent = after(rest[layer][1:], kvz)
        far_mlp.append((shift(up_sent, Z, 1), shift(down_sent, Z, -1)))
        mixed_b, *sends = attend_quarter(
            q, (kv, kvo, kvz, kvd), ((NA, NB), (NA, NB), (0, NB), (0, NB)),
            ids[2], ids[3], wo, total_a,
        )
        got = scatter_x(sends)
        middle, low = norm_step(layer, (layer, 1), stream, got, out_bias, norm_gain, norm_bias)
        own = (wq[layer][0], *rest[layer])
        oth = (wq[layer][1], far_out[layer], *far_mlp[layer])
        weights.append((own, oth))
        normed_two, up, act, *sends = mlp(layer, gather_x(low), own, oth, up_bias, ub_far)
        got = scatter_x(sends)
        kept.append(
            (stream, normed, q, kv, kvo, kvz, kvd, mixed_a, mixed_b, middle, normed_two, up, act)
        )
        if layer < layers - 1:
            next_q, next_out = after((wq_t[layer + 1], rest[layer + 1][0]), sends[0])
            wq.append((wq_t[layer + 1], far_projection(next_q)))
            far_out.append(shift(next_out, Z, 1))
            stream, low = norm_step(
                layer, (layer + 1, 0), middle, got, down_bias, norm_gain, norm_bias
            )
            chunks = gather_x(low)

    low, grad_flow, d_down_bias = call(
        cotangent_kernel,
        [shaped((NT, D), bf16), shaped((CHUNK, D), f32), shaped((1, D), f32)],
        after(cotangent, normed_two), ids[0], ids[2], pos=pos,
    )
    result = call(
        functools.partial(result_kernel, layers - 1), [shaped((CHUNK, D), bf16)],
        middle, *got, down_bias,
    )[0]
    chunks = [low]
    zeros = jnp.zeros((1, D), f32)
    wide = [[None] * 6 for _ in range(layers)]
    narrow = [None] * layers
    sums = {}
    for layer in reversed(range(layers)):
        own, oth = weights[layer]
        (stream_in, normed, q, kv, kvo, kvz, kvd, mixed_a, mixed_b, middle, normed_two, up, act) = (
            kept[layer]
        )
        last = layer == layers - 1
        d_up, d_up_bias, sends, grad_low = mlp_back(chunks, up, own, oth)
        got = scatter_x(sends)
        kept_m, sent_m = call(
            mlp_weights_kernel, [shaped((2, FP, D), bf16)] * 2,
            d_up, act, normed_two, grad_low, pos=pos,
        )
        feeds = [sent_m]
        if last:
            far_m = shift(sent_m, "c", 1)
            out_far = shift(after(result, sends[0]), "zl", 1)
        else:
            feeds.append(sums["a1"].advance(sends[0]))
            sums["m0"] = WeightSum(kept_m, sent_m, where, True, False)
        got = after(got, feeds)
        grad_mid, mid_low, norm_two = norm_back((layer, 1), middle, got, grad_flow, norm_gain)
        mid_chunks = gather_x(mid_low)
        if last:
            both = total_of((kept_m, after(far_m, mid_low)))
            sum_m1 = lax.psum(both, ("y", "zh", "zl"))
            feeds = [both]
        else:
            feeds = [sums["m0"].advance(mid_low), sums["a1"].advance(mid_low)]
        mid_chunks = after(mid_chunks, feeds)
        mid, dq, d_own, d_far, d_z = attend_back(
            mid_chunks, q, kv, kvo, kvz, kvd, ids, (own[1], oth[1])
        )
        d_far = shift(d_far, "c", 1)
        d_z = shift((d_z + d_far[..., NT:].astype(f32)).astype(bf16), "zl", 1)
        if last:
            near, beside = after((result, out_far), mid)
            out_slots = gather_x(near) + gather_x(beside)
        stacked, d_qv_bias, *sends = project_back(dq, d_own, d_far, d_z, own[0], oth[0])
        got = scatter_x(sends)
        wide[layer][1], wide[layer][3], wide[layer][4] = (norm_two[i : i + 1] for i in range(3))
        wide[layer][5] = d_down_bias
        narrow[layer] = [
            jnp.concatenate(
                [
                    d_qv_bias[g].reshape(1, 2 * CW),
                    d_up_bias[g],
                    jnp.zeros((1, D - 2 * CW - FP), f32),
                ],
                axis=1,
            )
            for g in range(2)
        ]
        extra = [jnp.zeros((4, 0, D), f32)] * 3
        if not last:
            rows = [row for part in wide for row in part]
            rows = [zeros if row is None else row for row in rows]
            rows = jnp.concatenate(rows + [zeros] * (4 * EXTRA - len(rows)), axis=0)
            extra = [rows.reshape(4, EXTRA, D)]
            for g in range(2):
                rows = [part[g] for part in narrow]
                rows = [zeros] * (6 * layers) + rows
                rows = jnp.concatenate(rows + [zeros] * (4 * EXTRA - len(rows)), axis=0)
                extra.append(rows.reshape(4, EXTRA, D))
        if last:
            kept_a, sent_a = call(
                plain_weights_kernel, [shaped((4, CW, D), bf16)] * 2,
                stacked, mixed_a, mixed_b, normed, mid, pos=pos,
            )
            sums["a1"] = WeightSum(kept_a, sent_a, where, False, True)
            feeds = [sent_a]
        else:
            kept_a, sent_a = call(
                attend_weights_kernel, [shaped((4, CW + EXTRA, D), bf16)] * 2,
                stacked, mixed_a, mixed_b, normed, mid, *extra, pos=pos,
            )
            sums["a0"] = WeightSum(kept_a, sent_a, where, True, True)
            feeds = [sent_a, sums["m0"].advance(sends[0]), sums["a1"].advance(sends[0])]
        got = after(got, feeds)
        grad_flow, low, norm_one = norm_back((layer, 0), stream_in, got, grad_mid, norm_gain)
        if layer > 0:
            wide[layer][0], wide[layer][2] = norm_one[0:1], norm_one[1:2]
            chunks = gather_x(low)
            feeds = sums["a1"].advance(low)
            chunks = after(chunks, feeds)
        d_down_bias = norm_one[2:3]

    in_far = shift(low, "zl", 1)
    late = jnp.zeros((4 * EXTRA, D), f32)
    late = late.at[0].set(norm_one[0]).at[2].set(norm_one[1]).reshape(4, EXTRA, D)
    late = jnp.pad(late, ((0, 0), (CW, 0), (0, 0)))
    sums["a0"].advance(low, late)
    sums["m0"].advance(low)
    in_slots = gather_x(low) + gather_x(in_far)
    outputs = placed_rows(pos, out_slots, bf16)
    sum_m1 = (sum_m1, shift(after(sum_m1, low), "c", 1))
    sum_m0 = sums["m0"].finish()
    sum_a0 = sums["a0"].finish()
    sum_a1 = sums["a1"].finish()
    d_qkv, d_out, wide_sum, narrow_sum = attend_final(pos, (sum_a0, sum_a1))
    wide_sum = total_of((wide_sum, shift(wide_sum, "zl", 1)))
    wide_sum = sum(part.astype(f32) for part in gather_x(wide_sum)).reshape(4 * EXTRA, D)
    input_grad = placed_rows(pos, in_slots, f32)
    d_up, d_down = mlp_final(pos, (sum_m0, sum_m1))
    wide_sum = wide_sum[: 6 * layers].reshape(layers, 6, D)
    narrow_sum = narrow_sum.reshape(4 * EXTRA, D)[6 * layers : 7 * layers]
    return (
        outputs,
        input_grad,
        wide_sum[:, 0:2],
        wide_sum[:, 2:4],
        jnp.swapaxes(d_qkv, 2, 3),
        narrow_sum[:, :CW],
        narrow_sum[:, CW : 2 * CW],
        d_out,
        wide_sum[:, 4],
        jnp.transpose(d_up, (1, 2, 0)),
        narrow_sum[:, 2 * CW : 2 * CW + FW],
        jnp.transpose(d_down, (1, 0, 2)),
        wide_sum[:, 5],
    )


def solution(mesh):
    cut = Mesh(mesh.devices.reshape(4, 2, 2, 2, 4), ("y", "zh", "c", "zl", "x"))
    dp, tensor = ("y", "zh"), ("zl", "x")
    weight_specs = (
        P(),
        P(),
        P(None, None, None, tensor),
        P(None, tensor),
        P(None, tensor),
        P(None, tensor, None),
        P(),
        P(None, None, tensor),
        P(None, tensor),
        P(None, tensor, None),
        P(),
    )
    return jax.shard_map(
        local,
        mesh=cut,
        in_specs=(P(dp, "c", None), P(dp, "c"), P(dp, "c", None), *weight_specs),
        out_specs=(P(dp, "c", None), P(dp, "c", None), *weight_specs),
        check_vma=False,
    )
```

```python
import functools

import jax
import jax.numpy as jnp
from jax import lax
from jax.experimental import pallas as pl
from jax.experimental.pallas import tpu as pltpu
from jax.sharding import Mesh
from jax.sharding import PartitionSpec as P

HEAD_DIM = 72
SCALE = HEAD_DIM**-0.5
D = 1152
CW = 144
FW = 538
FP = 576
NA = 256
NB = 128
NT = NA + NB
CA = NA // 4
CB = NB // 4
EXTRA = 8
norm_eps = 1e-06
gelu_coef = 0.7978845608028654
bf16 = jnp.bfloat16
f32 = jnp.float32
SIZES = {"y": 4, "x": 4, "c": 2, "zl": 2, ("zh", "zl"): 4}
Z = ("zh", "zl")
VMEM_LIMIT = 50 * 1024 * 1024


def shift(value, axis, by):
    n = SIZES[axis]
    return lax.ppermute(value, axis, [(i, (i + by) % n) for i in range(n)])


def dot(a, b):
    return lax.dot_general(a, b, (((1,), (0,)), ((), ())), preferred_element_type=f32)


def dot_nt(a, b):
    return lax.dot_general(a, b, (((1,), (1,)), ((), ())), preferred_element_type=f32)


def dot_tn(a, b):
    return lax.dot_general(a, b, (((0,), (0,)), ((), ())), preferred_element_type=f32)


def after(value, anchor):
    return lax.optimization_barrier((value, anchor))[0]


def shaped(shape, dtype):
    return jax.ShapeDtypeStruct(shape, dtype)


CHUNK = CA + CB
SENDS = [shaped((CHUNK, D), bf16)] * 3 + [shaped((CHUNK, D), f32)]


def call(kernel, outs, *args, pos=None):
    specs = [pl.BlockSpec(memory_space=pltpu.VMEM)] * len(args)
    if pos is not None:
        specs = [pl.BlockSpec(memory_space=pltpu.SMEM)] + specs
        args = (pos, *args)
    return pl.pallas_call(
        kernel,
        out_shape=outs,
        in_specs=specs,
        out_specs=[pl.BlockSpec(memory_space=pltpu.VMEM)] * len(outs),
        compiler_params=pltpu.CompilerParams(vmem_limit_bytes=VMEM_LIMIT),
    )(*args)


def whole(chunks):
    if len(chunks) == 1:
        return chunks[0][...]
    return jnp.concatenate([r[:CA] for r in chunks] + [r[CA:] for r in chunks], axis=0)


def put_sends(total, outs):
    for k in range(4):
        ref = outs[k - 1]
        ref[:CA] = total[CA * k : CA * (k + 1)].astype(ref.dtype)
        ref[CA:] = total[NA + CB * k : NA + CB * (k + 1)].astype(ref.dtype)


def ids_kernel(pos, near, far, qid_a, kid_a, qid_b, kid_b):
    first = pos[0] == 0
    x = pos[1]

    def turned(row, n):
        rows = jnp.broadcast_to(row, (8, n))
        return pltpu.roll(rows, (n - x * (n // 4)) % n, axis=1)

    def half(ref):
        return turned(jnp.where(first, ref[0:1], ref[1:2]), NA)

    def quarter(ref, own):
        low, high = ref[2:3, :NB], ref[2:3, NB:]
        return turned(jnp.where(first == own, low, high), NB)

    a, b = half(near), quarter(near, True)
    qid_a[...] = a.astype(f32).T.astype(jnp.int32)
    qid_b[...] = b.astype(f32).T.astype(jnp.int32)
    kid_a[...] = jnp.concatenate([a, half(far)], axis=1)
    kid_b[...] = jnp.concatenate(
        [b, quarter(far, True), quarter(near, False), quarter(far, False)], axis=1
    )


def arrange_ids(pos, near, far):
    i32 = jnp.int32
    outs = [shaped((NA, 8), i32), shaped((8, 2 * NA), i32)]
    outs += [shaped((NB, 8), i32), shaped((8, 4 * NB), i32)]
    return call(ids_kernel, outs, near, far, pos=pos)


def arranged(pos, ref):
    zl, x = pos[0], pos[1]
    rows, quarters = [], []
    for k in range(4):
        a = lax.rem(x + k, 4)
        rows.append(ref[zl, pl.ds(pl.multiple_of(a * CA, CA), CA)])
        quarters.append(ref[2, pl.ds(pl.multiple_of(zl * NB + a * CB, CB), CB)])
    return jnp.concatenate(rows + quarters, axis=0)


def first_kernel(pos, inputs, gain, bias, normed, stream):
    v = arranged(pos, inputs).astype(f32)
    stream[:CA] = v[:CA]
    stream[CA:] = v[NA : NA + CB]
    mean = jnp.mean(v, axis=-1, keepdims=True)
    centred = v - mean
    var = jnp.mean(centred * centred, axis=-1, keepdims=True)
    out = centred * lax.rsqrt(var + norm_eps) * gain[0, 0:1] + bias[0, 0:1]
    normed[...] = out.astype(bf16)


def cotangent_kernel(pos, cotangent, qid_a, qid_b, low, grad, total):
    live = jnp.concatenate([qid_a[...], qid_b[...]], axis=0)[:, :1] >= 0
    v = jnp.where(live, arranged(pos, cotangent).astype(f32), 0.0)
    low[...] = v.astype(bf16)
    own = jnp.concatenate([v[:CA], v[NA : NA + CB]], axis=0)
    grad[...] = own
    total[...] = jnp.sum(own, axis=0, keepdims=True)


def place_kernel(pos, *refs):
    out = refs[8]
    for dz in range(2):
        zl = pos[0] if dz == 0 else 1 - pos[0]
        for k in range(4):
            a = lax.rem(pos[1] + k, 4)
            chunk = refs[dz * 4 + k]
            out[zl, pl.ds(pl.multiple_of(a * CA, CA), CA)] = chunk[:CA].astype(out.dtype)
            out[2, pl.ds(pl.multiple_of(zl * NB + a * CB, CB), CB)] = chunk[CA:].astype(out.dtype)


def placed_rows(pos, slots, dtype):
    return call(place_kernel, [shaped((3, NA, D), dtype)], *slots, pos=pos)[0]


def norm_kernel(layer, at, stream, own, r1, r2, r3, extra, gain, bias, x_out, n_out):
    x = stream[...] + (own[...] + r1[...].astype(f32) + r2[...].astype(f32) + r3[...].astype(f32))
    x = x + extra[layer : layer + 1]
    x_out[...] = x
    mean = jnp.mean(x, axis=-1, keepdims=True)
    centred = x - mean
    var = jnp.mean(centred * centred, axis=-1, keepdims=True)
    g, b = (ref[at[0], at[1] : at[1] + 1] for ref in (gain, bias))
    n_out[...] = (centred * lax.rsqrt(var + norm_eps) * g + b).astype(bf16)


def norm_step(layer, at, stream, got, extra, gain, bias):
    return call(
        functools.partial(norm_kernel, layer, at),
        [shaped((CHUNK, D), f32), shaped((CHUNK, D), bf16)],
        stream, *got, extra, gain, bias,
    )


def result_kernel(layer, stream, own, r1, r2, r3, extra, out):
    x = stream[...] + (own[...] + r1[...].astype(f32) + r2[...].astype(f32) + r3[...].astype(f32))
    out[...] = (x + extra[layer : layer + 1]).astype(bf16)


def norm_back_kernel(at, x_ref, own, r1, r2, r3, grad_ref, gain, out, low, sums):
    x = x_ref[...]
    d = own[...] + r1[...].astype(f32) + r2[...].astype(f32) + r3[...].astype(f32)
    mean = jnp.mean(x, axis=-1, keepdims=True)
    centred = x - mean
    var = jnp.mean(centred * centred, axis=-1, keepdims=True)
    r = lax.rsqrt(var + norm_eps)
    xh = centred * r
    e = d * gain[at[0], at[1] : at[1] + 1]
    inner = e - jnp.mean(e, axis=-1, keepdims=True)
    inner = inner - xh * jnp.mean(e * xh, axis=-1, keepdims=True)
    grad = grad_ref[...] + r * inner
    out[...] = grad
    low[...] = grad.astype(bf16)
    sums[0:1] = jnp.sum(d * xh, axis=0, keepdims=True)
    sums[1:2] = jnp.sum(d, axis=0, keepdims=True)
    sums[2:3] = jnp.sum(grad, axis=0, keepdims=True)


def norm_back(at, x, got, grad, gain):
    return call(
        functools.partial(norm_back_kernel, at),
        [shaped((CHUNK, D), f32), shaped((CHUNK, D), bf16), shaped((3, D), f32)],
        x, *got, grad, gain,
    )


def qkv_kernel(layer, n, *refs):
    chunks, (w0, wa, wb, qb0, qb1, vb0, vb1) = refs[:n], refs[n : n + 7]
    q_out, kv_out, part_out = refs[n + 7 : n + 10]
    nt = whole(chunks)
    if n > 1:
        refs[n + 10][...] = nt
    w1 = jnp.concatenate([wa[...], wb[...]], axis=0)
    for g, w, qb, vb in ((0, w0[...], qb0, vb0), (1, w1, qb1, vb1)):
        q_out[g] = (dot_nt(nt, w[:CW]) + qb[layer : layer + 1]).astype(bf16)
        key = dot_nt(w[CW : 2 * CW], nt).astype(bf16)
        value = (dot_nt(nt, w[2 * CW :]) + vb[layer : layer + 1]).T.astype(bf16)
        kv_out[g, 0] = key
        kv_out[g, 1] = value
        part_out[1 - g, 0] = key[:, NA:]
        part_out[1 - g, 1] = value[:, NA:]


def project(layer, chunks, own, far, biases):
    n = len(chunks)
    outs = [shaped((2, NT, CW), bf16), shaped((2, 2, CW, NT), bf16), shaped((2, 2, CW, NB), bf16)]
    if n > 1:
        outs.append(shaped((NT, D), bf16))
    got = call(functools.partial(qkv_kernel, layer, n), outs, *chunks, own, *far, *biases)
    return (*got[:3], got[3] if n > 1 else chunks[0])


def lane_mask(head):
    lane = lax.broadcasted_iota(jnp.int32, (1, CW), 1)
    return (lane < HEAD_DIM) if head == 0 else (lane >= HEAD_DIM)


def row_mask(head):
    place = lax.broadcasted_iota(jnp.int32, (CW, 1), 0)
    return (place < HEAD_DIM) if head == 0 else (place >= HEAD_DIM)


def masked(mask, value):
    return jnp.where(mask, value.astype(f32), 0.0).astype(bf16)


def probabilities(qm, keys, allowed):
    scores = jnp.where(allowed, dot(qm, keys) * SCALE, -1e30)
    expanded = jnp.exp(scores - jnp.max(scores, axis=-1, keepdims=True))
    return expanded / jnp.sum(expanded, axis=-1, keepdims=True)


def slot_mask(qid, kid):
    return (kid >= 0) & ((qid == kid) | (qid < 0))


def attend_kernel(first, count, blocks, *refs):
    n = len(blocks)
    q, kvs, (qid, kid, wo0, wo1) = refs[0], refs[1 : 1 + n], refs[1 + n : 5 + n]
    rest = refs[5 + n :]
    allowed = slot_mask(qid[:, :1], kid[:1])
    mixed_out = rest[0] if first == 0 else rest[1]
    total = None
    for g, wo in ((0, wo0), (1, wo1)):
        keys = jnp.concatenate([r[g, 0, :, b : b + m] for r, (b, m) in zip(kvs, blocks)], axis=1)
        values = jnp.concatenate([r[g, 1, :, b : b + m] for r, (b, m) in zip(kvs, blocks)], axis=1)
        query = q[g, first : first + count]
        mixed = None
        for head in range(2):
            mask = lane_mask(head)
            probs = probabilities(masked(mask, query), keys, allowed).astype(bf16)
            got = dot_nt(probs, values)
            mixed = got if head == 0 else jnp.where(mask, got, mixed)
        mixed = mixed.astype(bf16)
        mixed_out[g] = mixed
        part = dot(mixed, wo[...])
        total = part if total is None else total + part
    if first == 0:
        rest[1][...] = total
    else:
        put_sends(jnp.concatenate([rest[0][...], total], axis=0), rest[2:])


def attend_row(q, kvs, blocks, qid, kid, wo):
    return call(
        functools.partial(attend_kernel, 0, NA, blocks),
        [shaped((2, NA, CW), bf16), shaped((NA, D), f32)],
        q, *kvs, qid, kid, *wo,
    )


def attend_quarter(q, kvs, blocks, qid, kid, wo, total):
    return call(
        functools.partial(attend_kernel, NA, NB, blocks),
        [shaped((2, NB, CW), bf16), *SENDS],
        q, *kvs, qid, kid, *wo, total,
    )


def attend_back_kernel(
    c0, c1, c2, c3, q, kv, kvo, kvz, kvd, qid_a, kid_a, qid_b, kid_b, wo0, wo1,
    mid_out, dq_out, own_out, far_out, z_out,
):
    allowed_a = slot_mask(qid_a[:, :1], kid_a[:1])
    allowed_b = slot_mask(qid_b[:, :1], kid_b[:1])
    mid = whole((c0, c1, c2, c3))
    mid_out[...] = mid
    for g, wo in ((0, wo0), (1, wo1)):
        d_mixed = dot_nt(mid, wo[...]).astype(bf16)
        d_mixed_t = dot_nt(wo[...], mid).astype(bf16)
        query = q[g]
        query_t = query.astype(f32).T.astype(bf16)
        for part in range(2):
            if part == 0:
                allowed, lo, hi = allowed_a, 0, NA
                keys = jnp.concatenate([kv[g, 0, :, :NA], kvo[g, 0, :, :NA]], axis=1)
                values = jnp.concatenate([kv[g, 1, :, :NA], kvo[g, 1, :, :NA]], axis=1)
            else:
                allowed, lo, hi = allowed_b, NA, NT
                keys = jnp.concatenate(
                    [kv[g, 0, :, NA:], kvo[g, 0, :, NA:], kvz[g, 0], kvd[g, 0]], axis=1
                )
                values = jnp.concatenate(
                    [kv[g, 1, :, NA:], kvo[g, 1, :, NA:], kvz[g, 1], kvd[g, 1]], axis=1
                )
            dq, dk, dv = None, None, None
            for head in range(2):
                mask, rmask = lane_mask(head), row_mask(head)
                probs = probabilities(masked(mask, query[lo:hi]), keys, allowed)
                d_probs = dot(masked(mask, d_mixed[lo:hi]), values)
                inner = jnp.sum(d_probs * probs, axis=-1, keepdims=True)
                d_raw = (SCALE * probs * (d_probs - inner)).astype(bf16)
                got_q = dot_nt(keys, d_raw)
                got_k = dot(query_t[:, lo:hi], d_raw)
                got_v = dot(d_mixed_t[:, lo:hi], probs.astype(bf16))
                if head == 0:
                    dq, dk, dv = got_q, got_k, got_v
                else:
                    dq = jnp.where(rmask, got_q, dq)
                    dk = jnp.where(rmask, got_k, dk)
                    dv = jnp.where(rmask, got_v, dv)
            dq_out[g, :, lo:hi] = dq.astype(bf16)
            n = hi - lo
            for j, grad in ((0, dk), (1, dv)):
                own_out[g, j, :, lo:hi] = grad[:, :n]
                far_out[g, j, :, lo:hi] = grad[:, n : 2 * n].astype(bf16)
                if part == 1:
                    z_out[1 - g, j] = grad[:, 2 * n : 3 * n]
                    far_out[1 - g, j, :, NT:] = grad[:, 3 * n :].astype(bf16)


def attend_back(chunks, q, kv, kvo, kvz, kvd, ids, wo):
    return call(
        attend_back_kernel,
        [
            shaped((NT, D), bf16),
            shaped((2, CW, NT), bf16),
            shaped((2, 2, CW, NT), f32),
            shaped((2, 2, CW, NT + NB), bf16),
            shaped((2, 2, CW, NB), f32),
        ],
        *chunks, q, kv, kvo, kvz, kvd, *ids, *wo,
    )


def project_back_kernel(dq, own, far, dz, w0, wa, wb, stack_out, sums, *sends):
    total = None
    w1 = jnp.concatenate([wa[...], wb[...]], axis=0)
    for g, w in ((0, w0[...]), (1, w1)):
        stack_out[g, 0] = dq[g]
        sums[g, 0] = jnp.sum(dq[g].astype(f32), axis=-1, keepdims=True)
        for j in range(2):
            grad = own[g, j] + far[g, j, :, :NT].astype(f32)
            low = jnp.concatenate(
                [grad[:, :NA], grad[:, NA:] + dz[g, j].astype(f32)], axis=1
            ).astype(bf16)
            stack_out[g, 1 + j] = low
            if j == 1:
                sums[g, 1] = jnp.sum(low.astype(f32), axis=-1, keepdims=True)
        for j in range(3):
            part = dot_tn(stack_out[g, j], w[CW * j : CW * (j + 1)])
            total = part if total is None else total + part
    put_sends(total, sends)


def project_back(dq, own, far, dz, w0, w1):
    return call(
        project_back_kernel,
        [shaped((2, 3, CW, NT), bf16), shaped((2, 2, CW, 1), f32), *SENDS],
        dq, own, far, dz, w0, *w1,
    )


def joined(parts):
    return jnp.concatenate([part[...] for part in parts], axis=0)


def mlp_kernel(layer, c0, c1, c2, c3, ub0, ub1, wu0, wd0, wu1, wu2, wd1, wd2, nt_out, up_out, act_out, *sends):
    nt = whole((c0, c1, c2, c3))
    nt_out[...] = nt
    total = None
    for g, wu, ub, wd in ((0, wu0, ub0, wd0), (1, joined((wu1, wu2)), ub1, joined((wd1, wd2)))):
        u = dot_nt(nt, wu[...]) + ub[layer : layer + 1]
        up_out[g] = u
        act = (0.5 * u * (1.0 + jnp.tanh(gelu_coef * (u + 0.044715 * u * u * u)))).astype(bf16)
        act_out[g] = act
        part = dot(act, wd[...])
        total = part if total is None else total + part
    put_sends(total, sends)


def mlp(layer, chunks, own, oth, ub0, ub1):
    return call(
        functools.partial(mlp_kernel, layer),
        [
            shaped((NT, D), bf16),
            shaped((2, NT, FP), f32),
            shaped((2, NT, FP), bf16),
            *SENDS,
        ],
        *chunks, ub0, ub1, own[2], own[3], *oth[2], *oth[3],
    )


def mlp_back_kernel(n, *refs):
    chunks, (up, wu0, wd0) = refs[:n], refs[n : n + 3]
    wu1, wd1 = joined(refs[n + 3 : n + 5]), joined(refs[n + 5 : n + 7])
    d_up_out, sums = refs[n + 7 : n + 9]
    sends = refs[n + 9 : n + 13]
    low = whole(chunks)
    if n > 1:
        refs[n + 13][...] = low
    total = None
    for g, wu, wd in ((0, wu0, wd0), (1, wu1, wd1)):
        d_act = dot_nt(low, wd[...])
        u = up[g]
        t = jnp.tanh(gelu_coef * (u + 0.044715 * u * u * u))
        slope = 0.5 * (1.0 + t) + 0.5 * u * (1.0 - t * t) * (
            gelu_coef * (1.0 + 3 * 0.044715 * u * u)
        )
        d_up = (d_act * slope).astype(bf16)
        d_up_out[g] = d_up
        sums[g] = jnp.sum(d_up.astype(f32), axis=0, keepdims=True)
        part = dot(d_up, wu[...])
        total = part if total is None else total + part
    put_sends(total, sends)


def mlp_back(chunks, up, own, oth):
    n = len(chunks)
    outs = [shaped((2, NT, FP), bf16), shaped((2, 1, FP), f32), *SENDS]
    if n > 1:
        outs.append(shaped((NT, D), bf16))
    got = call(
        functools.partial(mlp_back_kernel, n), outs, *chunks, up, own[2], own[3], *oth[2], *oth[3]
    )
    return got[0], got[1], got[2:6], (got[6] if n > 1 else chunks[0])


def mlp_weights_kernel(pos, d_up, act, nt, low, keep_out, sent_out):
    first = pos[2] == 0
    for j, (a, b) in enumerate(((d_up, nt), (act, low))):
        for out, g in ((keep_out, 0), (sent_out, 1)):
            picked = jnp.where(first, a[g], a[1 - g])
            got = dot_tn(picked, b[...]).astype(bf16)
            for k in range(2):
                out[2 * j + k] = got[2 * CW * k : 2 * CW * (k + 1)]


def attend_weights_kernel(
    pos, stacked, mixed_a, mixed_b, normed, mid, near, beside, keep_out, sent_out
):
    first = pos[2] == 0
    for out, g in ((keep_out, 0), (sent_out, 1)):
        for j in range(3):
            picked = jnp.where(first, stacked[g, j], stacked[1 - g, j])
            out[j, :CW] = dot(picked, normed[...]).astype(bf16)
        mixed = [jnp.concatenate([mixed_a[i], mixed_b[i]], axis=0) for i in (g, 1 - g)]
        out[3, :CW] = dot_tn(jnp.where(first, mixed[0], mixed[1]), mid[...]).astype(bf16)
        extra = (near, beside) if g == 0 else (beside, near)
        extra = jnp.where(first, extra[0][...], extra[1][...])
        out[:, CW:] = extra.astype(bf16)


def plain_weights_kernel(pos, stacked, mixed_a, mixed_b, normed, mid, keep_out, sent_out):
    first = pos[2] == 0
    for out, g in ((keep_out, 0), (sent_out, 1)):
        for j in range(3):
            picked = jnp.where(first, stacked[g, j], stacked[1 - g, j])
            out[j] = dot(picked, normed[...]).astype(bf16)
        mixed = [jnp.concatenate([mixed_a[i], mixed_b[i]], axis=0) for i in (g, 1 - g)]
        out[3] = dot_tn(jnp.where(first, mixed[0], mixed[1]), mid[...]).astype(bf16)


def mlp_final_kernel(pos, full0, other0, full1, other1, up, down):
    first = pos[2] == 0
    for layer, (full, other) in enumerate(((full0, other0), (full1, other1))):
        for j, out in enumerate((up, down)):
            got = [jnp.where(first, full[k], other[k]) for k in (2 * j, 2 * j + 1)]
            out[:, layer, :] = jnp.concatenate(got, axis=0)[:FW].astype(f32)


def mlp_final(pos, sums):
    args = [part for total in sums for part in total]
    return call(mlp_final_kernel, [shaped((FW, 2, D), f32)] * 2, *args, pos=pos)


def attend_final_kernel(pos, full0, other0, full1, other1, qkv, out, small):
    first = pos[2] == 0
    for layer, (full, other) in enumerate(((full0, other0), (full1, other1))):
        got = jnp.where(first, full[...], other[...]).astype(f32)
        for j in range(3):
            qkv[layer, j] = got[j, :CW]
        out[layer] = got[3, :CW]
        if layer == 0:
            small[...] = got[:, CW:]


def attend_final(pos, sums):
    args = [part for total in sums for part in total]
    outs = [shaped((2, 3, CW, D), f32), shaped((2, CW, D), f32)]
    outs += [shaped((4, EXTRA, D), f32)]
    return call(attend_final_kernel, outs, *args, pos=pos)


def gather_x(chunk):
    return [chunk] + [shift(chunk, "x", -k) for k in (1, 2, 3)]


def scatter_x(sends):
    return [sends[3]] + [shift(sends[k - 1], "x", k) for k in (1, 2, 3)]


def rolled(blocks, by):
    return lax.dynamic_slice_in_dim(jnp.concatenate([blocks, blocks], axis=0), by, 4, axis=0)


def pieces_of(value, index):
    return [
        lax.dynamic_index_in_dim(value, (index + k) % 4, 0, keepdims=False) for k in range(4)
    ]


def scatter_ring(pieces, axis):
    return [pieces[0]] + [shift(pieces[k], axis, k) for k in (1, 2, 3)]


def gather_ring(piece, axis, some):
    got = [piece]
    for k in (1, 2, 3):
        if not some:
            got.append(shift(piece, axis, -k))
        elif axis == "y":
            pairs = [
                (((y + k) % 4) * 4 + e, y * 4 + e) for y in range(4) for e in (0, 3)
            ]
            got.append(lax.ppermute(piece, ("y", "c", "zl"), pairs))
        else:
            pairs = []
            for z in range(4):
                c = z % 2
                src = (z + k) % 4
                pairs.append(
                    ((src // 2) * 4 + c * 2 + src % 2, (z // 2) * 4 + c * 2 + z % 2)
                )
            got.append(lax.ppermute(piece, ("zh", "c", "zl"), pairs))
    return got


def total_of(parts):
    return sum(part.astype(f32) for part in parts).astype(bf16)


def pieces_kernel(pos, *refs):
    ins, outs = refs[:-4], refs[-4:]
    for k in range(4):
        block = lax.rem(pos[0] + k, 4)
        outs[k][...] = sum(ref[block].astype(f32) for ref in ins).astype(bf16)


def sum_pieces(index, *parts):
    shape = parts[0].shape
    outs = [shaped(shape[1:], bf16)] * 4
    return call(pieces_kernel, outs, *parts, pos=index)


def total_kernel(*refs):
    refs[-1][...] = sum(ref[...].astype(f32) for ref in refs[:-1]).astype(bf16)


def sum_parts(*parts):
    return call(total_kernel, [shaped(parts[0].shape, bf16)], *parts)[0]


def blocks_kernel(pos, *refs):
    for k in range(4):
        refs[4][lax.rem(pos[0] + k, 4)] = refs[k][...]


def place_blocks(index, parts):
    return call(blocks_kernel, [shaped((4, *parts[0].shape), bf16)], *parts, pos=index)[0]


class WeightSum:
    def __init__(self, kept, sent, y):
        self.y = y[None]
        self.pending = (kept, shift(sent, "c", 1))
        self.step = 0

    def advance(self, anchor=None, late=None):
        pending = self.pending if anchor is None else after(self.pending, anchor)
        step, self.step = self.step, self.step + 1
        if step == 0:
            feed = sum_pieces(self.y, *pending)
            self.pending = scatter_ring(feed, "y")
        elif step == 1:
            feed = sum_parts(*(pending if late is None else (*pending, late)))
            self.pending = [feed] + [shift(feed, Z, k) for k in (1, 2, 3)]
        elif step == 2:
            feed = sum_parts(*pending)
            self.pending = gather_ring(feed, "y", True)
        else:
            feed = place_blocks(self.y, pending)
            self.pending = (feed, shift(feed, "c", 1))
        return feed


def sum_ring(value, axis):
    return value + sum(shift(value, axis, k) for k in range(1, SIZES[axis]))


def local(
    inputs,
    picture_ids,
    cotangent,
    norm_gain,
    norm_bias,
    w_qkv,
    q_bias,
    v_bias,
    w_out,
    out_bias,
    w_up,
    up_bias,
    w_down,
    down_bias,
):
    layers = w_qkv.shape[0]
    zl, c, x, y = (lax.axis_index(name) for name in ("zl", "c", "x", "y"))
    pos = jnp.stack([zl, x, jnp.where(zl == c, 0, 1)]).astype(jnp.int32)

    wq_t = jnp.swapaxes(w_qkv, 2, 3).reshape(layers, 3 * CW, D)
    half = 3 * CW // 2

    def far_projection(own):
        return shift(own[:half], Z, 1), shift(own[half:], Z, -1)

    wq = [(wq_t[0], far_projection(wq_t[0]))]
    up_bias = jnp.pad(up_bias, ((0, 0), (0, FP - FW)))
    qb_far, vb_far, ub_far = (shift(part, "zl", 1) for part in (q_bias, v_bias, up_bias))
    ids_far = shift(picture_ids, "c", 1)
    biases = (q_bias, qb_far, v_bias, vb_far)
    normed, stream = call(
        first_kernel, [shaped((NT, D), bf16), shaped((CHUNK, D), f32)],
        inputs, norm_gain, norm_bias, pos=pos,
    )

    w_out, w_up, w_down = after((w_out, w_up, w_down), normed)
    pad = ((0, FP - FW), (0, 0))
    rest = [
        (w_out[layer], jnp.pad(w_up[layer].T, pad), jnp.pad(w_down[layer], pad))
        for layer in range(layers)
    ]
    far_out = [shift(rest[0][0], Z, 1)]
    far_up, far_down = [[], []], [[], []]

    def fetch(layer, which, part, anchor):
        half_rows = after(rest[layer][which][part * FP // 2 : (part + 1) * FP // 2], anchor)
        got = shift(half_rows, Z, 1 if which == 1 else -1)
        (far_up if which == 1 else far_down)[layer].append(got)
        return got

    ids = arrange_ids(pos, picture_ids, ids_far)

    chunks = [after(normed, ub_far)]
    kept = []
    weights = []
    for layer in range(layers):
        more = layer < layers - 1
        q, kv, part, normed = project(layer, chunks, *wq[layer], biases)
        kvo = shift(kv, "c", 1)
        kvz = shift(part, "zl", 1)
        kvd = shift(kvz, "c", 1)
        wo = (rest[layer][0], far_out[layer])
        mixed_a, total_a = attend_row(q, (kv, kvo), ((0, NA), (0, NA)), ids[0], ids[1], wo)
        if layer == 0:
            halves = [fetch(0, which, 0, (kvz, far_out[0])) for which in (1, 2)]
        mixed_b, *sends = attend_quarter(
            q, (kv, kvo, kvz, kvd), ((NA, NB), (NA, NB), (0, NB), (0, NB)),
            ids[2], ids[3], wo, total_a,
        )
        got = scatter_x(sends)
        if layer == 0:
            later = [fetch(0, which, 1, (halves, got[1])) for which in (1, 2)]
        else:
            later = [fetch(layer, which, 1, sends[0]) for which in (1, 2)]
            low_in, grad_flow, d_down_bias = call(
                cotangent_kernel,
                [shaped((NT, D), bf16), shaped((CHUNK, D), f32), shaped((1, D), f32)],
                after(cotangent, sends[0]), ids[0], ids[2], pos=pos,
            )
            got = after(got, low_in)
        middle, low = norm_step(layer, (layer, 1), stream, got, out_bias, norm_gain, norm_bias)
        own = (wq[layer][0], *rest[layer])
        oth = (wq[layer][1], far_out[layer], far_up[layer], far_down[layer])
        weights.append((own, oth))
        chunks = gather_x(low)
        if more:
            wq.append((wq_t[layer + 1], far_projection(after(wq_t[layer + 1], chunks[1]))))
            chunks = after(chunks, later)
        normed_two, up, act, *sends = mlp(layer, chunks, own, oth, up_bias, ub_far)
        kept.append(
            (stream, normed, q, kv, kvo, kvz, kvd, mixed_a, mixed_b, middle, normed_two, up, act)
        )
        if more:
            got = scatter_x(sends)
            next_far = (wq[layer + 1][1], sends[0])
            far_out.append(shift(after(rest[layer + 1][0], next_far), Z, 1))
            halves = [fetch(layer + 1, which, 0, next_far) for which in (1, 2)]
            stream, low = norm_step(
                layer, (layer + 1, 0), middle, got, down_bias, norm_gain, norm_bias
            )
            chunks = gather_x(low)
            chunks = after(chunks, (halves, far_out[layer + 1]))

    last_sends, last_middle = sends, middle
    zeros = jnp.zeros((1, D), f32)
    here = picture_ids[0, 0] > -2

    def apart(work):
        shapes = jax.eval_shape(work)
        return lax.cond(
            here, work, lambda: jax.tree.map(lambda s: jnp.zeros(s.shape, s.dtype), shapes)
        )

    def feed_forward_back(layer, chunks, grad_flow):
        own, oth = weights[layer]
        middle, normed_two, up, act = kept[layer][-4:]
        d_up, d_up_bias, sends, grad_low = mlp_back(chunks, up, own, oth)
        got = scatter_x(sends)
        kept_m, sent_m = call(
            mlp_weights_kernel, [shaped((4, 2 * CW, D), bf16)] * 2,
            d_up, act, normed_two, grad_low, pos=pos,
        )
        far_m = shift(sent_m, "c", 1)
        got = after(got, sent_m)
        grad_mid, mid_low, norm_two = norm_back((layer, 1), middle, got, grad_flow, norm_gain)
        feed = sum_parts(kept_m, far_m)
        return grad_mid, mid_low, norm_two, d_up_bias, feed

    def attention_back(layer, mid_low, result=None):
        own, oth = weights[layer]
        stream_in, normed, q, kv, kvo, kvz, kvd, mixed_a, mixed_b = kept[layer][:9]
        mid_chunks = gather_x(mid_low)
        mid, dq, d_own, d_far, d_z = attend_back(
            mid_chunks, q, kv, kvo, kvz, kvd, ids, (own[1], oth[1])
        )
        d_far = shift(d_far, "c", 1)
        d_z = shift((d_z + d_far[..., NT:].astype(f32)).astype(bf16), "zl", 1)
        if result is not None:
            result = result(mid_chunks[0])
            d_z = after(d_z, result)
        stacked, d_qv_bias, *sends = project_back(dq, d_own, d_far, d_z, own[0], oth[0])
        return mid, stacked, d_qv_bias, sends, result

    def narrow_rows(d_qv_bias, d_up_bias):
        return [
            jnp.concatenate(
                [
                    d_qv_bias[g].reshape(1, 2 * CW),
                    d_up_bias[g],
                    jnp.zeros((1, D - 2 * CW - FP), f32),
                ],
                axis=1,
            )
            for g in range(2)
        ]

    def last_result(anchor):
        got = scatter_x(after(last_sends, anchor))
        return call(
            functools.partial(result_kernel, layers - 1), [shaped((CHUNK, D), bf16)],
            last_middle, *got, down_bias,
        )[0]

    grad_mid1, mid_low1, norm_two1, d_up_bias1, feed_m1 = feed_forward_back(1, [low_in], grad_flow)
    sum_m1 = lax.psum(feed_m1, ("y", "zh", "zl"))

    def first_block():
        stream_in, normed, q, kv, kvo, kvz, kvd, mixed_a, mixed_b = kept[1][:9]
        mid, stacked, d_qv_bias, sends, result = attention_back(1, mid_low1, last_result)
        got = scatter_x(sends)
        kept_a, sent_a = call(
            plain_weights_kernel, [shaped((4, CW, D), bf16)] * 2,
            stacked, mixed_a, mixed_b, normed, mid, pos=pos,
        )
        far_a = shift(sent_a, "c", 1)
        grad_flow, low, norm_one = norm_back((1, 0), stream_in, got, grad_mid1, norm_gain)
        chunks = gather_x(low)
        out_far = shift(after(result, low), "zl", 1)
        feed_a = sum_parts(kept_a, far_a)
        back = feed_forward_back(0, chunks, grad_flow)
        return d_qv_bias, norm_one, result, out_far, feed_a, back

    d_qv_bias1, norm_one1, result, out_far, feed_a1, back = apart(first_block)
    grad_mid0, mid_low0, norm_two0, d_up_bias0, feed_m0 = back
    sum_a1, sum_m0 = lax.psum(after((feed_a1, feed_m0), sum_m1), ("y", "zh", "zl"))

    def second_block():
        stream_in, normed, q, kv, kvo, kvz, kvd, mixed_a, mixed_b = kept[0][:9]
        mid, stacked, d_qv_bias0, sends, _ = attention_back(0, mid_low0)
        got = scatter_x(sends)
        narrow = (narrow_rows(d_qv_bias0, d_up_bias0), narrow_rows(d_qv_bias1, d_up_bias1))
        extra = []
        for g in range(2):
            rows = [zeros] * (6 * layers) + [part[g] for part in narrow]
            rows = jnp.concatenate(rows + [zeros] * (4 * EXTRA - len(rows)), axis=0)
            extra.append(rows.reshape(4, EXTRA, D))
        kept_a, sent_a = call(
            attend_weights_kernel, [shaped((4, CW + EXTRA, D), bf16)] * 2,
            stacked, mixed_a, mixed_b, normed, mid, *extra, pos=pos,
        )
        total = WeightSum(kept_a, sent_a, y)
        total.advance()
        grad_flow, low, norm_one = norm_back((0, 0), stream_in, got, grad_mid0, norm_gain)
        return low, norm_one, total.pending

    low, norm_one0, pending = apart(second_block)
    wide = [
        [one[0:1], two[0:1], one[1:2], two[1:2], two[2:3], down]
        for one, two, down in (
            (norm_one0, norm_two0, norm_one1[2:3]),
            (norm_one1, norm_two1, d_down_bias),
        )
    ]
    sums = {"a0": WeightSum.__new__(WeightSum)}
    sums["a0"].y, sums["a0"].pending, sums["a0"].step = y[None], pending, 1

    in_far = shift(low, "zl", 1)
    late = jnp.concatenate([row for part in wide for row in part], axis=0)
    late = sum_ring(sum_ring(late + shift(late, "c", 1), "x"), "y")
    out_slots = gather_x(after(jnp.stack([result, out_far]), low))
    late = jnp.concatenate([late, jnp.zeros((4 * EXTRA - 6 * layers, D), f32)], axis=0)
    late = lax.dynamic_slice_in_dim(late, y * EXTRA, EXTRA, axis=0)
    late = jnp.pad(late, ((CW, 0), (0, 0)))
    feed = sums["a0"].advance(in_far, late)
    in_slots = gather_x(after(jnp.stack([low, in_far]), feed))
    outputs = placed_rows(pos, [part[i] for i in range(2) for part in out_slots], bf16)
    sums["a0"].advance((in_slots, outputs))
    sum_m1, sum_m0 = ((part, shift(part, "c", 1)) for part in (sum_m1, sum_m0))
    sum_a1 = (sum_a1, shift(sum_a1, "c", 1))
    input_grad = placed_rows(pos, [part[i] for i in range(2) for part in in_slots], f32)
    d_up, d_down = mlp_final(pos, (sum_m0, sum_m1))
    sums["a0"].advance((input_grad, d_up))
    sum_a0 = sums["a0"].pending
    d_qkv, d_out, small = attend_final(pos, (sum_a0, sum_a1))
    small = small.reshape(4 * EXTRA, D)
    wide_sum = small[: 6 * layers].reshape(layers, 6, D)
    narrow_sum = small[6 * layers : 7 * layers]
    return (
        outputs,
        input_grad,
        wide_sum[:, 0:2],
        wide_sum[:, 2:4],
        jnp.swapaxes(d_qkv, 2, 3),
        narrow_sum[:, :CW],
        narrow_sum[:, CW : 2 * CW],
        d_out,
        wide_sum[:, 4],
        jnp.transpose(d_up, (1, 2, 0)),
        narrow_sum[:, 2 * CW : 2 * CW + FW],
        jnp.transpose(d_down, (1, 0, 2)),
        wide_sum[:, 5],
    )


def solution(mesh):
    cut = Mesh(mesh.devices.reshape(4, 2, 2, 2, 4), ("y", "zh", "c", "zl", "x"))
    dp, tensor = ("y", "zh"), ("zl", "x")
    weight_specs = (
        P(),
        P(),
        P(None, None, None, tensor),
        P(None, tensor),
        P(None, tensor),
        P(None, tensor, None),
        P(),
        P(None, None, tensor),
        P(None, tensor),
        P(None, tensor, None),
        P(),
    )
    return jax.shard_map(
        local,
        mesh=cut,
        in_specs=(P(dp, "c", None), P(dp, "c"), P(dp, "c", None), *weight_specs),
        out_specs=(P(dp, "c", None), P(dp, "c", None), *weight_specs),
        check_vma=False,
    )
```

```python
import functools
from typing import NamedTuple

import jax
import jax.numpy as jnp
from jax import lax
from jax.experimental import pallas as pl
from jax.experimental.pallas import tpu as pltpu
from jax.sharding import Mesh
from jax.sharding import PartitionSpec as P

HEAD_DIM = 72
SCALE = HEAD_DIM**-0.5
D = 1152
CW = 144
FW = 538
FP = 576
NA = 256
NB = 128
NT = NA + NB
CA = NA // 4
CB = NB // 4
V_AT, UP_AT = 256, 512
EXTRA = 8
norm_eps = 1e-06
gelu_coef = 0.7978845608028654
bf16 = jnp.bfloat16
f32 = jnp.float32
SIZES = {"y": 4, "x": 4, "c": 2, "zl": 2, ("zh", "zl"): 4}
Z = ("zh", "zl")
VMEM_LIMIT = 50 * 1024 * 1024


def shift(value, axis, by):
    n = SIZES[axis]
    return lax.ppermute(value, axis, [(i, (i + by) % n) for i in range(n)])


def dot(a, b):
    return lax.dot_general(a, b, (((1,), (0,)), ((), ())), preferred_element_type=f32)


def dot_nt(a, b):
    return lax.dot_general(a, b, (((1,), (1,)), ((), ())), preferred_element_type=f32)


def dot_tn(a, b):
    return lax.dot_general(a, b, (((0,), (0,)), ((), ())), preferred_element_type=f32)


def after(value, anchor):
    return lax.optimization_barrier((value, anchor))[0]


def shaped(shape, dtype):
    return jax.ShapeDtypeStruct(shape, dtype)


CHUNK = CA + CB
SENDS = [shaped((CHUNK, D), bf16)] * 3 + [shaped((CHUNK, D), f32)]


class Layer(NamedTuple):
    array: jax.Array
    index: int


def call(kernel, outs, *args, pos=None, scratch=()):
    specs = [pl.BlockSpec(memory_space=pltpu.VMEM)] * len(args)
    layers = [arg.index if isinstance(arg, Layer) else None for arg in args]
    args = [arg.array if isinstance(arg, Layer) else arg for arg in args]
    if any(layer is not None for layer in layers):
        on_layers, start = kernel, 0 if pos is None else 1

        def kernel(*refs):
            refs = list(refs)
            for i, layer in enumerate(layers, start):
                if layer is not None:
                    refs[i] = refs[i].at[layer]
            on_layers(*refs)

    if pos is not None:
        specs = [pl.BlockSpec(memory_space=pltpu.SMEM)] + specs
        args = (pos, *args)
    return pl.pallas_call(
        kernel,
        out_shape=outs,
        in_specs=specs,
        out_specs=[pl.BlockSpec(memory_space=pltpu.VMEM)] * len(outs),
        scratch_shapes=scratch,
        compiler_params=pltpu.CompilerParams(vmem_limit_bytes=VMEM_LIMIT),
    )(*args)


def whole(chunks):
    if len(chunks) == 1:
        return chunks[0][...]
    return jnp.concatenate([r[:CA] for r in chunks] + [r[CA:] for r in chunks], axis=0)


def put_sends(total, outs):
    for k in range(4):
        ref = outs[k - 1]
        ref[:CA] = total[CA * k : CA * (k + 1)].astype(ref.dtype)
        ref[CA:] = total[NA + CB * k : NA + CB * (k + 1)].astype(ref.dtype)


def ids_kernel(pos, near, far, qid_a, kid_a, qid_b, kid_b):
    first = pos[0] == 0
    x = pos[1]

    def turned(row, n):
        rows = jnp.broadcast_to(row, (8, n))
        return pltpu.roll(rows, (n - x * (n // 4)) % n, axis=1)

    def half(ref):
        return turned(jnp.where(first, ref[0:1], ref[1:2]), NA)

    def quarter(ref, own):
        low, high = ref[2:3, :NB], ref[2:3, NB:]
        return turned(jnp.where(first == own, low, high), NB)

    a, b = half(near), quarter(near, True)
    qid_a[...] = a.astype(f32).T.astype(jnp.int32)
    qid_b[...] = b.astype(f32).T.astype(jnp.int32)
    kid_a[...] = jnp.concatenate([a, half(far)], axis=1)
    kid_b[...] = jnp.concatenate(
        [b, quarter(far, True), quarter(near, False), quarter(far, False)], axis=1
    )


def arrange_ids(pos, near, far):
    i32 = jnp.int32
    outs = [shaped((NA, 8), i32), shaped((8, 2 * NA), i32)]
    outs += [shaped((NB, 8), i32), shaped((8, 4 * NB), i32)]
    return call(ids_kernel, outs, near, far, pos=pos)


def arranged(pos, ref):
    zl, x = pos[0], pos[1]
    rows, quarters = [], []
    for k in range(4):
        a = lax.rem(x + k, 4)
        rows.append(ref[zl, pl.ds(pl.multiple_of(a * CA, CA), CA)])
        quarters.append(ref[2, pl.ds(pl.multiple_of(zl * NB + a * CB, CB), CB)])
    return jnp.concatenate(rows + quarters, axis=0)


def first_kernel(pos, inputs, gain, bias, normed, stream):
    v = arranged(pos, inputs).astype(f32)
    stream[:CA] = v[:CA]
    stream[CA:] = v[NA : NA + CB]
    mean = jnp.mean(v, axis=-1, keepdims=True)
    centred = v - mean
    var = jnp.mean(centred * centred, axis=-1, keepdims=True)
    out = centred * lax.rsqrt(var + norm_eps) * gain[0, 0:1] + bias[0, 0:1]
    normed[...] = out.astype(bf16)


def cotangent_kernel(pos, cotangent, qid_a, qid_b, low, grad, total):
    live = jnp.concatenate([qid_a[...], qid_b[...]], axis=0)[:, :1] >= 0
    v = jnp.where(live, arranged(pos, cotangent).astype(f32), 0.0)
    low[...] = v.astype(bf16)
    own = jnp.concatenate([v[:CA], v[NA : NA + CB]], axis=0)
    grad[...] = own
    total[...] = jnp.sum(own, axis=0, keepdims=True)


def place_kernel(pos, *refs):
    out = refs[4]
    for dz in range(2):
        zl = pos[0] if dz == 0 else 1 - pos[0]
        for k in range(4):
            a = lax.rem(pos[1] + k, 4)
            chunk = refs[k].at[dz]
            out[zl, pl.ds(pl.multiple_of(a * CA, CA), CA)] = chunk[:CA].astype(out.dtype)
            out[2, pl.ds(pl.multiple_of(zl * NB + a * CB, CB), CB)] = chunk[CA:].astype(out.dtype)


def placed_rows(pos, slots, dtype):
    return call(place_kernel, [shaped((3, NA, D), dtype)], *slots, pos=pos)[0]


def norm_kernel(layer, at, stream, own, r1, r2, r3, extra, gain, bias, x_out, n_out):
    x = stream[...] + (own[...] + r1[...].astype(f32) + r2[...].astype(f32) + r3[...].astype(f32))
    x = x + extra[layer : layer + 1]
    x_out[...] = x
    mean = jnp.mean(x, axis=-1, keepdims=True)
    centred = x - mean
    var = jnp.mean(centred * centred, axis=-1, keepdims=True)
    g, b = (ref[at[0], at[1] : at[1] + 1] for ref in (gain, bias))
    n_out[...] = (centred * lax.rsqrt(var + norm_eps) * g + b).astype(bf16)


def norm_step(layer, at, stream, got, extra, gain, bias):
    return call(
        functools.partial(norm_kernel, layer, at),
        [shaped((CHUNK, D), f32), shaped((CHUNK, D), bf16)],
        stream, *got, extra, gain, bias,
    )


def result_kernel(layer, stream, own, r1, r2, r3, extra, out):
    x = stream[...] + (own[...] + r1[...].astype(f32) + r2[...].astype(f32) + r3[...].astype(f32))
    out[...] = (x + extra[layer : layer + 1]).astype(bf16)


def norm_back_kernel(at, x_ref, own, r1, r2, r3, grad_ref, gain, out, low, sums):
    x = x_ref[...]
    d = own[...] + r1[...].astype(f32) + r2[...].astype(f32) + r3[...].astype(f32)
    mean = jnp.mean(x, axis=-1, keepdims=True)
    centred = x - mean
    var = jnp.mean(centred * centred, axis=-1, keepdims=True)
    r = lax.rsqrt(var + norm_eps)
    xh = centred * r
    e = d * gain[at[0], at[1] : at[1] + 1]
    inner = e - jnp.mean(e, axis=-1, keepdims=True)
    inner = inner - xh * jnp.mean(e * xh, axis=-1, keepdims=True)
    grad = grad_ref[...] + r * inner
    out[...] = grad
    low[...] = grad.astype(bf16)
    sums[0:1] = jnp.sum(d * xh, axis=0, keepdims=True)
    sums[1:2] = jnp.sum(d, axis=0, keepdims=True)
    sums[2:3] = jnp.sum(grad, axis=0, keepdims=True)


def norm_back(at, x, got, grad, gain):
    return call(
        functools.partial(norm_back_kernel, at),
        [shaped((CHUNK, D), f32), shaped((CHUNK, D), bf16), shaped((3, D), f32)],
        x, *got, grad, gain,
    )


def qkv_kernel(layer, n, *refs):
    chunks, (w0, wa, wb, bias0, bias1) = refs[:n], refs[n : n + 5]
    q_out, kv_out, part_out = refs[n + 5 : n + 8]
    nt = whole(chunks)
    if n > 1:
        refs[n + 8][...] = nt
    w1 = jnp.concatenate([wa[: 3 * CW // 2], wb[: 3 * CW // 2]], axis=0)
    for g, w, bias in ((0, w0[...], bias0), (1, w1, bias1)):
        qb = bias[layer : layer + 1, :CW]
        vb = bias[layer : layer + 1, V_AT : V_AT + CW]
        q_out[g] = (dot_nt(nt, w[:CW]) + qb).astype(bf16)
        key = dot_nt(w[CW : 2 * CW], nt).astype(bf16)
        value = (dot_nt(nt, w[2 * CW :]) + vb).T.astype(bf16)
        kv_out[g, 0] = key
        kv_out[g, 1] = value
        part_out[1 - g, 0] = key[:, NA:]
        part_out[1 - g, 1] = value[:, NA:]


def project(layer, chunks, own, far, biases):
    n = len(chunks)
    outs = [shaped((2, NT, CW), bf16), shaped((2, 2, CW, NT), bf16), shaped((2, 2, CW, NB), bf16)]
    if n > 1:
        outs.append(shaped((NT, D), bf16))
    got = call(functools.partial(qkv_kernel, layer, n), outs, *chunks, own, *far, *biases)
    return (*got[:3], got[3] if n > 1 else chunks[0])


def lane_mask(head):
    lane = lax.broadcasted_iota(jnp.int32, (1, CW), 1)
    return (lane < HEAD_DIM) if head == 0 else (lane >= HEAD_DIM)


def row_mask(head):
    place = lax.broadcasted_iota(jnp.int32, (CW, 1), 0)
    return (place < HEAD_DIM) if head == 0 else (place >= HEAD_DIM)


def masked(mask, value):
    return jnp.where(mask, value.astype(f32), 0.0).astype(bf16)


def probabilities(qm, keys, allowed):
    scores = jnp.where(allowed, dot(qm, keys) * SCALE, -1e30)
    expanded = jnp.exp(scores - jnp.max(scores, axis=-1, keepdims=True))
    return expanded * (1.0 / jnp.sum(expanded, axis=-1, keepdims=True))


def slot_mask(qid, kid):
    return (kid >= 0) & ((qid == kid) | (qid < 0))


def out_rows_of(refs):
    if len(refs) == 1:
        return refs[0][...]
    return jnp.concatenate([ref[3 * CW // 2 :] for ref in refs], axis=0)


def attend_kernel(first, count, blocks, n_out, *refs):
    n = len(blocks)
    q, kvs, (qid, kid, wo0) = refs[0], refs[1 : 1 + n], refs[1 + n : 4 + n]
    wo1 = out_rows_of(refs[4 + n : 4 + n + n_out])
    rest = refs[4 + n + n_out :]
    allowed = slot_mask(qid[:, :1], kid[:1])
    mixed_out = rest[0] if first == 0 else rest[1]
    total = None
    for g, wo in ((0, wo0), (1, wo1)):
        keys = jnp.concatenate([r[g, 0, :, b : b + m] for r, (b, m) in zip(kvs, blocks)], axis=1)
        values = jnp.concatenate([r[g, 1, :, b : b + m] for r, (b, m) in zip(kvs, blocks)], axis=1)
        query = q[g, first : first + count]
        mixed = None
        for head in range(2):
            mask = lane_mask(head)
            probs = probabilities(masked(mask, query), keys, allowed).astype(bf16)
            got = dot_nt(probs, values)
            mixed = got if head == 0 else jnp.where(mask, got, mixed)
        mixed = mixed.astype(bf16)
        mixed_out[g] = mixed
        part = dot(mixed, wo[...])
        total = part if total is None else total + part
    if first == 0:
        rest[1][...] = total
    else:
        put_sends(jnp.concatenate([rest[0][...], total], axis=0), rest[2:])


def attend_row(q, kvs, blocks, qid, kid, wo):
    return call(
        functools.partial(attend_kernel, 0, NA, blocks, len(wo) - 1),
        [shaped((2, NA, CW), bf16), shaped((NA, D), f32)],
        q, *kvs, qid, kid, *wo,
    )


def attend_quarter(q, kvs, blocks, qid, kid, wo, total):
    return call(
        functools.partial(attend_kernel, NA, NB, blocks, len(wo) - 1),
        [shaped((2, NB, CW), bf16), *SENDS],
        q, *kvs, qid, kid, *wo, total,
    )


def attend_back_kernel(*refs):
    c0, c1, c2, c3, q, kv, kvo, kvz, kvd, mixed_a, mixed_b = refs[:11]
    qid_a, kid_a, qid_b, kid_b, wo0 = refs[11:16]
    wo1 = out_rows_of(refs[16:-5])
    mid_out, dq_out, own_out, far_out, z_out = refs[-5:]
    allowed_a = slot_mask(qid_a[:, :1], kid_a[:1])
    allowed_b = slot_mask(qid_b[:, :1], kid_b[:1])
    mid = whole((c0, c1, c2, c3))
    mid_out[...] = mid
    for g, wo in ((0, wo0), (1, wo1)):
        d_mixed = dot_nt(mid, wo[...]).astype(bf16)
        d_mixed_t = dot_nt(wo[...], mid).astype(bf16)
        along = jnp.concatenate([mixed_a[g], mixed_b[g]], axis=0).astype(f32) * d_mixed.astype(f32)
        query = q[g]
        query_t = query.astype(f32).T.astype(bf16)
        for part in range(2):
            if part == 0:
                allowed, lo, hi = allowed_a, 0, NA
                keys = jnp.concatenate([kv[g, 0, :, :NA], kvo[g, 0, :, :NA]], axis=1)
                values = jnp.concatenate([kv[g, 1, :, :NA], kvo[g, 1, :, :NA]], axis=1)
            else:
                allowed, lo, hi = allowed_b, NA, NT
                keys = jnp.concatenate(
                    [kv[g, 0, :, NA:], kvo[g, 0, :, NA:], kvz[g, 0], kvd[g, 0]], axis=1
                )
                values = jnp.concatenate(
                    [kv[g, 1, :, NA:], kvo[g, 1, :, NA:], kvz[g, 1], kvd[g, 1]], axis=1
                )
            dq, dk, dv = None, None, None
            for head in range(2):
                mask, rmask = lane_mask(head), row_mask(head)
                probs = probabilities(masked(mask, query[lo:hi]), keys, allowed)
                d_probs = dot(masked(mask, d_mixed[lo:hi]), values)
                inner = jnp.sum(jnp.where(mask, along[lo:hi], 0.0), axis=-1, keepdims=True)
                d_raw = (SCALE * probs * (d_probs - inner)).astype(bf16)
                got_q = dot_nt(keys, d_raw)
                got_k = dot(query_t[:, lo:hi], d_raw)
                got_v = dot(d_mixed_t[:, lo:hi], probs.astype(bf16))
                if head == 0:
                    dq, dk, dv = got_q, got_k, got_v
                else:
                    dq = jnp.where(rmask, got_q, dq)
                    dk = jnp.where(rmask, got_k, dk)
                    dv = jnp.where(rmask, got_v, dv)
            dq_out[g, :, lo:hi] = dq.astype(bf16)
            n = hi - lo
            for j, grad in ((0, dk), (1, dv)):
                own_out[g, j, :, lo:hi] = grad[:, :n]
                far_out[g, j, :, lo:hi] = grad[:, n : 2 * n].astype(bf16)
                if part == 1:
                    z_out[1 - g, j] = grad[:, 2 * n : 3 * n]
                    far_out[1 - g, j, :, NT:] = grad[:, 3 * n :].astype(bf16)


def attend_back(chunks, q, kv, kvo, kvz, kvd, mixed, ids, wo):
    return call(
        attend_back_kernel,
        [
            shaped((NT, D), bf16),
            shaped((2, CW, NT), bf16),
            shaped((2, 2, CW, NT), f32),
            shaped((2, 2, CW, NT + NB), bf16),
            shaped((2, 2, CW, NB), f32),
        ],
        *chunks, q, kv, kvo, kvz, kvd, *mixed, *ids, *wo,
    )


def project_back_kernel(dq, own, far, dz, w0, wa, wb, stack_out, sums, *sends):
    total = None
    ones = jnp.ones((8, NT), bf16)
    w1 = jnp.concatenate([wa[: 3 * CW // 2], wb[: 3 * CW // 2]], axis=0)
    for g, w in ((0, w0[...]), (1, w1)):
        stack_out[g, 0] = dq[g]
        sums[g, 0] = dot_nt(ones, dq[g])
        for j in range(2):
            grad = own[g, j] + far[g, j, :, :NT].astype(f32)
            low = jnp.concatenate(
                [grad[:, :NA], grad[:, NA:] + dz[g, j].astype(f32)], axis=1
            ).astype(bf16)
            stack_out[g, 1 + j] = low
            if j == 1:
                sums[g, 1] = dot_nt(ones, low)
        for j in range(3):
            part = dot_tn(stack_out[g, j], w[CW * j : CW * (j + 1)])
            total = part if total is None else total + part
    put_sends(total, sends)


def project_back(dq, own, far, dz, w0, w1):
    return call(
        project_back_kernel,
        [shaped((2, 3, CW, NT), bf16), shaped((2, 2, 8, CW), f32), *SENDS],
        dq, own, far, dz, w0, *w1,
    )


def mlp_kernel(
    layer, c0, c1, c2, c3, bias0, bias1, wu0, wd0, wu1, wd1, nt_out, up_out, act_out, *sends
):
    nt = whole((c0, c1, c2, c3))
    nt_out[...] = nt
    total = None
    for g, wu, bias, wd in ((0, wu0, bias0, wd0), (1, wu1, bias1, wd1)):
        u = dot_nt(nt, wu[...]) + bias[layer : layer + 1, UP_AT : UP_AT + FP]
        up_out[g] = u
        act = (0.5 * u * (1.0 + jnp.tanh(gelu_coef * (u + 0.044715 * u * u * u)))).astype(bf16)
        act_out[g] = act
        part = dot(act, wd[...])
        total = part if total is None else total + part
    put_sends(total, sends)


def mlp(layer, chunks, own, oth, biases):
    return call(
        functools.partial(mlp_kernel, layer),
        [
            shaped((NT, D), bf16),
            shaped((2, NT, FP), f32),
            shaped((2, NT, FP), bf16),
            *SENDS,
        ],
        *chunks, *biases, own[2], own[3], oth[2], oth[3],
    )


def mlp_back_kernel(n, *refs):
    chunks, (up, wu0, wd0) = refs[:n], refs[n : n + 3]
    wu1, wd1 = refs[n + 3 : n + 5]
    d_up_out, sums = refs[n + 5 : n + 7]
    sends = refs[n + 7 : n + 11]
    low = whole(chunks)
    if n > 1:
        refs[n + 11][...] = low
    total = None
    for g, wu, wd in ((0, wu0, wd0), (1, wu1, wd1)):
        d_act = dot_nt(low, wd[...])
        u = up[g]
        t = jnp.tanh(gelu_coef * (u + 0.044715 * u * u * u))
        slope = 0.5 * (1.0 + t) + 0.5 * u * (1.0 - t * t) * (
            gelu_coef * (1.0 + 3 * 0.044715 * u * u)
        )
        d_up = (d_act * slope).astype(bf16)
        d_up_out[g] = d_up
        sums[g] = jnp.sum(d_up.astype(f32), axis=0, keepdims=True)
        part = dot(d_up, wu[...])
        total = part if total is None else total + part
    put_sends(total, sends)


def mlp_back(chunks, up, own, oth):
    n = len(chunks)
    outs = [shaped((2, NT, FP), bf16), shaped((2, 1, FP), f32), *SENDS]
    if n > 1:
        outs.append(shaped((NT, D), bf16))
    got = call(
        functools.partial(mlp_back_kernel, n), outs, *chunks, up, own[2], own[3], oth[2], oth[3]
    )
    return got[0], got[1], got[2:6], (got[6] if n > 1 else chunks[0])


def mlp_weights_kernel(pos, d_up, act, nt, low, keep_out, sent_out):
    first = pos[2] == 0
    for j, (a, b) in enumerate(((d_up, nt), (act, low))):
        for out, g in ((keep_out, 0), (sent_out, 1)):
            picked = jnp.where(first, a[g], a[1 - g])
            got = dot_tn(picked, b[...]).astype(bf16)
            for k in range(2):
                out[2 * j + k] = got[2 * CW * k : 2 * CW * (k + 1)]


def attend_weights_kernel(
    pos, stacked, mixed_a, mixed_b, normed, mid, qv0, qv1, up0, up1, keep_out, sent_out, extra
):
    plain_weights_kernel(pos, stacked, mixed_a, mixed_b, normed, mid, keep_out, sent_out)
    first = pos[2] == 0
    for out, g in ((keep_out, 0), (sent_out, 1)):
        extra[...] = jnp.zeros_like(extra)
        for layer, (qv, up) in enumerate(((qv0, up0), (qv1, up1))):
            row = slice(4 + layer, 5 + layer)
            extra[row, :CW] = jnp.where(first, qv[g, 0, :1], qv[1 - g, 0, :1])
            extra[row, V_AT : V_AT + CW] = jnp.where(first, qv[g, 1, :1], qv[1 - g, 1, :1])
            extra[row, UP_AT : UP_AT + FP] = jnp.where(first, up[g], up[1 - g])
        for j in range(4):
            rows = extra[...] if j == 1 else jnp.zeros_like(extra)
            out[j, CW:] = rows.astype(bf16)


def plain_weights_kernel(pos, stacked, mixed_a, mixed_b, normed, mid, keep_out, sent_out):
    first = pos[2] == 0
    for out, g in ((keep_out, 0), (sent_out, 1)):
        for j in range(3):
            picked = jnp.where(first, stacked[g, j], stacked[1 - g, j])
            out[j, :CW] = dot(picked, normed[...]).astype(bf16)
        mixed = [jnp.concatenate([mixed_a[i], mixed_b[i]], axis=0) for i in (g, 1 - g)]
        out[3, :CW] = dot_tn(jnp.where(first, mixed[0], mixed[1]), mid[...]).astype(bf16)


def mlp_final_kernel(pos, *refs):
    first = pos[2] == 0
    for j, out in enumerate(refs[8:]):
        for layer in range(2):
            full, other = refs[4 * j + 2 * layer : 4 * j + 2 * layer + 2]
            out[:, layer, :] = jnp.where(first, full[...], other[...]).astype(f32)


def mlp_final(pos, sums):
    rows = 2 * CW
    args = [part for _ in range(2) for total in sums for part in total]
    specs = [pl.BlockSpec(memory_space=pltpu.SMEM)]
    for j in range(2):
        specs += [pl.BlockSpec((None, rows, D), lambda i, j=j: (2 * j + i, 0, 0))] * 4
    return pl.pallas_call(
        mlp_final_kernel,
        grid=(2,),
        out_shape=[shaped((FW, 2, D), f32)] * 2,
        in_specs=specs,
        out_specs=[pl.BlockSpec((rows, 2, D), lambda i: (i, 0, 0))] * 2,
        compiler_params=pltpu.CompilerParams(vmem_limit_bytes=VMEM_LIMIT),
    )(pos, *args)


def wide_kernel(one0, two0, one1, two1, down, out):
    rows = [one0[0:1], two0[0:1], one0[1:2], two0[1:3], one1[2:3]]
    rows += [one1[0:1], two1[0:1], one1[1:2], two1[1:3], down[...]]
    rows.append(jnp.zeros((2 * EXTRA - 12, D), f32))
    out[...] = jnp.concatenate(rows, axis=0).reshape(out.shape)


def attend_final_kernel(
    pos, full0, other0, full1, other1, qkv, out, gain, bias, q_bias, v_bias, out_bias, up, down
):
    first = pos[2] == 0
    for layer, (full, other) in enumerate(((full0, other0), (full1, other1))):
        for j in range(4):
            got = jnp.where(first, full[j, :CW], other[j, :CW]).astype(f32)
            if j < 3:
                qkv[layer, j] = got
            else:
                out[layer] = got
    small = [jnp.where(first, full0[j, CW:], other0[j, CW:]).astype(f32) for j in range(2)]
    small = jnp.concatenate(small, axis=0)
    for layer in range(2):
        at = 6 * layer
        gain[layer] = small[at : at + 2]
        bias[layer] = small[at + 2 : at + 4]
        out_bias[layer : layer + 1] = small[at + 4 : at + 5]
        down[layer : layer + 1] = small[at + 5 : at + 6]
        row = small[12 + layer : 13 + layer]
        q_bias[layer : layer + 1] = row[:, :CW]
        v_bias[layer : layer + 1] = row[:, V_AT : V_AT + CW]
        up[layer : layer + 1] = row[:, UP_AT : UP_AT + FW]


def attend_final(pos, sums):
    args = [part for total in sums for part in total]
    outs = [(2, 3, CW, D), (2, CW, D), (2, 2, D), (2, 2, D), (2, CW), (2, CW), (2, D)]
    outs = [shaped(shape, f32) for shape in (*outs, (2, FW), (2, D))]
    return call(attend_final_kernel, outs, *args, pos=pos)


def gather_x(chunk):
    return [chunk] + [shift(chunk, "x", -k) for k in (1, 2, 3)]


def scatter_x(sends):
    return [sends[3]] + [shift(sends[k - 1], "x", k) for k in (1, 2, 3)]


def scatter_ring(pieces, axis):
    return [pieces[0]] + [shift(pieces[k], axis, k) for k in (1, 2, 3)]


def gather_ring(piece, axis, some):
    got = [piece]
    for k in (1, 2, 3):
        if not some:
            got.append(shift(piece, axis, -k))
        elif axis == "y":
            pairs = [
                (((y + k) % 4) * 4 + e, y * 4 + e) for y in range(4) for e in (0, 3)
            ]
            got.append(lax.ppermute(piece, ("y", "c", "zl"), pairs))
        else:
            pairs = []
            for z in range(4):
                c = z % 2
                src = (z + k) % 4
                pairs.append(
                    ((src // 2) * 4 + c * 2 + src % 2, (z // 2) * 4 + c * 2 + z % 2)
                )
            got.append(lax.ppermute(piece, ("zh", "c", "zl"), pairs))
    return got


def pieces_kernel(pos, kept, far, *outs):
    for k in range(4):
        block = lax.rem(pos[0] + k, 4)
        outs[k][...] = (kept[block].astype(f32) + far[block].astype(f32)).astype(bf16)


def sum_pieces(index, kept, far):
    outs = [shaped(kept.shape[1:], bf16)] * 4
    return call(pieces_kernel, outs, kept, far, pos=index)


def last_piece_kernel(pos, *refs):
    late, out = refs[-2:]
    total = sum(ref[...].astype(f32) for ref in refs[:4])
    out[:CW] = total[:CW].astype(bf16)
    rows = late[jnp.minimum(pos[0], 1)]
    out[CW:] = (total[CW:] + jnp.where(pos[0] < 2, rows, 0.0)).astype(bf16)


def total_kernel(*refs):
    refs[-1][...] = sum(ref[...].astype(f32) for ref in refs[:-1]).astype(bf16)


def sum_parts(*parts):
    return call(total_kernel, [shaped(parts[0].shape, bf16)], *parts)[0]


def blocks_kernel(pos, *refs):
    for k in range(4):
        refs[4][lax.rem(pos[0] + k, 4)] = refs[k][...]


def place_blocks(index, parts):
    return call(blocks_kernel, [shaped((4, *parts[0].shape), bf16)], *parts, pos=index)[0]


def sum_ring(value, axis):
    return value + sum(shift(value, axis, k) for k in range(1, SIZES[axis]))


def local(
    inputs,
    picture_ids,
    cotangent,
    norm_gain,
    norm_bias,
    w_qkv,
    q_bias,
    v_bias,
    w_out,
    out_bias,
    w_up,
    up_bias,
    w_down,
    down_bias,
):
    layers = w_qkv.shape[0]
    zl, c, x, y = (lax.axis_index(name) for name in ("zl", "c", "x", "y"))
    pos = jnp.stack([zl, x, jnp.where(zl == c, 0, 1)]).astype(jnp.int32)

    y_index = y[None]
    here = picture_ids[0, 0] > -2

    def apart(work):
        shapes = jax.eval_shape(work)
        return lax.cond(
            here, work, lambda: jax.tree.map(lambda s: jnp.zeros(s.shape, s.dtype), shapes)
        )

    wq_t = jnp.swapaxes(w_qkv, 2, 3).reshape(layers, 3 * CW, D)
    half = 3 * CW // 2

    wq_far = [(shift(wq_t[0, :half], Z, 1), shift(wq_t[0, half:], Z, -1))]
    normed, stream = call(
        first_kernel, [shaped((NT, D), bf16), shaped((CHUNK, D), f32)],
        inputs, norm_gain, norm_bias, pos=pos,
    )
    w_out, w_up, w_down, q_bias, v_bias, up_bias = after(
        (w_out, w_up, w_down, q_bias, v_bias, up_bias), normed
    )
    bias = jnp.concatenate(
        [
            jnp.pad(part, ((0, 0), (0, size - part.shape[1])))
            for part, size in ((q_bias, V_AT), (v_bias, UP_AT - V_AT), (up_bias, FP))
        ],
        axis=1,
    )
    biases = (bias, shift(bias, "zl", 1))
    ids_far = shift(picture_ids, "c", 1)
    pad = ((0, FP - FW), (0, 0))
    wide_weights = [
        (jnp.pad(w_up[layer].T, pad), jnp.pad(w_down[layer], pad)) for layer in range(layers)
    ]
    out_far = [(shift(w_out[0], Z, 1),)]
    ids = arrange_ids(pos, picture_ids, ids_far)

    def far_wide(layer, anchor):
        up_rows, down_rows = after(wide_weights[layer], anchor)
        return shift(up_rows, Z, 1), shift(down_rows, Z, -1)

    def keys_step(layer, chunks):
        q, kv, part, normed = project(layer, chunks, Layer(wq_t, layer), wq_far[layer], biases)
        kvo = shift(kv, "c", 1)
        kvz = shift(part, "zl", 1)
        kvd = shift(kvz, "c", 1)
        wo = (Layer(w_out, layer), *out_far[layer])
        mixed_a, total_a = attend_row(q, (kv, kvo), ((0, NA), (0, NA)), ids[0], ids[1], wo)
        return q, kv, kvo, kvz, kvd, normed, wo, mixed_a, total_a

    def attention_step(layer, q, kv, kvo, kvz, kvd, wo, total_a, stream):
        mixed_b, *sends = attend_quarter(
            q, (kv, kvo, kvz, kvd), ((NA, NB), (NA, NB), (0, NB), (0, NB)),
            ids[2], ids[3], wo, total_a,
        )
        got = scatter_x(sends)
        middle, low = norm_step(layer, (layer, 1), stream, got, out_bias, norm_gain, norm_bias)
        return mixed_b, middle, gather_x(low)

    normed = after(normed, (wide_weights, ids))
    q, kv, kvo, kvz, kvd, normed, wo, mixed_a, total_a = keys_step(0, [normed])
    wide_far = [far_wide(0, (kvz, *out_far[0]))]
    def first_attention():
        split = (3 * CW + CW) // 2 - half
        sends = (
            jnp.concatenate([wq_t[1, :half], w_out[1, :split]], axis=0),
            jnp.concatenate([wq_t[1, half:], w_out[1, split:]], axis=0),
        )
        done = attention_step(0, q, kv, kvo, kvz, kvd, wo, total_a, stream)
        return done, sends

    (mixed_b, middle, chunks), next_sends = apart(first_attention)
    own = (Layer(wq_t, 0), Layer(w_out, 0), *wide_weights[0])
    weights = [(own, (wq_far[0], out_far[0], *wide_far[0]))]
    sent_up, sent_down = shift(next_sends[0], Z, 1), shift(next_sends[1], Z, -1)
    wq_far.append((sent_up, sent_down))
    out_far.append((sent_up, sent_down))

    def first_mlp():
        normed_two, up, act, *sends = mlp(0, chunks, *weights[0], biases)
        got = scatter_x(sends)
        stream, low = norm_step(0, (1, 0), middle, got, down_bias, norm_gain, norm_bias)
        return normed_two, up, act, stream, gather_x(low)

    normed_two, up, act, stream1, chunks1 = apart(first_mlp)
    kept = [(stream, normed, q, kv, kvo, kvz, kvd, mixed_a, mixed_b, middle, normed_two, up, act)]

    chunks1 = after(chunks1, wq_far[1])
    q1, kv1, kvo1, kvz1, kvd1, normed1, wo1, mixed_a1, total_a1 = keys_step(1, chunks1)
    wide_far.append(far_wide(1, (kvz1, total_a1)))

    def second_attention():
        low = call(
            cotangent_kernel,
            [shaped((NT, D), bf16), shaped((CHUNK, D), f32), shaped((1, D), f32)],
            cotangent, ids[0], ids[2], pos=pos,
        )
        return attention_step(1, q1, kv1, kvo1, kvz1, kvd1, wo1, total_a1, stream1), low

    (mixed_b1, middle1, chunks), (low_in, grad_flow, d_down_bias) = apart(second_attention)
    own = (Layer(wq_t, 1), Layer(w_out, 1), *wide_weights[1])
    weights.append((own, (wq_far[1], out_far[1], *wide_far[1])))
    normed_two, up, act, *last_sends = mlp(1, chunks, *weights[1], biases)
    kept.append(
        (stream1, normed1, q1, kv1, kvo1, kvz1, kvd1, mixed_a1, mixed_b1, middle1, normed_two, up, act)
    )

    def feed_forward_back(layer, chunks, grad_flow):
        own, oth = weights[layer]
        middle, normed_two, up, act = kept[layer][-4:]
        d_up, d_up_bias, sends, grad_low = mlp_back(chunks, up, own, oth)
        got = scatter_x(sends)
        kept_m, sent_m = call(
            mlp_weights_kernel, [shaped((4, 2 * CW, D), bf16)] * 2,
            d_up, act, normed_two, grad_low, pos=pos,
        )
        grad_mid, mid_low, norm_two = norm_back((layer, 1), middle, got, grad_flow, norm_gain)
        return grad_mid, mid_low, norm_two, d_up_bias, (kept_m, sent_m)

    def gather_mid(mid_low, *kept_and_sent):
        sums = [sum_parts(kept, shift(sent, "c", 1)) for kept, sent in kept_and_sent]
        return gather_x(mid_low), sums

    def attention_back(layer, mid_chunks, last_result=None):
        own, oth = weights[layer]
        q, kv, kvo, kvz, kvd = kept[layer][2:7]
        mid, dq, d_own, d_far, d_z = attend_back(
            mid_chunks, q, kv, kvo, kvz, kvd, kept[layer][7:9], ids, (own[1], *oth[1])
        )
        d_far = shift(d_far, "c", 1)
        d_z = shift((d_z + d_far[..., NT:].astype(f32)).astype(bf16), "zl", 1)
        result = None
        if last_result is not None:
            result = last_result()
            d_z = after(d_z, result)
        stacked, d_qv_bias, *sends = project_back(dq, d_own, d_far, d_z, own[0], oth[0])
        return mid, stacked, d_qv_bias, scatter_x(sends), result

    def last_result():
        return call(
            functools.partial(result_kernel, layers - 1), [shaped((CHUNK, D), bf16)],
            middle1, *scatter_x(last_sends), down_bias,
        )[0]

    grad_mid1, mid_low1, norm_two1, d_up_bias1, part_m1 = feed_forward_back(
        1, [low_in], grad_flow
    )
    mid_chunks1, (feed_m1,) = apart(lambda: gather_mid(mid_low1, part_m1))
    sum_m1 = lax.psum(feed_m1, ("y", "zh", "zl"))

    def first_block():
        stream_in, normed = kept[1][:2]
        mid, stacked, d_qv_bias, got, _ = attention_back(1, mid_chunks1)
        part_a = call(
            plain_weights_kernel, [shaped((4, CW, D), bf16)] * 2,
            stacked, *kept[1][7:9], normed, mid, pos=pos,
        )
        grad_flow, low, norm_one = norm_back((1, 0), stream_in, got, grad_mid1, norm_gain)
        chunks = gather_x(low)
        back = feed_forward_back(0, chunks, grad_flow)
        return d_qv_bias, norm_one, part_a, back

    d_qv_bias1, norm_one1, part_a1, back = apart(first_block)
    grad_mid0, mid_low0, norm_two0, d_up_bias0, part_m0 = back
    mid_chunks0, (feed_a1, feed_m0) = apart(lambda: gather_mid(mid_low0, part_a1, part_m0))
    sum_a1, sum_m0 = lax.psum((feed_a1, feed_m0), ("zh", "zl", "y"))

    def second_block():
        stream_in, normed = kept[0][:2]
        mid, stacked, d_qv_bias0, got, result = attention_back(0, mid_chunks0, last_result)
        part_a = call(
            attend_weights_kernel, [shaped((4, CW + EXTRA, D), bf16)] * 2,
            stacked, *kept[0][7:9], normed, mid, d_qv_bias0, d_qv_bias1, d_up_bias0, d_up_bias1,
            pos=pos, scratch=[pltpu.VMEM((EXTRA, D), f32)],
        )
        _, low, norm_one = norm_back((0, 0), stream_in, got, grad_mid0, norm_gain)
        pieces = sum_pieces(y_index, part_a[0], shift(part_a[1], "c", 1))
        return low, norm_one, pieces, result

    low, norm_one0, pieces, result = apart(second_block)

    def first_sums():
        parts = scatter_ring(pieces, "y")
        both = jnp.stack([low, shift(low, "zl", 1)])
        in_slots = gather_x(both)
        late = call(
            wide_kernel, [shaped((2, EXTRA, D), f32)],
            norm_one0, norm_two0, norm_one1, norm_two1, d_down_bias,
        )[0].astype(bf16)
        late = late + shift(late, "c", 1)
        late = sum_ring(late.astype(f32), "x")
        late = sum_ring(after(late, parts), "y")
        piece = call(
            last_piece_kernel, [shaped((CW + EXTRA, D), bf16)], *parts, late, pos=y_index
        )[0]
        return in_slots, piece, jnp.stack([result, shift(result, "zl", 1)])

    in_slots, piece, results = apart(first_sums)

    def second_sums():
        parts = [piece] + [shift(piece, Z, k) for k in (1, 2, 3)]
        out_slots = gather_x(results)
        return sum_parts(*parts), out_slots

    total, out_slots = apart(second_sums)
    sum_a1, sum_m0, sum_m1 = ((part, shift(part, "c", 1)) for part in (sum_a1, sum_m0, sum_m1))

    def last_sums():
        full = place_blocks(y_index, gather_ring(total, "y", True))
        input_grad = placed_rows(pos, in_slots, f32)
        outputs = placed_rows(pos, out_slots, bf16)
        return input_grad, outputs, (full, shift(full, "c", 1))

    input_grad, outputs, sum_a0 = apart(last_sums)
    d_up, d_down = mlp_final(pos, (sum_m0, sum_m1))
    d_qkv, d_out, d_gain, d_bias, d_q, d_v, d_out_bias, d_up_bias, d_down_bias = attend_final(
        pos, (sum_a0, sum_a1)
    )
    return (
        outputs,
        input_grad,
        d_gain,
        d_bias,
        jnp.swapaxes(d_qkv, 2, 3),
        d_q,
        d_v,
        d_out,
        d_out_bias,
        jnp.transpose(d_up, (1, 2, 0)),
        d_up_bias,
        jnp.transpose(d_down, (1, 0, 2)),
        d_down_bias,
    )


def solution(mesh):
    cut = Mesh(mesh.devices.reshape(4, 2, 2, 2, 4), ("y", "zh", "c", "zl", "x"))
    dp, tensor = ("y", "zh"), ("zl", "x")
    weight_specs = (
        P(),
        P(),
        P(None, None, None, tensor),
        P(None, tensor),
        P(None, tensor),
        P(None, tensor, None),
        P(),
        P(None, None, tensor),
        P(None, tensor),
        P(None, tensor, None),
        P(),
    )
    return jax.shard_map(
        local,
        mesh=cut,
        in_specs=(P(dp, "c", None), P(dp, "c"), P(dp, "c", None), *weight_specs),
        out_specs=(P(dp, "c", None), P(dp, "c", None), *weight_specs),
        check_vma=False,
    )
```

```python
import functools
from typing import NamedTuple

import jax
import jax.numpy as jnp
from jax import lax
from jax.experimental import pallas as pl
from jax.experimental.pallas import tpu as pltpu
from jax.sharding import Mesh
from jax.sharding import PartitionSpec as P

HEAD_DIM = 72
SCALE = HEAD_DIM**-0.5
D = 1152
CW = 144
FW = 538
FP = 576
NA = 256
NB = 128
NT = NA + NB
CA = NA // 4
CB = NB // 4
V_AT, UP_AT = 256, 512
EXTRA = 8
norm_eps = 1e-06
gelu_coef = 0.7978845608028654
bf16 = jnp.bfloat16
f32 = jnp.float32
SIZES = {"y": 4, "x": 4, "c": 2, "zl": 2, ("zh", "zl"): 4}
Z = ("zh", "zl")
VMEM_LIMIT = 24 * 1024 * 1024


def shift(value, axis, by):
    n = SIZES[axis]
    return lax.ppermute(value, axis, [(i, (i + by) % n) for i in range(n)])


def dot(a, b):
    return lax.dot_general(a, b, (((1,), (0,)), ((), ())), preferred_element_type=f32)


def dot_nt(a, b):
    return lax.dot_general(a, b, (((1,), (1,)), ((), ())), preferred_element_type=f32)


def dot_tn(a, b):
    return lax.dot_general(a, b, (((0,), (0,)), ((), ())), preferred_element_type=f32)


def after(value, anchor):
    return lax.optimization_barrier((value, anchor))[0]


def shaped(shape, dtype):
    return jax.ShapeDtypeStruct(shape, dtype)


CHUNK = CA + CB
SENDS = [shaped((CHUNK, D), bf16)] * 3 + [shaped((CHUNK, D), f32)]


class Layer(NamedTuple):
    array: jax.Array
    index: int


def call(kernel, outs, *args, pos=None, scratch=()):
    specs = [pl.BlockSpec(memory_space=pltpu.VMEM)] * len(args)
    layers = [arg.index if isinstance(arg, Layer) else None for arg in args]
    args = [arg.array if isinstance(arg, Layer) else arg for arg in args]
    if any(layer is not None for layer in layers):
        on_layers, start = kernel, 0 if pos is None else 1

        def kernel(*refs):
            refs = list(refs)
            for i, layer in enumerate(layers, start):
                if layer is not None:
                    refs[i] = refs[i].at[layer]
            on_layers(*refs)

    if pos is not None:
        specs = [pl.BlockSpec(memory_space=pltpu.SMEM)] + specs
        args = (pos, *args)
    return pl.pallas_call(
        kernel,
        out_shape=outs,
        in_specs=specs,
        out_specs=[pl.BlockSpec(memory_space=pltpu.VMEM)] * len(outs),
        scratch_shapes=scratch,
        compiler_params=pltpu.CompilerParams(vmem_limit_bytes=VMEM_LIMIT),
    )(*args)


def whole(chunks):
    if len(chunks) == 1:
        return chunks[0][...]
    return jnp.concatenate([r[:CA] for r in chunks] + [r[CA:] for r in chunks], axis=0)


def put_sends(total, outs):
    for k in range(4):
        ref = outs[k - 1]
        ref[:CA] = total[CA * k : CA * (k + 1)].astype(ref.dtype)
        ref[CA:] = total[NA + CB * k : NA + CB * (k + 1)].astype(ref.dtype)


def ids_kernel(pos, near, far, qid_a, kid_a, qid_b, kid_b):
    first = pos[0] == 0
    x = pos[1]

    def turned(row, n):
        rows = jnp.broadcast_to(row, (8, n))
        return pltpu.roll(rows, (n - x * (n // 4)) % n, axis=1)

    def half(ref):
        return turned(jnp.where(first, ref[0:1], ref[1:2]), NA)

    def quarter(ref, own):
        low, high = ref[2:3, :NB], ref[2:3, NB:]
        return turned(jnp.where(first == own, low, high), NB)

    a, b = half(near), quarter(near, True)
    qid_a[...] = a.astype(f32).T.astype(jnp.int32)
    qid_b[...] = b.astype(f32).T.astype(jnp.int32)
    kid_a[...] = jnp.concatenate([a, half(far)], axis=1)
    kid_b[...] = jnp.concatenate(
        [b, quarter(far, True), quarter(near, False), quarter(far, False)], axis=1
    )


def arrange_ids(pos, near, far):
    i32 = jnp.int32
    outs = [shaped((NA, 8), i32), shaped((8, 2 * NA), i32)]
    outs += [shaped((NB, 8), i32), shaped((8, 4 * NB), i32)]
    return call(ids_kernel, outs, near, far, pos=pos)


def arranged(pos, ref):
    zl, x = pos[0], pos[1]
    rows, quarters = [], []
    for k in range(4):
        a = lax.rem(x + k, 4)
        rows.append(ref[zl, pl.ds(pl.multiple_of(a * CA, CA), CA)])
        quarters.append(ref[2, pl.ds(pl.multiple_of(zl * NB + a * CB, CB), CB)])
    return jnp.concatenate(rows + quarters, axis=0)


def first_kernel(pos, inputs, gain, bias, normed, stream):
    v = arranged(pos, inputs).astype(f32)
    stream[:CA] = v[:CA]
    stream[CA:] = v[NA : NA + CB]
    mean = jnp.mean(v, axis=-1, keepdims=True)
    centred = v - mean
    var = jnp.mean(centred * centred, axis=-1, keepdims=True)
    out = centred * lax.rsqrt(var + norm_eps) * gain[0, 0:1] + bias[0, 0:1]
    normed[...] = out.astype(bf16)


def cotangent_kernel(pos, cotangent, qid_a, qid_b, low, grad, total):
    live = jnp.concatenate([qid_a[...], qid_b[...]], axis=0)[:, :1] >= 0
    v = jnp.where(live, arranged(pos, cotangent).astype(f32), 0.0)
    low[...] = v.astype(bf16)
    own = jnp.concatenate([v[:CA], v[NA : NA + CB]], axis=0)
    grad[...] = own
    total[...] = jnp.sum(own, axis=0, keepdims=True)


def place_kernel(pos, *refs):
    out = refs[4]
    for dz in range(2):
        zl = pos[0] if dz == 0 else 1 - pos[0]
        for k in range(4):
            a = lax.rem(pos[1] + k, 4)
            chunk = refs[k].at[dz]
            out[zl, pl.ds(pl.multiple_of(a * CA, CA), CA)] = chunk[:CA].astype(out.dtype)
            out[2, pl.ds(pl.multiple_of(zl * NB + a * CB, CB), CB)] = chunk[CA:].astype(out.dtype)


def placed_rows(pos, slots, dtype):
    return call(place_kernel, [shaped((3, NA, D), dtype)], *slots, pos=pos)[0]


def norm_kernel(layer, at, stream, own, r1, r2, r3, extra, gain, bias, x_out, n_out):
    x = stream[...] + (own[...] + r1[...].astype(f32) + r2[...].astype(f32) + r3[...].astype(f32))
    x = x + extra[layer : layer + 1]
    x_out[...] = x
    mean = jnp.mean(x, axis=-1, keepdims=True)
    centred = x - mean
    var = jnp.mean(centred * centred, axis=-1, keepdims=True)
    g, b = (ref[at[0], at[1] : at[1] + 1] for ref in (gain, bias))
    n_out[...] = (centred * lax.rsqrt(var + norm_eps) * g + b).astype(bf16)


def norm_step(layer, at, stream, got, extra, gain, bias):
    return call(
        functools.partial(norm_kernel, layer, at),
        [shaped((CHUNK, D), f32), shaped((CHUNK, D), bf16)],
        stream, *got, extra, gain, bias,
    )


def result_kernel(layer, stream, own, r1, r2, r3, extra, out):
    x = stream[...] + (own[...] + r1[...].astype(f32) + r2[...].astype(f32) + r3[...].astype(f32))
    out[...] = (x + extra[layer : layer + 1]).astype(bf16)


def norm_back_kernel(at, x_ref, own, r1, r2, r3, grad_ref, gain, out, low, sums):
    x = x_ref[...]
    d = own[...] + r1[...].astype(f32) + r2[...].astype(f32) + r3[...].astype(f32)
    mean = jnp.mean(x, axis=-1, keepdims=True)
    centred = x - mean
    var = jnp.mean(centred * centred, axis=-1, keepdims=True)
    r = lax.rsqrt(var + norm_eps)
    xh = centred * r
    e = d * gain[at[0], at[1] : at[1] + 1]
    inner = e - jnp.mean(e, axis=-1, keepdims=True)
    inner = inner - xh * jnp.mean(e * xh, axis=-1, keepdims=True)
    grad = grad_ref[...] + r * inner
    out[...] = grad
    low[...] = grad.astype(bf16)
    sums[0:1] = jnp.sum(d * xh, axis=0, keepdims=True)
    sums[1:2] = jnp.sum(d, axis=0, keepdims=True)
    sums[2:3] = jnp.sum(grad, axis=0, keepdims=True)


def norm_back(at, x, got, grad, gain):
    return call(
        functools.partial(norm_back_kernel, at),
        [shaped((CHUNK, D), f32), shaped((CHUNK, D), bf16), shaped((3, D), f32)],
        x, *got, grad, gain,
    )


def qkv_kernel(layer, n, *refs):
    chunks, (w0, wa, wb, bias0, bias1) = refs[:n], refs[n : n + 5]
    q_out, kv_out, part_out = refs[n + 5 : n + 8]
    nt = whole(chunks)
    if n > 1:
        refs[n + 8][...] = nt
    w1 = jnp.concatenate([wa[: 3 * CW // 2], wb[: 3 * CW // 2]], axis=0)
    for g, w, bias in ((0, w0[...], bias0), (1, w1, bias1)):
        qb = bias[layer : layer + 1, :CW]
        vb = bias[layer : layer + 1, V_AT : V_AT + CW]
        q_out[g] = (dot_nt(nt, w[:CW]) + qb).astype(bf16)
        key = dot_nt(w[CW : 2 * CW], nt).astype(bf16)
        value = (dot_nt(nt, w[2 * CW :]) + vb).T.astype(bf16)
        kv_out[g, 0] = key
        kv_out[g, 1] = value
        part_out[1 - g, 0] = key[:, NA:]
        part_out[1 - g, 1] = value[:, NA:]


def project(layer, chunks, own, far, biases):
    n = len(chunks)
    outs = [shaped((2, NT, CW), bf16), shaped((2, 2, CW, NT), bf16), shaped((2, 2, CW, NB), bf16)]
    if n > 1:
        outs.append(shaped((NT, D), bf16))
    got = call(functools.partial(qkv_kernel, layer, n), outs, *chunks, own, *far, *biases)
    return (*got[:3], got[3] if n > 1 else chunks[0])


def lane_mask(head):
    lane = lax.broadcasted_iota(jnp.int32, (1, CW), 1)
    return (lane < HEAD_DIM) if head == 0 else (lane >= HEAD_DIM)


def row_mask(head):
    place = lax.broadcasted_iota(jnp.int32, (CW, 1), 0)
    return (place < HEAD_DIM) if head == 0 else (place >= HEAD_DIM)


def masked(mask, value):
    return jnp.where(mask, value.astype(f32), 0.0).astype(bf16)


def probabilities(qm, keys, allowed):
    scores = jnp.where(allowed, dot(qm, keys) * SCALE, -1e30)
    expanded = jnp.exp(scores - jnp.max(scores, axis=-1, keepdims=True))
    return expanded * (1.0 / jnp.sum(expanded, axis=-1, keepdims=True))


def slot_mask(qid, kid):
    return (kid >= 0) & ((qid == kid) | (qid < 0))


def out_rows_of(refs):
    if len(refs) == 1:
        return refs[0][...]
    return jnp.concatenate([ref[3 * CW // 2 :] for ref in refs], axis=0)


def attend_kernel(first, count, blocks, n_out, *refs):
    n = len(blocks)
    q, kvs, (qid, kid, wo0) = refs[0], refs[1 : 1 + n], refs[1 + n : 4 + n]
    wo1 = out_rows_of(refs[4 + n : 4 + n + n_out])
    rest = refs[4 + n + n_out :]
    allowed = slot_mask(qid[:, :1], kid[:1])
    mixed_out = rest[0] if first == 0 else rest[1]
    total = None
    for g, wo in ((0, wo0), (1, wo1)):
        keys = jnp.concatenate([r[g, 0, :, b : b + m] for r, (b, m) in zip(kvs, blocks)], axis=1)
        values = jnp.concatenate([r[g, 1, :, b : b + m] for r, (b, m) in zip(kvs, blocks)], axis=1)
        query = q[g, first : first + count]
        mixed = None
        for head in range(2):
            mask = lane_mask(head)
            probs = probabilities(masked(mask, query), keys, allowed).astype(bf16)
            got = dot_nt(probs, values)
            mixed = got if head == 0 else jnp.where(mask, got, mixed)
        mixed = mixed.astype(bf16)
        mixed_out[g] = mixed
        part = dot(mixed, wo[...])
        total = part if total is None else total + part
    if first == 0:
        rest[1][...] = total
    else:
        put_sends(jnp.concatenate([rest[0][...], total], axis=0), rest[2:])


def attend_row(q, kvs, blocks, qid, kid, wo):
    return call(
        functools.partial(attend_kernel, 0, NA, blocks, len(wo) - 1),
        [shaped((2, NA, CW), bf16), shaped((NA, D), f32)],
        q, *kvs, qid, kid, *wo,
    )


def attend_quarter(q, kvs, blocks, qid, kid, wo, total):
    return call(
        functools.partial(attend_kernel, NA, NB, blocks, len(wo) - 1),
        [shaped((2, NB, CW), bf16), *SENDS],
        q, *kvs, qid, kid, *wo, total,
    )


def attend_back_kernel(*refs):
    c0, c1, c2, c3, q, kv, kvo, kvz, kvd, qid_a, kid_a, qid_b, kid_b, wo0 = refs[:14]
    wo1 = out_rows_of(refs[14:-5])
    mid_out, dq_out, own_out, far_out, z_out = refs[-5:]
    allowed_a = slot_mask(qid_a[:, :1], kid_a[:1])
    allowed_b = slot_mask(qid_b[:, :1], kid_b[:1])
    mid = whole((c0, c1, c2, c3))
    mid_out[...] = mid
    for g, wo in ((0, wo0), (1, wo1)):
        d_mixed = dot_nt(mid, wo[...]).astype(bf16)
        d_mixed_t = dot_nt(wo[...], mid).astype(bf16)
        query = q[g]
        query_t = query.astype(f32).T.astype(bf16)
        for part in range(2):
            if part == 0:
                allowed, lo, hi = allowed_a, 0, NA
                keys = jnp.concatenate([kv[g, 0, :, :NA], kvo[g, 0, :, :NA]], axis=1)
                values = jnp.concatenate([kv[g, 1, :, :NA], kvo[g, 1, :, :NA]], axis=1)
            else:
                allowed, lo, hi = allowed_b, NA, NT
                keys = jnp.concatenate(
                    [kv[g, 0, :, NA:], kvo[g, 0, :, NA:], kvz[g, 0], kvd[g, 0]], axis=1
                )
                values = jnp.concatenate(
                    [kv[g, 1, :, NA:], kvo[g, 1, :, NA:], kvz[g, 1], kvd[g, 1]], axis=1
                )
            dq, dk, dv = None, None, None
            for head in range(2):
                mask, rmask = lane_mask(head), row_mask(head)
                probs = probabilities(masked(mask, query[lo:hi]), keys, allowed)
                d_probs = dot(masked(mask, d_mixed[lo:hi]), values)
                inner = jnp.sum(d_probs * probs, axis=-1, keepdims=True)
                d_raw = (SCALE * probs * (d_probs - inner)).astype(bf16)
                got_q = dot_nt(keys, d_raw)
                got_k = dot(query_t[:, lo:hi], d_raw)
                got_v = dot(d_mixed_t[:, lo:hi], probs.astype(bf16))
                if head == 0:
                    dq, dk, dv = got_q, got_k, got_v
                else:
                    dq = jnp.where(rmask, got_q, dq)
                    dk = jnp.where(rmask, got_k, dk)
                    dv = jnp.where(rmask, got_v, dv)
            dq_out[g, :, lo:hi] = dq.astype(bf16)
            n = hi - lo
            for j, grad in ((0, dk), (1, dv)):
                own_out[g, j, :, lo:hi] = grad[:, :n]
                far_out[g, j, :, lo:hi] = grad[:, n : 2 * n].astype(bf16)
                if part == 1:
                    z_out[1 - g, j] = grad[:, 2 * n : 3 * n]
                    far_out[1 - g, j, :, NT:] = grad[:, 3 * n :].astype(bf16)


def attend_back(chunks, q, kv, kvo, kvz, kvd, ids, wo):
    return call(
        attend_back_kernel,
        [
            shaped((NT, D), bf16),
            shaped((2, CW, NT), bf16),
            shaped((2, 2, CW, NT), f32),
            shaped((2, 2, CW, NT + NB), bf16),
            shaped((2, 2, CW, NB), f32),
        ],
        *chunks, q, kv, kvo, kvz, kvd, *ids, *wo,
    )


def project_back_kernel(dq, own, far, dz, w0, wa, wb, stack_out, sums, *sends):
    total = None
    ones = jnp.ones((8, NT), bf16)
    w1 = jnp.concatenate([wa[: 3 * CW // 2], wb[: 3 * CW // 2]], axis=0)
    for g, w in ((0, w0[...]), (1, w1)):
        stack_out[g, 0] = dq[g]
        sums[g, 0] = dot_nt(ones, dq[g])
        for j in range(2):
            grad = own[g, j] + far[g, j, :, :NT].astype(f32)
            low = jnp.concatenate(
                [grad[:, :NA], grad[:, NA:] + dz[g, j].astype(f32)], axis=1
            ).astype(bf16)
            stack_out[g, 1 + j] = low
            if j == 1:
                sums[g, 1] = dot_nt(ones, low)
        for j in range(3):
            part = dot_tn(stack_out[g, j], w[CW * j : CW * (j + 1)])
            total = part if total is None else total + part
    put_sends(total, sends)


def project_back(dq, own, far, dz, w0, w1):
    return call(
        project_back_kernel,
        [shaped((2, 3, CW, NT), bf16), shaped((2, 2, 8, CW), f32), *SENDS],
        dq, own, far, dz, w0, *w1,
    )


def mlp_kernel(
    layer, c0, c1, c2, c3, bias0, bias1, wu0, wd0, wu1, wd1, nt_out, up_out, act_out, *sends
):
    nt = whole((c0, c1, c2, c3))
    nt_out[...] = nt
    total = None
    for g, wu, bias, wd in ((0, wu0, bias0, wd0), (1, wu1, bias1, wd1)):
        u = dot_nt(nt, wu[...]) + bias[layer : layer + 1, UP_AT : UP_AT + FP]
        up_out[g] = u
        act = (0.5 * u * (1.0 + jnp.tanh(gelu_coef * (u + 0.044715 * u * u * u)))).astype(bf16)
        act_out[g] = act
        part = dot(act, wd[...])
        total = part if total is None else total + part
    put_sends(total, sends)


def mlp(layer, chunks, own, oth, biases):
    return call(
        functools.partial(mlp_kernel, layer),
        [
            shaped((NT, D), bf16),
            shaped((2, NT, FP), f32),
            shaped((2, NT, FP), bf16),
            *SENDS,
        ],
        *chunks, *biases, own[2], own[3], oth[2], oth[3],
    )


def mlp_back_kernel(n, *refs):
    chunks, (up, wu0, wd0) = refs[:n], refs[n : n + 3]
    wu1, wd1 = refs[n + 3 : n + 5]
    d_up_out, sums = refs[n + 5 : n + 7]
    sends = refs[n + 7 : n + 11]
    low = whole(chunks)
    if n > 1:
        refs[n + 11][...] = low
    total = None
    for g, wu, wd in ((0, wu0, wd0), (1, wu1, wd1)):
        d_act = dot_nt(low, wd[...])
        u = up[g]
        t = jnp.tanh(gelu_coef * (u + 0.044715 * u * u * u))
        slope = 0.5 * (1.0 + t) + 0.5 * u * (1.0 - t * t) * (
            gelu_coef * (1.0 + 3 * 0.044715 * u * u)
        )
        d_up = (d_act * slope).astype(bf16)
        d_up_out[g] = d_up
        sums[g] = jnp.sum(d_up.astype(f32), axis=0, keepdims=True)
        part = dot(d_up, wu[...])
        total = part if total is None else total + part
    put_sends(total, sends)


def mlp_back(chunks, up, own, oth):
    n = len(chunks)
    outs = [shaped((2, NT, FP), bf16), shaped((2, 1, FP), f32), *SENDS]
    if n > 1:
        outs.append(shaped((NT, D), bf16))
    got = call(
        functools.partial(mlp_back_kernel, n), outs, *chunks, up, own[2], own[3], oth[2], oth[3]
    )
    return got[0], got[1], got[2:6], (got[6] if n > 1 else chunks[0])


def mlp_weights_kernel(pos, d_up, act, nt, low, keep_out, sent_out):
    first = pos[2] == 0
    for j, (a, b) in enumerate(((d_up, nt), (act, low))):
        for out, g in ((keep_out, 0), (sent_out, 1)):
            picked = jnp.where(first, a[g], a[1 - g])
            got = dot_tn(picked, b[...]).astype(bf16)
            for k in range(2):
                out[2 * j + k] = got[2 * CW * k : 2 * CW * (k + 1)]


def attend_weights_kernel(
    pos, stacked, mixed_a, mixed_b, normed, mid, qv0, qv1, up0, up1, keep_out, sent_out, extra
):
    plain_weights_kernel(pos, stacked, mixed_a, mixed_b, normed, mid, keep_out, sent_out)
    first = pos[2] == 0
    for out, g in ((keep_out, 0), (sent_out, 1)):
        extra[...] = jnp.zeros_like(extra)
        for layer, (qv, up) in enumerate(((qv0, up0), (qv1, up1))):
            row = slice(4 + layer, 5 + layer)
            extra[row, :CW] = jnp.where(first, qv[g, 0, :1], qv[1 - g, 0, :1])
            extra[row, V_AT : V_AT + CW] = jnp.where(first, qv[g, 1, :1], qv[1 - g, 1, :1])
            extra[row, UP_AT : UP_AT + FP] = jnp.where(first, up[g], up[1 - g])
        for j in range(4):
            rows = extra[...] if j == 1 else jnp.zeros_like(extra)
            out[j, CW:] = rows.astype(bf16)


def plain_weights_kernel(pos, stacked, mixed_a, mixed_b, normed, mid, keep_out, sent_out):
    first = pos[2] == 0
    for out, g in ((keep_out, 0), (sent_out, 1)):
        for j in range(3):
            picked = jnp.where(first, stacked[g, j], stacked[1 - g, j])
            out[j, :CW] = dot(picked, normed[...]).astype(bf16)
        mixed = [jnp.concatenate([mixed_a[i], mixed_b[i]], axis=0) for i in (g, 1 - g)]
        out[3, :CW] = dot_tn(jnp.where(first, mixed[0], mixed[1]), mid[...]).astype(bf16)


def mlp_final_kernel(pos, *refs):
    first = pos[2] == 0
    for j, out in enumerate(refs[8:]):
        for layer in range(2):
            full, other = refs[4 * j + 2 * layer : 4 * j + 2 * layer + 2]
            out[:, layer, :] = jnp.where(first, full[...], other[...]).astype(f32)


def mlp_final(pos, sums):
    rows = 2 * CW
    args = [part for _ in range(2) for total in sums for part in total]
    specs = [pl.BlockSpec(memory_space=pltpu.SMEM)]
    for j in range(2):
        specs += [pl.BlockSpec((None, rows, D), lambda i, j=j: (2 * j + i, 0, 0))] * 4
    return pl.pallas_call(
        mlp_final_kernel,
        grid=(2,),
        out_shape=[shaped((FW, 2, D), f32)] * 2,
        in_specs=specs,
        out_specs=[pl.BlockSpec((rows, 2, D), lambda i: (i, 0, 0))] * 2,
        compiler_params=pltpu.CompilerParams(vmem_limit_bytes=VMEM_LIMIT),
    )(pos, *args)


def wide_kernel(one0, two0, one1, two1, down, out):
    rows = [one0[0:1], two0[0:1], one0[1:2], two0[1:3], one1[2:3]]
    rows += [one1[0:1], two1[0:1], one1[1:2], two1[1:3], down[...]]
    rows.append(jnp.zeros((2 * EXTRA - 12, D), f32))
    out[...] = jnp.concatenate(rows, axis=0).reshape(out.shape)


def attend_final_kernel(
    pos, full0, other0, full1, other1, qkv, out, gain, bias, q_bias, v_bias, out_bias, up, down
):
    first = pos[2] == 0
    for layer, (full, other) in enumerate(((full0, other0), (full1, other1))):
        for j in range(4):
            got = jnp.where(first, full[j, :CW], other[j, :CW]).astype(f32)
            if j < 3:
                qkv[layer, j] = got
            else:
                out[layer] = got
    small = [jnp.where(first, full0[j, CW:], other0[j, CW:]).astype(f32) for j in range(2)]
    small = jnp.concatenate(small, axis=0)
    for layer in range(2):
        at = 6 * layer
        gain[layer] = small[at : at + 2]
        bias[layer] = small[at + 2 : at + 4]
        out_bias[layer : layer + 1] = small[at + 4 : at + 5]
        down[layer : layer + 1] = small[at + 5 : at + 6]
        row = small[12 + layer : 13 + layer]
        q_bias[layer : layer + 1] = row[:, :CW]
        v_bias[layer : layer + 1] = row[:, V_AT : V_AT + CW]
        up[layer : layer + 1] = row[:, UP_AT : UP_AT + FW]


def attend_final(pos, sums):
    args = [part for total in sums for part in total]
    outs = [(2, 3, CW, D), (2, CW, D), (2, 2, D), (2, 2, D), (2, CW), (2, CW), (2, D)]
    outs = [shaped(shape, f32) for shape in (*outs, (2, FW), (2, D))]
    return call(attend_final_kernel, outs, *args, pos=pos)


def gather_x(chunk):
    return [chunk] + [shift(chunk, "x", -k) for k in (1, 2, 3)]


def scatter_x(sends):
    return [sends[3]] + [shift(sends[k - 1], "x", k) for k in (1, 2, 3)]


def scatter_ring(pieces, axis):
    return [pieces[0]] + [shift(pieces[k], axis, k) for k in (1, 2, 3)]


def gather_ring(piece, axis, some):
    got = [piece]
    for k in (1, 2, 3):
        if not some:
            got.append(shift(piece, axis, -k))
        elif axis == "y":
            pairs = [
                (((y + k) % 4) * 4 + e, y * 4 + e) for y in range(4) for e in (0, 3)
            ]
            got.append(lax.ppermute(piece, ("y", "c", "zl"), pairs))
        else:
            pairs = []
            for z in range(4):
                c = z % 2
                src = (z + k) % 4
                pairs.append(
                    ((src // 2) * 4 + c * 2 + src % 2, (z // 2) * 4 + c * 2 + z % 2)
                )
            got.append(lax.ppermute(piece, ("zh", "c", "zl"), pairs))
    return got


def pieces_kernel(pos, kept, far, *outs):
    for k in range(4):
        block = lax.rem(pos[0] + k, 4)
        outs[k][...] = (kept[block].astype(f32) + far[block].astype(f32)).astype(bf16)


def sum_pieces(index, kept, far):
    outs = [shaped(kept.shape[1:], bf16)] * 4
    return call(pieces_kernel, outs, kept, far, pos=index)


def last_piece_kernel(pos, *refs):
    late, out = refs[-2:]
    total = sum(ref[...].astype(f32) for ref in refs[:4])
    out[:CW] = total[:CW].astype(bf16)
    rows = late[jnp.minimum(pos[0], 1)]
    out[CW:] = (total[CW:] + jnp.where(pos[0] < 2, rows, 0.0)).astype(bf16)


def total_kernel(*refs):
    refs[-1][...] = sum(ref[...].astype(f32) for ref in refs[:-1]).astype(bf16)


def sum_parts(*parts):
    return call(total_kernel, [shaped(parts[0].shape, bf16)], *parts)[0]


def blocks_kernel(pos, *refs):
    for k in range(4):
        refs[4][lax.rem(pos[0] + k, 4)] = refs[k][...]


def place_blocks(index, parts):
    return call(blocks_kernel, [shaped((4, *parts[0].shape), bf16)], *parts, pos=index)[0]


def sum_ring(value, axis):
    return value + sum(shift(value, axis, k) for k in range(1, SIZES[axis]))


def local(
    inputs,
    picture_ids,
    cotangent,
    norm_gain,
    norm_bias,
    w_qkv,
    q_bias,
    v_bias,
    w_out,
    out_bias,
    w_up,
    up_bias,
    w_down,
    down_bias,
):
    layers = w_qkv.shape[0]
    zl, c, x, y = (lax.axis_index(name) for name in ("zl", "c", "x", "y"))
    pos = jnp.stack([zl, x, jnp.where(zl == c, 0, 1)]).astype(jnp.int32)

    z_index = (lax.axis_index("zh") * 2 + zl)[None]
    here = picture_ids[0, 0] > -2

    def apart(work):
        shapes = jax.eval_shape(work)
        return lax.cond(
            here, work, lambda: jax.tree.map(lambda s: jnp.zeros(s.shape, s.dtype), shapes)
        )

    wq_t = jnp.swapaxes(w_qkv, 2, 3).reshape(layers, 3 * CW, D)
    half = 3 * CW // 2

    wq_far = [(shift(wq_t[0, :half], Z, 1), shift(wq_t[0, half:], Z, -1))]
    normed, stream = call(
        first_kernel, [shaped((NT, D), bf16), shaped((CHUNK, D), f32)],
        inputs, norm_gain, norm_bias, pos=pos,
    )
    w_out, w_up, w_down, q_bias, v_bias, up_bias = after(
        (w_out, w_up, w_down, q_bias, v_bias, up_bias), normed
    )
    bias = jnp.concatenate(
        [
            jnp.pad(part, ((0, 0), (0, size - part.shape[1])))
            for part, size in ((q_bias, V_AT), (v_bias, UP_AT - V_AT), (up_bias, FP))
        ],
        axis=1,
    )
    biases = (bias, shift(bias, "zl", 1))
    ids_far = shift(picture_ids, "c", 1)
    pad = ((0, FP - FW), (0, 0))
    wide_weights = [
        (jnp.pad(w_up[layer].T, pad), jnp.pad(w_down[layer], pad)) for layer in range(layers)
    ]
    out_far = [(shift(w_out[0], Z, 1),)]
    ids = arrange_ids(pos, picture_ids, ids_far)

    def far_wide(layer, anchor):
        up_rows, down_rows = after(wide_weights[layer], anchor)
        return shift(up_rows, Z, 1), shift(down_rows, Z, -1)

    def keys_step(layer, chunks):
        q, kv, part, normed = project(layer, chunks, Layer(wq_t, layer), wq_far[layer], biases)
        kvo = shift(kv, "c", 1)
        kvz = shift(part, "zl", 1)
        kvd = shift(kvz, "c", 1)
        wo = (Layer(w_out, layer), *out_far[layer])
        mixed_a, total_a = attend_row(q, (kv, kvo), ((0, NA), (0, NA)), ids[0], ids[1], wo)
        return q, kv, kvo, kvz, kvd, normed, wo, mixed_a, total_a

    def attention_step(layer, q, kv, kvo, kvz, kvd, wo, total_a, stream):
        mixed_b, *sends = attend_quarter(
            q, (kv, kvo, kvz, kvd), ((NA, NB), (NA, NB), (0, NB), (0, NB)),
            ids[2], ids[3], wo, total_a,
        )
        got = scatter_x(sends)
        middle, low = norm_step(layer, (layer, 1), stream, got, out_bias, norm_gain, norm_bias)
        return mixed_b, middle, gather_x(low)

    normed = after(normed, (wide_weights, ids))
    q, kv, kvo, kvz, kvd, normed, wo, mixed_a, total_a = keys_step(0, [normed])
    wide_far = [far_wide(0, (kvz, *out_far[0]))]
    def first_attention():
        split = (3 * CW + CW) // 2 - half
        sends = (
            jnp.concatenate([wq_t[1, :half], w_out[1, :split]], axis=0),
            jnp.concatenate([wq_t[1, half:], w_out[1, split:]], axis=0),
        )
        done = attention_step(0, q, kv, kvo, kvz, kvd, wo, total_a, stream)
        return done, sends

    (mixed_b, middle, chunks), next_sends = apart(first_attention)
    own = (Layer(wq_t, 0), Layer(w_out, 0), *wide_weights[0])
    weights = [(own, (wq_far[0], out_far[0], *wide_far[0]))]
    sent_up, sent_down = shift(next_sends[0], Z, 1), shift(next_sends[1], Z, -1)
    wq_far.append((sent_up, sent_down))
    out_far.append((sent_up, sent_down))

    def first_mlp():
        normed_two, up, act, *sends = mlp(0, chunks, *weights[0], biases)
        got = scatter_x(sends)
        stream, low = norm_step(0, (1, 0), middle, got, down_bias, norm_gain, norm_bias)
        return normed_two, up, act, stream, gather_x(low)

    normed_two, up, act, stream1, chunks1 = apart(first_mlp)
    kept = [(stream, normed, q, kv, kvo, kvz, kvd, mixed_a, mixed_b, middle, normed_two, up, act)]

    chunks1 = after(chunks1, wq_far[1])
    q1, kv1, kvo1, kvz1, kvd1, normed1, wo1, mixed_a1, total_a1 = keys_step(1, chunks1)
    wide_far.append(far_wide(1, (kvz1, total_a1)))

    def second_attention():
        low = call(
            cotangent_kernel,
            [shaped((NT, D), bf16), shaped((CHUNK, D), f32), shaped((1, D), f32)],
            cotangent, ids[0], ids[2], pos=pos,
        )
        return attention_step(1, q1, kv1, kvo1, kvz1, kvd1, wo1, total_a1, stream1), low

    (mixed_b1, middle1, chunks), (low_in, grad_flow, d_down_bias) = apart(second_attention)
    own = (Layer(wq_t, 1), Layer(w_out, 1), *wide_weights[1])
    weights.append((own, (wq_far[1], out_far[1], *wide_far[1])))
    normed_two, up, act, *last_sends = mlp(1, chunks, *weights[1], biases)
    kept.append(
        (stream1, normed1, q1, kv1, kvo1, kvz1, kvd1, mixed_a1, mixed_b1, middle1, normed_two, up, act)
    )

    def feed_forward_back(layer, chunks, grad_flow):
        own, oth = weights[layer]
        middle, normed_two, up, act = kept[layer][-4:]
        d_up, d_up_bias, sends, grad_low = mlp_back(chunks, up, own, oth)
        got = scatter_x(sends)
        kept_m, sent_m = call(
            mlp_weights_kernel, [shaped((4, 2 * CW, D), bf16)] * 2,
            d_up, act, normed_two, grad_low, pos=pos,
        )
        grad_mid, mid_low, norm_two = norm_back((layer, 1), middle, got, grad_flow, norm_gain)
        return grad_mid, mid_low, norm_two, d_up_bias, (kept_m, sent_m)

    def gather_mid(mid_low, *kept_and_sent):
        sums = [sum_parts(kept, shift(sent, "c", 1)) for kept, sent in kept_and_sent]
        return gather_x(mid_low), sums

    def attention_back(layer, mid_chunks, last_result=None):
        own, oth = weights[layer]
        q, kv, kvo, kvz, kvd = kept[layer][2:7]
        mid, dq, d_own, d_far, d_z = attend_back(
            mid_chunks, q, kv, kvo, kvz, kvd, ids, (own[1], *oth[1])
        )
        d_far = shift(d_far, "c", 1)
        d_z = shift((d_z + d_far[..., NT:].astype(f32)).astype(bf16), "zl", 1)
        result = None
        if last_result is not None:
            result = last_result()
            d_z = after(d_z, result)
        stacked, d_qv_bias, *sends = project_back(dq, d_own, d_far, d_z, own[0], oth[0])
        return mid, stacked, d_qv_bias, scatter_x(sends), result

    def last_result():
        return call(
            functools.partial(result_kernel, layers - 1), [shaped((CHUNK, D), bf16)],
            middle1, *scatter_x(last_sends), down_bias,
        )[0]

    grad_mid1, mid_low1, norm_two1, d_up_bias1, part_m1 = feed_forward_back(
        1, [low_in], grad_flow
    )
    mid_chunks1, (feed_m1,) = apart(lambda: gather_mid(mid_low1, part_m1))
    sum_m1 = lax.psum(feed_m1, ("y", "zh", "zl"))

    def first_block():
        stream_in, normed = kept[1][:2]
        mid, stacked, d_qv_bias, got, _ = attention_back(1, mid_chunks1)
        part_a = call(
            plain_weights_kernel, [shaped((4, CW, D), bf16)] * 2,
            stacked, *kept[1][7:9], normed, mid, pos=pos,
        )
        grad_flow, low, norm_one = norm_back((1, 0), stream_in, got, grad_mid1, norm_gain)
        chunks = gather_x(low)
        back = feed_forward_back(0, chunks, grad_flow)
        return d_qv_bias, norm_one, part_a, back

    d_qv_bias1, norm_one1, part_a1, back = apart(first_block)
    grad_mid0, mid_low0, norm_two0, d_up_bias0, part_m0 = back
    mid_chunks0, (feed_a1, feed_m0) = apart(lambda: gather_mid(mid_low0, part_a1, part_m0))
    sum_a1, sum_m0 = lax.psum((feed_a1, feed_m0), ("zh", "zl", "y"))

    def second_block():
        stream_in, normed = kept[0][:2]
        mid, stacked, d_qv_bias0, got, result = attention_back(0, mid_chunks0, last_result)
        part_a = call(
            attend_weights_kernel, [shaped((4, CW + EXTRA, D), bf16)] * 2,
            stacked, *kept[0][7:9], normed, mid, d_qv_bias0, d_qv_bias1, d_up_bias0, d_up_bias1,
            pos=pos, scratch=[pltpu.VMEM((EXTRA, D), f32)],
        )
        _, low, norm_one = norm_back((0, 0), stream_in, got, grad_mid0, norm_gain)
        pieces = sum_pieces(z_index, part_a[0], shift(part_a[1], "c", 1))
        return low, norm_one, pieces, result

    low, norm_one0, pieces, result = apart(second_block)

    def first_sums():
        parts = scatter_ring(pieces, Z)
        both = jnp.stack([low, shift(low, "zl", 1)])
        in_slots = gather_x(both)
        late = call(
            wide_kernel, [shaped((2, EXTRA, D), f32)],
            norm_one0, norm_two0, norm_one1, norm_two1, d_down_bias,
        )[0]
        late = sum_ring(late + shift(late, "c", 1), "x")
        late = sum_ring(after(late, parts), Z)
        piece = call(
            last_piece_kernel, [shaped((CW + EXTRA, D), bf16)], *parts, late, pos=z_index
        )[0]
        return in_slots, piece, jnp.stack([result, shift(result, "zl", 1)])

    in_slots, piece, results = apart(first_sums)

    def second_sums():
        parts = [piece] + [shift(piece, "y", k) for k in (1, 2, 3)]
        out_slots = gather_x(results)
        return sum_parts(*parts), out_slots

    total, out_slots = apart(second_sums)

    def last_sums():
        parts = gather_ring(total, Z, True)
        sums = [(part, shift(part, "c", 1)) for part in (sum_m0, sum_m1)]
        weight_grads = mlp_final(pos, sums)
        parts = after(parts, weight_grads)
        full = place_blocks(z_index, parts)
        input_grad = placed_rows(pos, in_slots, f32)
        outputs = placed_rows(pos, out_slots, bf16)
        other_a1 = shift(after(sum_a1, parts[1]), "c", 1)
        return input_grad, outputs, (full, shift(full, "c", 1)), (sum_a1, other_a1), weight_grads

    input_grad, outputs, sum_a0, sum_a1, (d_up, d_down) = apart(last_sums)
    d_qkv, d_out, d_gain, d_bias, d_q, d_v, d_out_bias, d_up_bias, d_down_bias = attend_final(
        pos, (sum_a0, sum_a1)
    )
    return (
        outputs,
        input_grad,
        d_gain,
        d_bias,
        jnp.swapaxes(d_qkv, 2, 3),
        d_q,
        d_v,
        d_out,
        d_out_bias,
        jnp.transpose(d_up, (1, 2, 0)),
        d_up_bias,
        jnp.transpose(d_down, (1, 0, 2)),
        d_down_bias,
    )


def solution(mesh):
    cut = Mesh(mesh.devices.reshape(4, 2, 2, 2, 4), ("y", "zh", "c", "zl", "x"))
    dp, tensor = ("y", "zh"), ("zl", "x")
    weight_specs = (
        P(),
        P(),
        P(None, None, None, tensor),
        P(None, tensor),
        P(None, tensor),
        P(None, tensor, None),
        P(),
        P(None, None, tensor),
        P(None, tensor),
        P(None, tensor, None),
        P(),
    )
    return jax.shard_map(
        local,
        mesh=cut,
        in_specs=(P(dp, "c", None), P(dp, "c"), P(dp, "c", None), *weight_specs),
        out_specs=(P(dp, "c", None), P(dp, "c", None), *weight_specs),
        check_vma=False,
    )
```

```python
import functools
from typing import NamedTuple

import jax
import jax.numpy as jnp
from jax import lax
from jax.experimental import pallas as pl
from jax.experimental.pallas import tpu as pltpu
from jax.sharding import Mesh
from jax.sharding import PartitionSpec as P

HEAD_DIM = 72
SCALE = HEAD_DIM**-0.5
D = 1152
CW = 144
FW = 538
FP = 544
HF = FP // 2
NA = 256
NB = 128
NT = NA + NB
CA = NA // 4
CB = NB // 4
V_AT, UP_AT = 256, 512
EXTRA = 8
norm_eps = 1e-06
gelu_coef = 0.7978845608028654
bf16 = jnp.bfloat16
f32 = jnp.float32
SIZES = {"y": 4, "x": 4, "c": 2, "zl": 2, ("zh", "zl"): 4}
Z = ("zh", "zl")
VMEM_LIMIT = 24 * 1024 * 1024


def shift(value, axis, by):
    n = SIZES[axis]
    return lax.ppermute(value, axis, [(i, (i + by) % n) for i in range(n)])


def dot(a, b):
    return lax.dot_general(a, b, (((1,), (0,)), ((), ())), preferred_element_type=f32)


def dot_nt(a, b):
    return lax.dot_general(a, b, (((1,), (1,)), ((), ())), preferred_element_type=f32)


def dot_tn(a, b):
    return lax.dot_general(a, b, (((0,), (0,)), ((), ())), preferred_element_type=f32)


def after(value, anchor):
    return lax.optimization_barrier((value, anchor))[0]


def shaped(shape, dtype):
    return jax.ShapeDtypeStruct(shape, dtype)


CHUNK = CA + CB
SENDS = [shaped((CHUNK, D), bf16)] * 3 + [shaped((CHUNK, D), f32)]


class Layer(NamedTuple):
    array: jax.Array
    index: int


def call(kernel, outs, *args, pos=None, scratch=()):
    specs = [pl.BlockSpec(memory_space=pltpu.VMEM)] * len(args)
    layers = [arg.index if isinstance(arg, Layer) else None for arg in args]
    args = [arg.array if isinstance(arg, Layer) else arg for arg in args]
    if any(layer is not None for layer in layers):
        on_layers, start = kernel, 0 if pos is None else 1

        def kernel(*refs):
            refs = list(refs)
            for i, layer in enumerate(layers, start):
                if layer is not None:
                    refs[i] = refs[i].at[layer]
            on_layers(*refs)

    if pos is not None:
        specs = [pl.BlockSpec(memory_space=pltpu.SMEM)] + specs
        args = (pos, *args)
    return pl.pallas_call(
        kernel,
        out_shape=outs,
        in_specs=specs,
        out_specs=[pl.BlockSpec(memory_space=pltpu.VMEM)] * len(outs),
        scratch_shapes=scratch,
        compiler_params=pltpu.CompilerParams(vmem_limit_bytes=VMEM_LIMIT),
    )(*args)


def whole(chunks):
    if len(chunks) == 1:
        return chunks[0][...]
    return jnp.concatenate([r[:CA] for r in chunks] + [r[CA:] for r in chunks], axis=0)


def put_sends(total, outs):
    for k in range(4):
        ref = outs[k - 1]
        ref[:CA] = total[CA * k : CA * (k + 1)].astype(ref.dtype)
        ref[CA:] = total[NA + CB * k : NA + CB * (k + 1)].astype(ref.dtype)


def ids_kernel(pos, near, far, qid_a, kid_a, qid_b, kid_b):
    first = pos[0] == 0
    x = pos[1]

    def turned(row, n):
        rows = jnp.broadcast_to(row, (8, n))
        return pltpu.roll(rows, (n - x * (n // 4)) % n, axis=1)

    def half(ref):
        return turned(jnp.where(first, ref[0:1], ref[1:2]), NA)

    def quarter(ref, own):
        low, high = ref[2:3, :NB], ref[2:3, NB:]
        return turned(jnp.where(first == own, low, high), NB)

    a, b = half(near), quarter(near, True)
    qid_a[...] = a.astype(f32).T.astype(jnp.int32)
    qid_b[...] = b.astype(f32).T.astype(jnp.int32)
    kid_a[...] = jnp.concatenate([a, half(far)], axis=1)
    kid_b[...] = jnp.concatenate(
        [b, quarter(far, True), quarter(near, False), quarter(far, False)], axis=1
    )


def arrange_ids(pos, near, far):
    i32 = jnp.int32
    outs = [shaped((NA, 8), i32), shaped((8, 2 * NA), i32)]
    outs += [shaped((NB, 8), i32), shaped((8, 4 * NB), i32)]
    return call(ids_kernel, outs, near, far, pos=pos)


def arranged(pos, ref):
    zl, x = pos[0], pos[1]
    rows, quarters = [], []
    for k in range(4):
        a = lax.rem(x + k, 4)
        rows.append(ref[zl, pl.ds(pl.multiple_of(a * CA, CA), CA)])
        quarters.append(ref[2, pl.ds(pl.multiple_of(zl * NB + a * CB, CB), CB)])
    return jnp.concatenate(rows + quarters, axis=0)


def first_kernel(pos, inputs, gain, bias, normed, stream):
    v = arranged(pos, inputs).astype(f32)
    stream[:CA] = v[:CA]
    stream[CA:] = v[NA : NA + CB]
    mean = jnp.mean(v, axis=-1, keepdims=True)
    centred = v - mean
    var = jnp.mean(centred * centred, axis=-1, keepdims=True)
    out = centred * lax.rsqrt(var + norm_eps) * gain[0, 0:1] + bias[0, 0:1]
    normed[...] = out.astype(bf16)


def cotangent_kernel(pos, cotangent, qid_a, qid_b, low, grad, total):
    live = jnp.concatenate([qid_a[...], qid_b[...]], axis=0)[:, :1] >= 0
    v = jnp.where(live, arranged(pos, cotangent).astype(f32), 0.0)
    low[...] = v.astype(bf16)
    own = jnp.concatenate([v[:CA], v[NA : NA + CB]], axis=0)
    grad[...] = own
    total[...] = jnp.sum(own, axis=0, keepdims=True)


def place_kernel(pos, *refs):
    out = refs[4]
    for dz in range(2):
        zl = pos[0] if dz == 0 else 1 - pos[0]
        for k in range(4):
            a = lax.rem(pos[1] + k, 4)
            chunk = refs[k].at[dz]
            out[zl, pl.ds(pl.multiple_of(a * CA, CA), CA)] = chunk[:CA].astype(out.dtype)
            out[2, pl.ds(pl.multiple_of(zl * NB + a * CB, CB), CB)] = chunk[CA:].astype(out.dtype)


def placed_rows(pos, slots, dtype):
    return call(place_kernel, [shaped((3, NA, D), dtype)], *slots, pos=pos)[0]


def norm_kernel(layer, at, stream, own, r1, r2, r3, extra, gain, bias, x_out, n_out):
    x = stream[...] + (own[...] + r1[...].astype(f32) + r2[...].astype(f32) + r3[...].astype(f32))
    x = x + extra[layer : layer + 1]
    x_out[...] = x
    mean = jnp.mean(x, axis=-1, keepdims=True)
    centred = x - mean
    var = jnp.mean(centred * centred, axis=-1, keepdims=True)
    g, b = (ref[at[0], at[1] : at[1] + 1] for ref in (gain, bias))
    n_out[...] = (centred * lax.rsqrt(var + norm_eps) * g + b).astype(bf16)


def norm_step(layer, at, stream, got, extra, gain, bias):
    return call(
        functools.partial(norm_kernel, layer, at),
        [shaped((CHUNK, D), f32), shaped((CHUNK, D), bf16)],
        stream, *got, extra, gain, bias,
    )


def result_kernel(layer, stream, own, r1, r2, r3, extra, out):
    x = stream[...] + (own[...] + r1[...].astype(f32) + r2[...].astype(f32) + r3[...].astype(f32))
    out[...] = (x + extra[layer : layer + 1]).astype(bf16)


def norm_back_kernel(at, x_ref, own, r1, r2, r3, grad_ref, gain, out, low, sums):
    x = x_ref[...]
    d = own[...] + r1[...].astype(f32) + r2[...].astype(f32) + r3[...].astype(f32)
    mean = jnp.mean(x, axis=-1, keepdims=True)
    centred = x - mean
    var = jnp.mean(centred * centred, axis=-1, keepdims=True)
    r = lax.rsqrt(var + norm_eps)
    xh = centred * r
    e = d * gain[at[0], at[1] : at[1] + 1]
    inner = e - jnp.mean(e, axis=-1, keepdims=True)
    inner = inner - xh * jnp.mean(e * xh, axis=-1, keepdims=True)
    grad = grad_ref[...] + r * inner
    out[...] = grad
    low[...] = grad.astype(bf16)
    sums[0:1] = jnp.sum(d * xh, axis=0, keepdims=True)
    sums[1:2] = jnp.sum(d, axis=0, keepdims=True)
    sums[2:3] = jnp.sum(grad, axis=0, keepdims=True)


def norm_back(at, x, got, grad, gain):
    return call(
        functools.partial(norm_back_kernel, at),
        [shaped((CHUNK, D), f32), shaped((CHUNK, D), bf16), shaped((3, D), f32)],
        x, *got, grad, gain,
    )


def qkv_kernel(layer, n, *refs):
    chunks, (w0, wa, wb, bias0, bias1) = refs[:n], refs[n : n + 5]
    q_out, kv_out, part_out = refs[n + 5 : n + 8]
    nt = whole(chunks)
    if n > 1:
        refs[n + 8][...] = nt
    w1 = jnp.concatenate([wa[: 3 * CW // 2], wb[: 3 * CW // 2]], axis=0)
    for g, w, bias in ((0, w0[...], bias0), (1, w1, bias1)):
        qb = bias[layer : layer + 1, :CW]
        vb = bias[layer : layer + 1, V_AT : V_AT + CW]
        q_out[g] = (dot_nt(nt, w[:CW]) + qb).astype(bf16)
        key = dot_nt(w[CW : 2 * CW], nt).astype(bf16)
        value = (dot_nt(nt, w[2 * CW :]) + vb).T.astype(bf16)
        kv_out[g, 0] = key
        kv_out[g, 1] = value
        part_out[1 - g, 0] = key[:, NA:]
        part_out[1 - g, 1] = value[:, NA:]


def project(layer, chunks, own, far, biases):
    n = len(chunks)
    outs = [shaped((2, NT, CW), bf16), shaped((2, 2, CW, NT), bf16), shaped((2, 2, CW, NB), bf16)]
    if n > 1:
        outs.append(shaped((NT, D), bf16))
    got = call(functools.partial(qkv_kernel, layer, n), outs, *chunks, own, *far, *biases)
    return (*got[:3], got[3] if n > 1 else chunks[0])


def lane_mask(head):
    lane = lax.broadcasted_iota(jnp.int32, (1, CW), 1)
    return (lane < HEAD_DIM) if head == 0 else (lane >= HEAD_DIM)


def row_mask(head):
    place = lax.broadcasted_iota(jnp.int32, (CW, 1), 0)
    return (place < HEAD_DIM) if head == 0 else (place >= HEAD_DIM)


def masked(mask, value):
    return jnp.where(mask, value.astype(f32), 0.0).astype(bf16)


def probabilities(qm, keys, allowed):
    scores = jnp.where(allowed, dot(qm, keys) * SCALE, -1e30)
    expanded = jnp.exp(scores - jnp.max(scores, axis=-1, keepdims=True))
    return expanded * (1.0 / jnp.sum(expanded, axis=-1, keepdims=True))


def slot_mask(qid, kid):
    return (kid >= 0) & ((qid == kid) | (qid < 0))


def out_rows_of(refs):
    if len(refs) == 1:
        return refs[0][...]
    return jnp.concatenate([ref[3 * CW // 2 :] for ref in refs], axis=0)


def attend_kernel(first, count, blocks, n_out, *refs):
    n = len(blocks)
    q, kvs, (qid, kid, wo0) = refs[0], refs[1 : 1 + n], refs[1 + n : 4 + n]
    wo1 = out_rows_of(refs[4 + n : 4 + n + n_out])
    rest = refs[4 + n + n_out :]
    allowed = slot_mask(qid[:, :1], kid[:1])
    mixed_out = rest[0] if first == 0 else rest[1]
    total = None
    for g, wo in ((0, wo0), (1, wo1)):
        keys = jnp.concatenate([r[g, 0, :, b : b + m] for r, (b, m) in zip(kvs, blocks)], axis=1)
        values = jnp.concatenate([r[g, 1, :, b : b + m] for r, (b, m) in zip(kvs, blocks)], axis=1)
        query = q[g, first : first + count]
        mixed = None
        for head in range(2):
            mask = lane_mask(head)
            probs = probabilities(masked(mask, query), keys, allowed).astype(bf16)
            got = dot_nt(probs, values)
            mixed = got if head == 0 else jnp.where(mask, got, mixed)
        mixed = mixed.astype(bf16)
        mixed_out[g] = mixed
        part = dot(mixed, wo[...])
        total = part if total is None else total + part
    if first == 0:
        rest[1][...] = total
    else:
        put_sends(jnp.concatenate([rest[0][...], total], axis=0), rest[2:])


def attend_row(q, kvs, blocks, qid, kid, wo):
    return call(
        functools.partial(attend_kernel, 0, NA, blocks, len(wo) - 1),
        [shaped((2, NA, CW), bf16), shaped((NA, D), f32)],
        q, *kvs, qid, kid, *wo,
    )


def attend_quarter(q, kvs, blocks, qid, kid, wo, total):
    return call(
        functools.partial(attend_kernel, NA, NB, blocks, len(wo) - 1),
        [shaped((2, NB, CW), bf16), *SENDS],
        q, *kvs, qid, kid, *wo, total,
    )


def attend_back_kernel(*refs):
    c0, c1, c2, c3, q, kv, kvo, kvz, kvd, qid_a, kid_a, qid_b, kid_b, wo0 = refs[:14]
    wo1 = out_rows_of(refs[14:-5])
    mid_out, dq_out, own_out, far_out, z_out = refs[-5:]
    allowed_a = slot_mask(qid_a[:, :1], kid_a[:1])
    allowed_b = slot_mask(qid_b[:, :1], kid_b[:1])
    mid = whole((c0, c1, c2, c3))
    mid_out[...] = mid
    for g, wo in ((0, wo0), (1, wo1)):
        d_mixed = dot_nt(mid, wo[...]).astype(bf16)
        d_mixed_t = dot_nt(wo[...], mid).astype(bf16)
        query = q[g]
        query_t = query.astype(f32).T.astype(bf16)
        for part in range(2):
            if part == 0:
                allowed, lo, hi = allowed_a, 0, NA
                keys = jnp.concatenate([kv[g, 0, :, :NA], kvo[g, 0, :, :NA]], axis=1)
                values = jnp.concatenate([kv[g, 1, :, :NA], kvo[g, 1, :, :NA]], axis=1)
            else:
                allowed, lo, hi = allowed_b, NA, NT
                keys = jnp.concatenate(
                    [kv[g, 0, :, NA:], kvo[g, 0, :, NA:], kvz[g, 0], kvd[g, 0]], axis=1
                )
                values = jnp.concatenate(
                    [kv[g, 1, :, NA:], kvo[g, 1, :, NA:], kvz[g, 1], kvd[g, 1]], axis=1
                )
            dq, dk, dv = None, None, None
            for head in range(2):
                mask, rmask = lane_mask(head), row_mask(head)
                probs = probabilities(masked(mask, query[lo:hi]), keys, allowed)
                d_probs = dot(masked(mask, d_mixed[lo:hi]), values)
                inner = jnp.sum(d_probs * probs, axis=-1, keepdims=True)
                d_raw = (SCALE * probs * (d_probs - inner)).astype(bf16)
                got_q = dot_nt(keys, d_raw)
                got_k = dot(query_t[:, lo:hi], d_raw)
                got_v = dot(d_mixed_t[:, lo:hi], probs.astype(bf16))
                if head == 0:
                    dq, dk, dv = got_q, got_k, got_v
                else:
                    dq = jnp.where(rmask, got_q, dq)
                    dk = jnp.where(rmask, got_k, dk)
                    dv = jnp.where(rmask, got_v, dv)
            dq_out[g, :, lo:hi] = dq.astype(bf16)
            n = hi - lo
            for j, grad in ((0, dk), (1, dv)):
                own_out[g, j, :, lo:hi] = grad[:, :n]
                far_out[g, j, :, lo:hi] = grad[:, n : 2 * n].astype(bf16)
                if part == 1:
                    z_out[1 - g, j] = grad[:, 2 * n : 3 * n]
                    far_out[1 - g, j, :, NT:] = grad[:, 3 * n :].astype(bf16)


def attend_back(chunks, q, kv, kvo, kvz, kvd, ids, wo):
    return call(
        attend_back_kernel,
        [
            shaped((NT, D), bf16),
            shaped((2, CW, NT), bf16),
            shaped((2, 2, CW, NT), f32),
            shaped((2, 2, CW, NT + NB), bf16),
            shaped((2, 2, CW, NB), f32),
        ],
        *chunks, q, kv, kvo, kvz, kvd, *ids, *wo,
    )


def project_back_kernel(dq, own, far, dz, w0, wa, wb, stack_out, sums, *sends):
    total = None
    ones = jnp.ones((8, NT), bf16)
    w1 = jnp.concatenate([wa[: 3 * CW // 2], wb[: 3 * CW // 2]], axis=0)
    for g, w in ((0, w0[...]), (1, w1)):
        stack_out[g, 0] = dq[g]
        sums[g, 0] = dot_nt(ones, dq[g])
        for j in range(2):
            grad = own[g, j] + far[g, j, :, :NT].astype(f32)
            low = jnp.concatenate(
                [grad[:, :NA], grad[:, NA:] + dz[g, j].astype(f32)], axis=1
            ).astype(bf16)
            stack_out[g, 1 + j] = low
            if j == 1:
                sums[g, 1] = dot_nt(ones, low)
        for j in range(3):
            part = dot_tn(stack_out[g, j], w[CW * j : CW * (j + 1)])
            total = part if total is None else total + part
    put_sends(total, sends)


def project_back(dq, own, far, dz, w0, w1):
    return call(
        project_back_kernel,
        [shaped((2, 3, CW, NT), bf16), shaped((2, 2, 8, CW), f32), *SENDS],
        dq, own, far, dz, w0, *w1,
    )


def mlp_kernel(
    layer, c0, c1, c2, c3, bias0, bias1, wu0, wd0, wu1, wd1, nt_out, up_out, act_out, *sends
):
    nt = whole((c0, c1, c2, c3))
    nt_out[...] = nt
    total = None
    for g, wu, bias, wd in ((0, wu0, bias0, wd0), (1, wu1, bias1, wd1)):
        u = dot_nt(nt, wu[...]) + bias[layer : layer + 1, UP_AT : UP_AT + FP]
        up_out[g] = u
        act = (0.5 * u * (1.0 + jnp.tanh(gelu_coef * (u + 0.044715 * u * u * u)))).astype(bf16)
        act_out[g] = act
        part = dot(act, wd[...])
        total = part if total is None else total + part
    put_sends(total, sends)


def mlp(layer, chunks, own, oth, biases):
    return call(
        functools.partial(mlp_kernel, layer),
        [
            shaped((NT, D), bf16),
            shaped((2, NT, FP), f32),
            shaped((2, NT, FP), bf16),
            *SENDS,
        ],
        *chunks, *biases, own[2], own[3], oth[2], oth[3],
    )


def mlp_back_kernel(n, *refs):
    chunks, (up, wu0, wd0) = refs[:n], refs[n : n + 3]
    wu1, wd1 = refs[n + 3 : n + 5]
    d_up_out, sums = refs[n + 5 : n + 7]
    sends = refs[n + 7 : n + 11]
    low = whole(chunks)
    if n > 1:
        refs[n + 11][...] = low
    total = None
    for g, wu, wd in ((0, wu0, wd0), (1, wu1, wd1)):
        d_act = dot_nt(low, wd[...])
        u = up[g]
        t = jnp.tanh(gelu_coef * (u + 0.044715 * u * u * u))
        slope = 0.5 * (1.0 + t) + 0.5 * u * (1.0 - t * t) * (
            gelu_coef * (1.0 + 3 * 0.044715 * u * u)
        )
        d_up = (d_act * slope).astype(bf16)
        d_up_out[g] = d_up
        sums[g] = jnp.sum(d_up.astype(f32), axis=0, keepdims=True)
        part = dot(d_up, wu[...])
        total = part if total is None else total + part
    put_sends(total, sends)


def mlp_back(chunks, up, own, oth):
    n = len(chunks)
    outs = [shaped((2, NT, FP), bf16), shaped((2, 1, FP), f32), *SENDS]
    if n > 1:
        outs.append(shaped((NT, D), bf16))
    got = call(
        functools.partial(mlp_back_kernel, n), outs, *chunks, up, own[2], own[3], oth[2], oth[3]
    )
    return got[0], got[1], got[2:6], (got[6] if n > 1 else chunks[0])


def mlp_weights_kernel(pos, d_up, act, nt, low, keep_out, sent_out):
    first = pos[2] == 0
    for j, (a, b) in enumerate(((d_up, nt), (act, low))):
        for out, g in ((keep_out, 0), (sent_out, 1)):
            picked = jnp.where(first, a[g], a[1 - g])
            got = dot_tn(picked, b[...]).astype(bf16)
            for k in range(2):
                out[2 * j + k] = got[HF * k : HF * (k + 1)]


def attend_weights_kernel(
    pos, stacked, mixed_a, mixed_b, normed, mid, qv0, qv1, up0, up1, keep_out, sent_out, extra
):
    plain_weights_kernel(pos, stacked, mixed_a, mixed_b, normed, mid, keep_out, sent_out)
    first = pos[2] == 0
    for out, g in ((keep_out, 0), (sent_out, 1)):
        extra[...] = jnp.zeros_like(extra)
        for layer, (qv, up) in enumerate(((qv0, up0), (qv1, up1))):
            row = slice(4 + layer, 5 + layer)
            extra[row, :CW] = jnp.where(first, qv[g, 0, :1], qv[1 - g, 0, :1])
            extra[row, V_AT : V_AT + CW] = jnp.where(first, qv[g, 1, :1], qv[1 - g, 1, :1])
            extra[row, UP_AT : UP_AT + FP] = jnp.where(first, up[g], up[1 - g])
        for j in range(4):
            rows = extra[...] if j == 1 else jnp.zeros_like(extra)
            out[j, CW:] = rows.astype(bf16)


def plain_weights_kernel(pos, stacked, mixed_a, mixed_b, normed, mid, keep_out, sent_out):
    first = pos[2] == 0
    for out, g in ((keep_out, 0), (sent_out, 1)):
        for j in range(3):
            picked = jnp.where(first, stacked[g, j], stacked[1 - g, j])
            out[j, :CW] = dot(picked, normed[...]).astype(bf16)
        mixed = [jnp.concatenate([mixed_a[i], mixed_b[i]], axis=0) for i in (g, 1 - g)]
        out[3, :CW] = dot_tn(jnp.where(first, mixed[0], mixed[1]), mid[...]).astype(bf16)


def mlp_final_kernel(pos, *refs):
    first = pos[2] == 0
    for j, out in enumerate(refs[8:]):
        for layer in range(2):
            full, other = refs[4 * j + 2 * layer : 4 * j + 2 * layer + 2]
            out[:, layer, :] = jnp.where(first, full[...], other[...]).astype(f32)


def mlp_final(pos, sums):
    rows = HF
    args = [part for _ in range(2) for total in sums for part in total]
    specs = [pl.BlockSpec(memory_space=pltpu.SMEM)]
    for j in range(2):
        specs += [pl.BlockSpec((None, rows, D), lambda i, j=j: (2 * j + i, 0, 0))] * 4
    return pl.pallas_call(
        mlp_final_kernel,
        grid=(2,),
        out_shape=[shaped((FW, 2, D), f32)] * 2,
        in_specs=specs,
        out_specs=[pl.BlockSpec((rows, 2, D), lambda i: (i, 0, 0))] * 2,
        compiler_params=pltpu.CompilerParams(vmem_limit_bytes=VMEM_LIMIT),
    )(pos, *args)


def wide_kernel(one0, two0, one1, two1, down, out):
    rows = [one0[0:1], two0[0:1], one0[1:2], two0[1:3], one1[2:3]]
    rows += [one1[0:1], two1[0:1], one1[1:2], two1[1:3], down[...]]
    rows.append(jnp.zeros((2 * EXTRA - 12, D), f32))
    out[...] = jnp.concatenate(rows, axis=0).reshape(out.shape)


def attend_final_kernel(
    pos, full0, other0, full1, other1, qkv, out, gain, bias, q_bias, v_bias, out_bias, up, down
):
    first = pos[2] == 0
    for layer, (full, other) in enumerate(((full0, other0), (full1, other1))):
        for j in range(4):
            got = jnp.where(first, full[j, :CW], other[j, :CW]).astype(f32)
            if j < 3:
                qkv[layer, j] = got
            else:
                out[layer] = got
    small = [jnp.where(first, full0[j, CW:], other0[j, CW:]).astype(f32) for j in range(2)]
    small = jnp.concatenate(small, axis=0)
    for layer in range(2):
        at = 6 * layer
        gain[layer] = small[at : at + 2]
        bias[layer] = small[at + 2 : at + 4]
        out_bias[layer : layer + 1] = small[at + 4 : at + 5]
        down[layer : layer + 1] = small[at + 5 : at + 6]
        row = small[12 + layer : 13 + layer]
        q_bias[layer : layer + 1] = row[:, :CW]
        v_bias[layer : layer + 1] = row[:, V_AT : V_AT + CW]
        up[layer : layer + 1] = row[:, UP_AT : UP_AT + FW]


def attend_final(pos, sums):
    args = [part for total in sums for part in total]
    outs = [(2, 3, CW, D), (2, CW, D), (2, 2, D), (2, 2, D), (2, CW), (2, CW), (2, D)]
    outs = [shaped(shape, f32) for shape in (*outs, (2, FW), (2, D))]
    return call(attend_final_kernel, outs, *args, pos=pos)


def gather_x(chunk):
    return [chunk] + [shift(chunk, "x", -k) for k in (1, 2, 3)]


def scatter_x(sends):
    return [sends[3]] + [shift(sends[k - 1], "x", k) for k in (1, 2, 3)]


def scatter_ring(pieces, axis):
    return [pieces[0]] + [shift(pieces[k], axis, k) for k in (1, 2, 3)]


def gather_ring(piece, axis, some):
    got = [piece]
    for k in (1, 2, 3):
        if not some:
            got.append(shift(piece, axis, -k))
        elif axis == "y":
            pairs = [
                (((y + k) % 4) * 4 + e, y * 4 + e) for y in range(4) for e in (0, 3)
            ]
            got.append(lax.ppermute(piece, ("y", "c", "zl"), pairs))
        else:
            pairs = []
            for z in range(4):
                c = z % 2
                src = (z + k) % 4
                pairs.append(
                    ((src // 2) * 4 + c * 2 + src % 2, (z // 2) * 4 + c * 2 + z % 2)
                )
            got.append(lax.ppermute(piece, ("zh", "c", "zl"), pairs))
    return got


def pieces_kernel(pos, kept, far, *outs):
    for k in range(4):
        block = lax.rem(pos[0] + k, 4)
        outs[k][...] = (kept[block].astype(f32) + far[block].astype(f32)).astype(bf16)


def sum_pieces(index, kept, far):
    outs = [shaped(kept.shape[1:], bf16)] * 4
    return call(pieces_kernel, outs, kept, far, pos=index)


def last_piece_kernel(pos, *refs):
    late, out = refs[-2:]
    total = sum(ref[...].astype(f32) for ref in refs[:4])
    out[:CW] = total[:CW].astype(bf16)
    rows = late[jnp.minimum(pos[0], 1)]
    out[CW:] = (total[CW:] + jnp.where(pos[0] < 2, rows, 0.0)).astype(bf16)


def total_kernel(*refs):
    refs[-1][...] = sum(ref[...].astype(f32) for ref in refs[:-1]).astype(bf16)


def sum_parts(*parts):
    return call(total_kernel, [shaped(parts[0].shape, bf16)], *parts)[0]


def blocks_kernel(pos, *refs):
    for k in range(4):
        refs[4][lax.rem(pos[0] + k, 4)] = refs[k][...]


def place_blocks(index, parts):
    return call(blocks_kernel, [shaped((4, *parts[0].shape), bf16)], *parts, pos=index)[0]


def sum_ring(value, axis):
    return value + sum(shift(value, axis, k) for k in range(1, SIZES[axis]))


def local(
    inputs,
    picture_ids,
    cotangent,
    norm_gain,
    norm_bias,
    w_qkv,
    q_bias,
    v_bias,
    w_out,
    out_bias,
    w_up,
    up_bias,
    w_down,
    down_bias,
):
    layers = w_qkv.shape[0]
    zl, c, x, y = (lax.axis_index(name) for name in ("zl", "c", "x", "y"))
    pos = jnp.stack([zl, x, jnp.where(zl == c, 0, 1)]).astype(jnp.int32)

    z_index = (lax.axis_index("zh") * 2 + zl)[None]
    here = picture_ids[0, 0] > -2

    def apart(work):
        shapes = jax.eval_shape(work)
        return lax.cond(
            here, work, lambda: jax.tree.map(lambda s: jnp.zeros(s.shape, s.dtype), shapes)
        )

    wq_t = jnp.swapaxes(w_qkv, 2, 3).reshape(layers, 3 * CW, D)
    half = 3 * CW // 2

    wq_far = [(shift(wq_t[0, :half], Z, 1), shift(wq_t[0, half:], Z, -1))]
    normed, stream = call(
        first_kernel, [shaped((NT, D), bf16), shaped((CHUNK, D), f32)],
        inputs, norm_gain, norm_bias, pos=pos,
    )
    w_out, w_up, w_down, q_bias, v_bias, up_bias = after(
        (w_out, w_up, w_down, q_bias, v_bias, up_bias), normed
    )
    bias = jnp.concatenate(
        [
            jnp.pad(part, ((0, 0), (0, size - part.shape[1])))
            for part, size in ((q_bias, V_AT), (v_bias, UP_AT - V_AT), (up_bias, FP))
        ],
        axis=1,
    )
    biases = (bias, shift(bias, "zl", 1))
    ids_far = shift(picture_ids, "c", 1)
    pad = ((0, FP - FW), (0, 0))
    wide_weights = [
        (jnp.pad(w_up[layer].T, pad), jnp.pad(w_down[layer], pad)) for layer in range(layers)
    ]
    out_far = [(shift(w_out[0], Z, 1),)]
    ids = arrange_ids(pos, picture_ids, ids_far)

    def far_wide(layer, anchor):
        up_rows, down_rows = after(wide_weights[layer], anchor)
        return shift(up_rows, Z, 1), shift(down_rows, Z, -1)

    def keys_step(layer, chunks):
        q, kv, part, normed = project(layer, chunks, Layer(wq_t, layer), wq_far[layer], biases)
        kvo = shift(kv, "c", 1)
        kvz = shift(part, "zl", 1)
        kvd = shift(kvz, "c", 1)
        wo = (Layer(w_out, layer), *out_far[layer])
        mixed_a, total_a = attend_row(q, (kv, kvo), ((0, NA), (0, NA)), ids[0], ids[1], wo)
        return q, kv, kvo, kvz, kvd, normed, wo, mixed_a, total_a

    def attention_step(layer, q, kv, kvo, kvz, kvd, wo, total_a, stream):
        mixed_b, *sends = attend_quarter(
            q, (kv, kvo, kvz, kvd), ((NA, NB), (NA, NB), (0, NB), (0, NB)),
            ids[2], ids[3], wo, total_a,
        )
        got = scatter_x(sends)
        middle, low = norm_step(layer, (layer, 1), stream, got, out_bias, norm_gain, norm_bias)
        return mixed_b, middle, gather_x(low)

    normed = after(normed, (wide_weights, ids))
    q, kv, kvo, kvz, kvd, normed, wo, mixed_a, total_a = keys_step(0, [normed])
    wide_far = [far_wide(0, (kvz, *out_far[0]))]
    def first_attention():
        split = (3 * CW + CW) // 2 - half
        sends = (
            jnp.concatenate([wq_t[1, :half], w_out[1, :split]], axis=0),
            jnp.concatenate([wq_t[1, half:], w_out[1, split:]], axis=0),
        )
        done = attention_step(0, q, kv, kvo, kvz, kvd, wo, total_a, stream)
        return done, sends

    (mixed_b, middle, chunks), next_sends = apart(first_attention)
    own = (Layer(wq_t, 0), Layer(w_out, 0), *wide_weights[0])
    weights = [(own, (wq_far[0], out_far[0], *wide_far[0]))]
    sent_up, sent_down = shift(next_sends[0], Z, 1), shift(next_sends[1], Z, -1)
    wq_far.append((sent_up, sent_down))
    out_far.append((sent_up, sent_down))

    def first_mlp():
        normed_two, up, act, *sends = mlp(0, chunks, *weights[0], biases)
        got = scatter_x(sends)
        stream, low = norm_step(0, (1, 0), middle, got, down_bias, norm_gain, norm_bias)
        return normed_two, up, act, stream, gather_x(low)

    normed_two, up, act, stream1, chunks1 = apart(first_mlp)
    kept = [(stream, normed, q, kv, kvo, kvz, kvd, mixed_a, mixed_b, middle, normed_two, up, act)]

    chunks1 = after(chunks1, wq_far[1])
    q1, kv1, kvo1, kvz1, kvd1, normed1, wo1, mixed_a1, total_a1 = keys_step(1, chunks1)
    wide_far.append(far_wide(1, (kvz1, total_a1)))

    def second_attention():
        low = call(
            cotangent_kernel,
            [shaped((NT, D), bf16), shaped((CHUNK, D), f32), shaped((1, D), f32)],
            cotangent, ids[0], ids[2], pos=pos,
        )
        return attention_step(1, q1, kv1, kvo1, kvz1, kvd1, wo1, total_a1, stream1), low

    (mixed_b1, middle1, chunks), (low_in, grad_flow, d_down_bias) = apart(second_attention)
    own = (Layer(wq_t, 1), Layer(w_out, 1), *wide_weights[1])
    weights.append((own, (wq_far[1], out_far[1], *wide_far[1])))
    normed_two, up, act, *last_sends = mlp(1, chunks, *weights[1], biases)
    kept.append(
        (stream1, normed1, q1, kv1, kvo1, kvz1, kvd1, mixed_a1, mixed_b1, middle1, normed_two, up, act)
    )

    def feed_forward_back(layer, chunks, grad_flow):
        own, oth = weights[layer]
        middle, normed_two, up, act = kept[layer][-4:]
        d_up, d_up_bias, sends, grad_low = mlp_back(chunks, up, own, oth)
        got = scatter_x(sends)
        kept_m, sent_m = call(
            mlp_weights_kernel, [shaped((4, HF, D), bf16)] * 2,
            d_up, act, normed_two, grad_low, pos=pos,
        )
        grad_mid, mid_low, norm_two = norm_back((layer, 1), middle, got, grad_flow, norm_gain)
        return grad_mid, mid_low, norm_two, d_up_bias, (kept_m, sent_m)

    def gather_mid(mid_low, *kept_and_sent):
        sums = [sum_parts(kept, shift(sent, "c", 1)) for kept, sent in kept_and_sent]
        return gather_x(mid_low), sums

    def attention_back(layer, mid_chunks, last_result=None):
        own, oth = weights[layer]
        q, kv, kvo, kvz, kvd = kept[layer][2:7]
        mid, dq, d_own, d_far, d_z = attend_back(
            mid_chunks, q, kv, kvo, kvz, kvd, ids, (own[1], *oth[1])
        )
        d_far = shift(d_far, "c", 1)
        d_z = shift((d_z + d_far[..., NT:].astype(f32)).astype(bf16), "zl", 1)
        result = None
        if last_result is not None:
            result = last_result()
            d_z = after(d_z, result)
        stacked, d_qv_bias, *sends = project_back(dq, d_own, d_far, d_z, own[0], oth[0])
        return mid, stacked, d_qv_bias, scatter_x(sends), result

    def last_result():
        return call(
            functools.partial(result_kernel, layers - 1), [shaped((CHUNK, D), bf16)],
            middle1, *scatter_x(last_sends), down_bias,
        )[0]

    grad_mid1, mid_low1, norm_two1, d_up_bias1, part_m1 = feed_forward_back(
        1, [low_in], grad_flow
    )
    mid_chunks1, (feed_m1,) = apart(lambda: gather_mid(mid_low1, part_m1))
    sum_m1 = lax.psum(feed_m1, ("y", "zh", "zl"))

    def first_block():
        stream_in, normed = kept[1][:2]
        mid, stacked, d_qv_bias, got, _ = attention_back(1, mid_chunks1)
        part_a = call(
            plain_weights_kernel, [shaped((4, CW, D), bf16)] * 2,
            stacked, *kept[1][7:9], normed, mid, pos=pos,
        )
        grad_flow, low, norm_one = norm_back((1, 0), stream_in, got, grad_mid1, norm_gain)
        chunks = gather_x(low)
        back = feed_forward_back(0, chunks, grad_flow)
        return d_qv_bias, norm_one, part_a, back

    d_qv_bias1, norm_one1, part_a1, back = apart(first_block)
    grad_mid0, mid_low0, norm_two0, d_up_bias0, part_m0 = back
    mid_chunks0, (feed_a1, feed_m0) = apart(lambda: gather_mid(mid_low0, part_a1, part_m0))
    sum_a1, sum_m0 = lax.psum((feed_a1, feed_m0), ("zh", "zl", "y"))

    def second_block():
        stream_in, normed = kept[0][:2]
        mid, stacked, d_qv_bias0, got, result = attention_back(0, mid_chunks0, last_result)
        part_a = call(
            attend_weights_kernel, [shaped((4, CW + EXTRA, D), bf16)] * 2,
            stacked, *kept[0][7:9], normed, mid, d_qv_bias0, d_qv_bias1, d_up_bias0, d_up_bias1,
            pos=pos, scratch=[pltpu.VMEM((EXTRA, D), f32)],
        )
        _, low, norm_one = norm_back((0, 0), stream_in, got, grad_mid0, norm_gain)
        pieces = sum_pieces(z_index, part_a[0], shift(part_a[1], "c", 1))
        return low, norm_one, pieces, result

    low, norm_one0, pieces, result = apart(second_block)

    def first_sums():
        parts = scatter_ring(pieces, Z)
        both = jnp.stack([low, shift(low, "zl", 1)])
        in_slots = gather_x(both)
        late = call(
            wide_kernel, [shaped((2, EXTRA, D), f32)],
            norm_one0, norm_two0, norm_one1, norm_two1, d_down_bias,
        )[0]
        late = sum_ring(late + shift(late, "c", 1), "x")
        late = sum_ring(after(late, parts), Z)
        piece = call(
            last_piece_kernel, [shaped((CW + EXTRA, D), bf16)], *parts, late, pos=z_index
        )[0]
        return in_slots, piece, jnp.stack([result, shift(result, "zl", 1)])

    in_slots, piece, results = apart(first_sums)

    def second_sums():
        parts = [piece] + [shift(piece, "y", k) for k in (1, 2, 3)]
        out_slots = gather_x(results)
        return sum_parts(*parts), out_slots

    total, out_slots = apart(second_sums)

    def last_sums():
        parts = gather_ring(total, Z, True)
        sums = [(part, shift(part, "c", 1)) for part in (sum_m0, sum_m1)]
        weight_grads = mlp_final(pos, sums)
        parts = after(parts, weight_grads)
        full = place_blocks(z_index, parts)
        input_grad = placed_rows(pos, in_slots, f32)
        outputs = placed_rows(pos, out_slots, bf16)
        other_a1 = shift(after(sum_a1, parts[1]), "c", 1)
        return input_grad, outputs, (full, shift(full, "c", 1)), (sum_a1, other_a1), weight_grads

    input_grad, outputs, sum_a0, sum_a1, (d_up, d_down) = apart(last_sums)
    d_qkv, d_out, d_gain, d_bias, d_q, d_v, d_out_bias, d_up_bias, d_down_bias = attend_final(
        pos, (sum_a0, sum_a1)
    )
    return (
        outputs,
        input_grad,
        d_gain,
        d_bias,
        jnp.swapaxes(d_qkv, 2, 3),
        d_q,
        d_v,
        d_out,
        d_out_bias,
        jnp.transpose(d_up, (1, 2, 0)),
        d_up_bias,
        jnp.transpose(d_down, (1, 0, 2)),
        d_down_bias,
    )


def solution(mesh):
    cut = Mesh(mesh.devices.reshape(4, 2, 2, 2, 4), ("y", "zh", "c", "zl", "x"))
    dp, tensor = ("y", "zh"), ("zl", "x")
    weight_specs = (
        P(),
        P(),
        P(None, None, None, tensor),
        P(None, tensor),
        P(None, tensor),
        P(None, tensor, None),
        P(),
        P(None, None, tensor),
        P(None, tensor),
        P(None, tensor, None),
        P(),
    )
    return jax.shard_map(
        local,
        mesh=cut,
        in_specs=(P(dp, "c", None), P(dp, "c"), P(dp, "c", None), *weight_specs),
        out_specs=(P(dp, "c", None), P(dp, "c", None), *weight_specs),
        check_vma=False,
    )
```

```python
import functools
from typing import NamedTuple

import jax
import jax.numpy as jnp
from jax import lax
from jax.experimental import pallas as pl
from jax.experimental.pallas import tpu as pltpu
from jax.sharding import Mesh
from jax.sharding import PartitionSpec as P

HEAD_DIM = 72
SCALE = HEAD_DIM**-0.5
D = 1152
CW = 144
FW = 538
FP = 544
HF = FP // 2
NA = 256
NB = 128
NT = NA + NB
CA = NA // 4
CB = NB // 4
V_AT, UP_AT = 256, 512
EXTRA = 8
norm_eps = 1e-06
gelu_coef = 0.7978845608028654
bf16 = jnp.bfloat16
f32 = jnp.float32
SIZES = {"y": 4, "x": 4, "c": 2, "zl": 2, ("zh", "zl"): 4}
Z = ("zh", "zl")
VMEM_LIMIT = 24 * 1024 * 1024


def shift(value, axis, by):
    n = SIZES[axis]
    return lax.ppermute(value, axis, [(i, (i + by) % n) for i in range(n)])


def dot(a, b):
    return lax.dot_general(a, b, (((1,), (0,)), ((), ())), preferred_element_type=f32)


def dot_nt(a, b):
    return lax.dot_general(a, b, (((1,), (1,)), ((), ())), preferred_element_type=f32)


def dot_tn(a, b):
    return lax.dot_general(a, b, (((0,), (0,)), ((), ())), preferred_element_type=f32)


def after(value, anchor):
    return lax.optimization_barrier((value, anchor))[0]


def shaped(shape, dtype):
    return jax.ShapeDtypeStruct(shape, dtype)


CHUNK = CA + CB
SENDS = [shaped((CHUNK, D), bf16)] * 3 + [shaped((CHUNK, D), f32)]


class Layer(NamedTuple):
    array: jax.Array
    index: int


def call(kernel, outs, *args, pos=None, scratch=()):
    specs = [pl.BlockSpec(memory_space=pltpu.VMEM)] * len(args)
    layers = [arg.index if isinstance(arg, Layer) else None for arg in args]
    args = [arg.array if isinstance(arg, Layer) else arg for arg in args]
    if any(layer is not None for layer in layers):
        on_layers, start = kernel, 0 if pos is None else 1

        def kernel(*refs):
            refs = list(refs)
            for i, layer in enumerate(layers, start):
                if layer is not None:
                    refs[i] = refs[i].at[layer]
            on_layers(*refs)

    if pos is not None:
        specs = [pl.BlockSpec(memory_space=pltpu.SMEM)] + specs
        args = (pos, *args)
    return pl.pallas_call(
        kernel,
        out_shape=outs,
        in_specs=specs,
        out_specs=[pl.BlockSpec(memory_space=pltpu.VMEM)] * len(outs),
        scratch_shapes=scratch,
        compiler_params=pltpu.CompilerParams(vmem_limit_bytes=VMEM_LIMIT),
    )(*args)


def whole(chunks):
    if len(chunks) == 1:
        return chunks[0][...]
    return jnp.concatenate([r[:CA] for r in chunks] + [r[CA:] for r in chunks], axis=0)


def put_sends(total, outs):
    for k in range(4):
        ref = outs[k - 1]
        ref[:CA] = total[CA * k : CA * (k + 1)].astype(ref.dtype)
        ref[CA:] = total[NA + CB * k : NA + CB * (k + 1)].astype(ref.dtype)


def ids_kernel(pos, near, far, qid_a, kid_a, qid_b, kid_b):
    first = pos[0] == 0
    x = pos[1]

    def turned(row, n):
        rows = jnp.broadcast_to(row, (8, n))
        return pltpu.roll(rows, (n - x * (n // 4)) % n, axis=1)

    def half(ref):
        return turned(jnp.where(first, ref[0:1], ref[1:2]), NA)

    def quarter(ref, own):
        low, high = ref[2:3, :NB], ref[2:3, NB:]
        return turned(jnp.where(first == own, low, high), NB)

    a, b = half(near), quarter(near, True)
    qid_a[...] = a.astype(f32).T.astype(jnp.int32)
    qid_b[...] = b.astype(f32).T.astype(jnp.int32)
    kid_a[...] = jnp.concatenate([a, half(far)], axis=1)
    kid_b[...] = jnp.concatenate(
        [b, quarter(far, True), quarter(near, False), quarter(far, False)], axis=1
    )


def arrange_ids(pos, near, far):
    i32 = jnp.int32
    outs = [shaped((NA, 8), i32), shaped((8, 2 * NA), i32)]
    outs += [shaped((NB, 8), i32), shaped((8, 4 * NB), i32)]
    return call(ids_kernel, outs, near, far, pos=pos)


def arranged(pos, ref):
    zl, x = pos[0], pos[1]
    rows, quarters = [], []
    for k in range(4):
        a = lax.rem(x + k, 4)
        rows.append(ref[zl, pl.ds(pl.multiple_of(a * CA, CA), CA)])
        quarters.append(ref[2, pl.ds(pl.multiple_of(zl * NB + a * CB, CB), CB)])
    return jnp.concatenate(rows + quarters, axis=0)


def first_kernel(pos, inputs, gain, bias, normed, stream):
    v = arranged(pos, inputs).astype(f32)
    stream[:CA] = v[:CA]
    stream[CA:] = v[NA : NA + CB]
    mean = jnp.mean(v, axis=-1, keepdims=True)
    centred = v - mean
    var = jnp.mean(centred * centred, axis=-1, keepdims=True)
    out = centred * lax.rsqrt(var + norm_eps) * gain[0, 0:1] + bias[0, 0:1]
    normed[...] = out.astype(bf16)


def cotangent_kernel(pos, cotangent, qid_a, qid_b, low, grad, total):
    live = jnp.concatenate([qid_a[...], qid_b[...]], axis=0)[:, :1] >= 0
    v = jnp.where(live, arranged(pos, cotangent).astype(f32), 0.0)
    low[...] = v.astype(bf16)
    own = jnp.concatenate([v[:CA], v[NA : NA + CB]], axis=0)
    grad[...] = own
    total[...] = jnp.sum(own, axis=0, keepdims=True)


def place_kernel(pos, *refs):
    out = refs[4]
    for dz in range(2):
        zl = pos[0] if dz == 0 else 1 - pos[0]
        for k in range(4):
            a = lax.rem(pos[1] + k, 4)
            chunk = refs[k].at[dz]
            out[zl, pl.ds(pl.multiple_of(a * CA, CA), CA)] = chunk[:CA].astype(out.dtype)
            out[2, pl.ds(pl.multiple_of(zl * NB + a * CB, CB), CB)] = chunk[CA:].astype(out.dtype)


def placed_rows(pos, slots, dtype):
    return call(place_kernel, [shaped((3, NA, D), dtype)], *slots, pos=pos)[0]


def norm_kernel(layer, at, stream, own, r1, r2, r3, extra, gain, bias, x_out, n_out):
    x = stream[...] + (own[...] + r1[...].astype(f32) + r2[...].astype(f32) + r3[...].astype(f32))
    x = x + extra[layer : layer + 1]
    x_out[...] = x
    mean = jnp.mean(x, axis=-1, keepdims=True)
    centred = x - mean
    var = jnp.mean(centred * centred, axis=-1, keepdims=True)
    g, b = (ref[at[0], at[1] : at[1] + 1] for ref in (gain, bias))
    n_out[...] = (centred * lax.rsqrt(var + norm_eps) * g + b).astype(bf16)


def norm_step(layer, at, stream, got, extra, gain, bias):
    return call(
        functools.partial(norm_kernel, layer, at),
        [shaped((CHUNK, D), f32), shaped((CHUNK, D), bf16)],
        stream, *got, extra, gain, bias,
    )


def result_kernel(layer, stream, own, r1, r2, r3, extra, out):
    x = stream[...] + (own[...] + r1[...].astype(f32) + r2[...].astype(f32) + r3[...].astype(f32))
    out[...] = (x + extra[layer : layer + 1]).astype(bf16)


def norm_back_kernel(at, x_ref, own, r1, r2, r3, grad_ref, gain, out, low, sums):
    x = x_ref[...]
    d = own[...] + r1[...].astype(f32) + r2[...].astype(f32) + r3[...].astype(f32)
    mean = jnp.mean(x, axis=-1, keepdims=True)
    centred = x - mean
    var = jnp.mean(centred * centred, axis=-1, keepdims=True)
    r = lax.rsqrt(var + norm_eps)
    xh = centred * r
    e = d * gain[at[0], at[1] : at[1] + 1]
    inner = e - jnp.mean(e, axis=-1, keepdims=True)
    inner = inner - xh * jnp.mean(e * xh, axis=-1, keepdims=True)
    grad = grad_ref[...] + r * inner
    out[...] = grad
    low[...] = grad.astype(bf16)
    sums[0:1] = jnp.sum(d * xh, axis=0, keepdims=True)
    sums[1:2] = jnp.sum(d, axis=0, keepdims=True)
    sums[2:3] = jnp.sum(grad, axis=0, keepdims=True)


def norm_back(at, x, got, grad, gain):
    return call(
        functools.partial(norm_back_kernel, at),
        [shaped((CHUNK, D), f32), shaped((CHUNK, D), bf16), shaped((3, D), f32)],
        x, *got, grad, gain,
    )


def qkv_kernel(layer, n, *refs):
    chunks, (w0, wa, wb, bias0, bias1) = refs[:n], refs[n : n + 5]
    q_out, kv_out, part_out = refs[n + 5 : n + 8]
    nt = whole(chunks)
    if n > 1:
        refs[n + 8][...] = nt
    w1 = jnp.concatenate([wa[: 3 * CW // 2], wb[: 3 * CW // 2]], axis=0)
    for g, w, bias in ((0, w0[...], bias0), (1, w1, bias1)):
        qb = bias[layer : layer + 1, :CW]
        vb = bias[layer : layer + 1, V_AT : V_AT + CW]
        q_out[g] = (dot_nt(nt, w[:CW]) + qb).astype(bf16)
        key = dot_nt(w[CW : 2 * CW], nt).astype(bf16)
        value = (dot_nt(nt, w[2 * CW :]) + vb).T.astype(bf16)
        kv_out[g, 0] = key
        kv_out[g, 1] = value
        part_out[1 - g, 0] = key[:, NA:]
        part_out[1 - g, 1] = value[:, NA:]


def project(layer, chunks, own, far, biases):
    n = len(chunks)
    outs = [shaped((2, NT, CW), bf16), shaped((2, 2, CW, NT), bf16), shaped((2, 2, CW, NB), bf16)]
    if n > 1:
        outs.append(shaped((NT, D), bf16))
    got = call(functools.partial(qkv_kernel, layer, n), outs, *chunks, own, *far, *biases)
    return (*got[:3], got[3] if n > 1 else chunks[0])


def lane_mask(head):
    lane = lax.broadcasted_iota(jnp.int32, (1, CW), 1)
    return (lane < HEAD_DIM) if head == 0 else (lane >= HEAD_DIM)


def row_mask(head):
    place = lax.broadcasted_iota(jnp.int32, (CW, 1), 0)
    return (place < HEAD_DIM) if head == 0 else (place >= HEAD_DIM)


def masked(mask, value):
    return jnp.where(mask, value.astype(f32), 0.0).astype(bf16)


def probabilities(qm, keys, allowed):
    scores = jnp.where(allowed, dot(qm, keys) * SCALE, -1e30)
    expanded = jnp.exp(scores - jnp.max(scores, axis=-1, keepdims=True))
    return expanded * (1.0 / jnp.sum(expanded, axis=-1, keepdims=True))


def slot_mask(qid, kid):
    return (kid >= 0) & ((qid == kid) | (qid < 0))


def out_rows_of(refs):
    if len(refs) == 1:
        return refs[0][...]
    return jnp.concatenate([ref[3 * CW // 2 :] for ref in refs], axis=0)


def attend_kernel(first, count, blocks, n_out, *refs):
    n = len(blocks)
    q, kvs, (qid, kid, wo0) = refs[0], refs[1 : 1 + n], refs[1 + n : 4 + n]
    wo1 = out_rows_of(refs[4 + n : 4 + n + n_out])
    rest = refs[4 + n + n_out :]
    allowed = slot_mask(qid[:, :1], kid[:1])
    mixed_out = rest[0] if first == 0 else rest[1]
    total = None
    for g, wo in ((0, wo0), (1, wo1)):
        keys = jnp.concatenate([r[g, 0, :, b : b + m] for r, (b, m) in zip(kvs, blocks)], axis=1)
        values = jnp.concatenate([r[g, 1, :, b : b + m] for r, (b, m) in zip(kvs, blocks)], axis=1)
        query = q[g, first : first + count]
        mixed = None
        for head in range(2):
            mask = lane_mask(head)
            probs = probabilities(masked(mask, query), keys, allowed).astype(bf16)
            got = dot_nt(probs, values)
            mixed = got if head == 0 else jnp.where(mask, got, mixed)
        mixed = mixed.astype(bf16)
        mixed_out[g] = mixed
        part = dot(mixed, wo[...])
        total = part if total is None else total + part
    if first == 0:
        rest[1][...] = total
    else:
        put_sends(jnp.concatenate([rest[0][...], total], axis=0), rest[2:])


def attend_row(q, kvs, blocks, qid, kid, wo):
    return call(
        functools.partial(attend_kernel, 0, NA, blocks, len(wo) - 1),
        [shaped((2, NA, CW), bf16), shaped((NA, D), f32)],
        q, *kvs, qid, kid, *wo,
    )


def attend_quarter(q, kvs, blocks, qid, kid, wo, total):
    return call(
        functools.partial(attend_kernel, NA, NB, blocks, len(wo) - 1),
        [shaped((2, NB, CW), bf16), *SENDS],
        q, *kvs, qid, kid, *wo, total,
    )


def attend_back_kernel(*refs):
    c0, c1, c2, c3, q, kv, kvo, kvz, kvd, qid_a, kid_a, qid_b, kid_b, wo0 = refs[:14]
    wo1 = out_rows_of(refs[14:-5])
    mid_out, dq_out, own_out, far_out, z_out = refs[-5:]
    allowed_a = slot_mask(qid_a[:, :1], kid_a[:1])
    allowed_b = slot_mask(qid_b[:, :1], kid_b[:1])
    mid = whole((c0, c1, c2, c3))
    mid_out[...] = mid
    for g, wo in ((0, wo0), (1, wo1)):
        d_mixed = dot_nt(mid, wo[...]).astype(bf16)
        d_mixed_t = dot_nt(wo[...], mid).astype(bf16)
        query = q[g]
        query_t = query.astype(f32).T.astype(bf16)
        for part in range(2):
            if part == 0:
                allowed, lo, hi = allowed_a, 0, NA
                keys = jnp.concatenate([kv[g, 0, :, :NA], kvo[g, 0, :, :NA]], axis=1)
                values = jnp.concatenate([kv[g, 1, :, :NA], kvo[g, 1, :, :NA]], axis=1)
            else:
                allowed, lo, hi = allowed_b, NA, NT
                keys = jnp.concatenate(
                    [kv[g, 0, :, NA:], kvo[g, 0, :, NA:], kvz[g, 0], kvd[g, 0]], axis=1
                )
                values = jnp.concatenate(
                    [kv[g, 1, :, NA:], kvo[g, 1, :, NA:], kvz[g, 1], kvd[g, 1]], axis=1
                )
            dq, dk, dv = None, None, None
            for head in range(2):
                mask, rmask = lane_mask(head), row_mask(head)
                probs = probabilities(masked(mask, query[lo:hi]), keys, allowed)
                d_probs = dot(masked(mask, d_mixed[lo:hi]), values)
                inner = jnp.sum(d_probs * probs, axis=-1, keepdims=True)
                d_raw = (SCALE * probs * (d_probs - inner)).astype(bf16)
                got_q = dot_nt(keys, d_raw)
                got_k = dot(query_t[:, lo:hi], d_raw)
                got_v = dot(d_mixed_t[:, lo:hi], probs.astype(bf16))
                if head == 0:
                    dq, dk, dv = got_q, got_k, got_v
                else:
                    dq = jnp.where(rmask, got_q, dq)
                    dk = jnp.where(rmask, got_k, dk)
                    dv = jnp.where(rmask, got_v, dv)
            dq_out[g, :, lo:hi] = dq.astype(bf16)
            n = hi - lo
            for j, grad in ((0, dk), (1, dv)):
                own_out[g, j, :, lo:hi] = grad[:, :n]
                far_out[g, j, :, lo:hi] = grad[:, n : 2 * n].astype(bf16)
                if part == 1:
                    z_out[1 - g, j] = grad[:, 2 * n : 3 * n]
                    far_out[1 - g, j, :, NT:] = grad[:, 3 * n :].astype(bf16)


def attend_back(chunks, q, kv, kvo, kvz, kvd, ids, wo):
    return call(
        attend_back_kernel,
        [
            shaped((NT, D), bf16),
            shaped((2, CW, NT), bf16),
            shaped((2, 2, CW, NT), f32),
            shaped((2, 2, CW, NT + NB), bf16),
            shaped((2, 2, CW, NB), f32),
        ],
        *chunks, q, kv, kvo, kvz, kvd, *ids, *wo,
    )


def project_back_kernel(dq, own, far, dz, w0, wa, wb, stack_out, sums, *sends):
    total = None
    ones = jnp.ones((8, NT), bf16)
    w1 = jnp.concatenate([wa[: 3 * CW // 2], wb[: 3 * CW // 2]], axis=0)
    for g, w in ((0, w0[...]), (1, w1)):
        stack_out[g, 0] = dq[g]
        sums[g, 0] = dot_nt(ones, dq[g])
        for j in range(2):
            grad = own[g, j] + far[g, j, :, :NT].astype(f32)
            low = jnp.concatenate(
                [grad[:, :NA], grad[:, NA:] + dz[g, j].astype(f32)], axis=1
            ).astype(bf16)
            stack_out[g, 1 + j] = low
            if j == 1:
                sums[g, 1] = dot_nt(ones, low)
        for j in range(3):
            part = dot_tn(stack_out[g, j], w[CW * j : CW * (j + 1)])
            total = part if total is None else total + part
    put_sends(total, sends)


def project_back(dq, own, far, dz, w0, w1):
    return call(
        project_back_kernel,
        [shaped((2, 3, CW, NT), bf16), shaped((2, 2, 8, CW), f32), *SENDS],
        dq, own, far, dz, w0, *w1,
    )


def mlp_kernel(
    layer, c0, c1, c2, c3, bias0, bias1, wu0, wd0, wu1, wd1, nt_out, up_out, act_out, *sends
):
    nt = whole((c0, c1, c2, c3))
    nt_out[...] = nt
    total = None
    for g, wu, bias, wd in ((0, wu0, bias0, wd0), (1, wu1, bias1, wd1)):
        u = dot_nt(nt, wu[...]) + bias[layer : layer + 1, UP_AT : UP_AT + FP]
        up_out[g] = u
        act = (0.5 * u * (1.0 + jnp.tanh(gelu_coef * (u + 0.044715 * u * u * u)))).astype(bf16)
        act_out[g] = act
        part = dot(act, wd[...])
        total = part if total is None else total + part
    put_sends(total, sends)


def mlp(layer, chunks, own, oth, biases):
    return call(
        functools.partial(mlp_kernel, layer),
        [
            shaped((NT, D), bf16),
            shaped((2, NT, FP), f32),
            shaped((2, NT, FP), bf16),
            *SENDS,
        ],
        *chunks, *biases, own[2], own[3], oth[2], oth[3],
    )


def mlp_back_kernel(n, *refs):
    chunks, (up, wu0, wd0) = refs[:n], refs[n : n + 3]
    wu1, wd1 = refs[n + 3 : n + 5]
    d_up_out, sums = refs[n + 5 : n + 7]
    sends = refs[n + 7 : n + 11]
    low = whole(chunks)
    if n > 1:
        refs[n + 11][...] = low
    total = None
    for g, wu, wd in ((0, wu0, wd0), (1, wu1, wd1)):
        d_act = dot_nt(low, wd[...])
        u = up[g]
        t = jnp.tanh(gelu_coef * (u + 0.044715 * u * u * u))
        slope = 0.5 * (1.0 + t) + 0.5 * u * (1.0 - t * t) * (
            gelu_coef * (1.0 + 3 * 0.044715 * u * u)
        )
        d_up = (d_act * slope).astype(bf16)
        d_up_out[g] = d_up
        sums[g] = jnp.sum(d_up.astype(f32), axis=0, keepdims=True)
        part = dot(d_up, wu[...])
        total = part if total is None else total + part
    put_sends(total, sends)


def mlp_back(chunks, up, own, oth):
    n = len(chunks)
    outs = [shaped((2, NT, FP), bf16), shaped((2, 1, FP), f32), *SENDS]
    if n > 1:
        outs.append(shaped((NT, D), bf16))
    got = call(
        functools.partial(mlp_back_kernel, n), outs, *chunks, up, own[2], own[3], oth[2], oth[3]
    )
    return got[0], got[1], got[2:6], (got[6] if n > 1 else chunks[0])


def mlp_weights_kernel(pos, d_up, act, nt, low, keep_out, sent_out):
    first = pos[2] == 0
    for j, (a, b) in enumerate(((d_up, nt), (act, low))):
        for out, g in ((keep_out, 0), (sent_out, 1)):
            picked = jnp.where(first, a[g], a[1 - g])
            got = dot_tn(picked, b[...]).astype(bf16)
            for k in range(2):
                out[2 * j + k] = got[HF * k : HF * (k + 1)]


def attend_weights_kernel(
    pos, stacked, mixed_a, mixed_b, normed, mid, qv0, qv1, up0, up1, keep_out, sent_out, extra
):
    plain_weights_kernel(pos, stacked, mixed_a, mixed_b, normed, mid, keep_out, sent_out)
    first = pos[2] == 0
    for out, g in ((keep_out, 0), (sent_out, 1)):
        extra[...] = jnp.zeros_like(extra)
        for layer, (qv, up) in enumerate(((qv0, up0), (qv1, up1))):
            row = slice(4 + layer, 5 + layer)
            extra[row, :CW] = jnp.where(first, qv[g, 0, :1], qv[1 - g, 0, :1])
            extra[row, V_AT : V_AT + CW] = jnp.where(first, qv[g, 1, :1], qv[1 - g, 1, :1])
            extra[row, UP_AT : UP_AT + FP] = jnp.where(first, up[g], up[1 - g])
        for j in range(4):
            rows = extra[...] if j == 1 else jnp.zeros_like(extra)
            out[j, CW:] = rows.astype(bf16)


def plain_weights_kernel(pos, stacked, mixed_a, mixed_b, normed, mid, keep_out, sent_out):
    first = pos[2] == 0
    for out, g in ((keep_out, 0), (sent_out, 1)):
        for j in range(3):
            picked = jnp.where(first, stacked[g, j], stacked[1 - g, j])
            out[j, :CW] = dot(picked, normed[...]).astype(bf16)
        mixed = [jnp.concatenate([mixed_a[i], mixed_b[i]], axis=0) for i in (g, 1 - g)]
        out[3, :CW] = dot_tn(jnp.where(first, mixed[0], mixed[1]), mid[...]).astype(bf16)


def mlp_final_kernel(pos, *refs):
    first = pos[2] == 0
    for j, out in enumerate(refs[8:]):
        for layer in range(2):
            full, other = refs[4 * j + 2 * layer : 4 * j + 2 * layer + 2]
            out[:, layer, :] = jnp.where(first, full[...], other[...]).astype(f32)


def mlp_final(pos, sums):
    rows = HF
    args = [part for _ in range(2) for total in sums for part in total]
    specs = [pl.BlockSpec(memory_space=pltpu.SMEM)]
    for j in range(2):
        specs += [pl.BlockSpec((None, rows, D), lambda i, j=j: (2 * j + i, 0, 0))] * 4
    return pl.pallas_call(
        mlp_final_kernel,
        grid=(2,),
        out_shape=[shaped((FW, 2, D), f32)] * 2,
        in_specs=specs,
        out_specs=[pl.BlockSpec((rows, 2, D), lambda i: (i, 0, 0))] * 2,
        compiler_params=pltpu.CompilerParams(vmem_limit_bytes=VMEM_LIMIT),
    )(pos, *args)


def wide_kernel(one0, two0, one1, two1, down, out):
    rows = [one0[0:1], two0[0:1], one0[1:2], two0[1:3], one1[2:3]]
    rows += [one1[0:1], two1[0:1], one1[1:2], two1[1:3], down[...]]
    rows.append(jnp.zeros((2 * EXTRA - 12, D), f32))
    out[...] = jnp.concatenate(rows, axis=0).reshape(out.shape)


def attend_final_kernel(
    pos, full0, other0, full1, other1, qkv, out, gain, bias, q_bias, v_bias, out_bias, up, down
):
    first, j = pos[2] == 0, pl.program_id(0)
    got = [jnp.where(first, a[:CW], b[:CW]) for a, b in ((full0, other0), (full1, other1))]

    @pl.when(j < 3)
    def _():
        for layer in range(2):
            qkv[layer] = got[layer].astype(f32)

    @pl.when(j == 3)
    def _():
        for layer in range(2):
            out[layer] = got[layer].astype(f32)

    small = jnp.where(first, full0[CW:], other0[CW:]).astype(f32)

    @pl.when(j == 0)
    def _():
        gain[0], bias[0] = small[0:2], small[2:4]
        out_bias[0:1], down[0:1] = small[4:5], small[5:6]
        gain[1] = small[6:8]

    @pl.when(j == 1)
    def _():
        bias[1] = small[0:2]
        out_bias[1:2], down[1:2] = small[2:3], small[3:4]
        for layer in range(2):
            row = small[4 + layer : 5 + layer]
            q_bias[layer : layer + 1] = row[:, :CW]
            v_bias[layer : layer + 1] = row[:, V_AT : V_AT + CW]
            up[layer : layer + 1] = row[:, UP_AT : UP_AT + FW]


def attend_final(pos, sums):
    args = [part for total in sums for part in total]
    shapes = [(2, 2, D), (2, 2, D), (2, CW), (2, CW), (2, D), (2, FW), (2, D)]
    specs = [pl.BlockSpec(memory_space=pltpu.SMEM)]
    specs += [pl.BlockSpec((None, *arg.shape[1:]), lambda j: (j, 0, 0)) for arg in args]
    outs = [pl.BlockSpec((2, None, CW, D), lambda j: (0, jnp.minimum(j, 2), 0, 0))]
    outs.append(pl.BlockSpec((2, CW, D), lambda j: (0, 0, 0)))
    outs += [pl.BlockSpec(s, lambda j, n=len(s): (0,) * n) for s in shapes]
    return pl.pallas_call(
        attend_final_kernel,
        grid=(4,),
        out_shape=[shaped(s, f32) for s in ((2, 3, CW, D), (2, CW, D), *shapes)],
        in_specs=specs,
        out_specs=outs,
        compiler_params=pltpu.CompilerParams(vmem_limit_bytes=VMEM_LIMIT),
    )(pos, *args)


def gather_x(chunk):
    return [chunk] + [shift(chunk, "x", -k) for k in (1, 2, 3)]


def scatter_x(sends):
    return [sends[3]] + [shift(sends[k - 1], "x", k) for k in (1, 2, 3)]


def scatter_ring(pieces, axis):
    return [pieces[0]] + [shift(pieces[k], axis, k) for k in (1, 2, 3)]


def gather_ring(piece, axis, some):
    got = [piece]
    for k in (1, 2, 3):
        if not some:
            got.append(shift(piece, axis, -k))
        elif axis == "y":
            pairs = [
                (((y + k) % 4) * 4 + e, y * 4 + e) for y in range(4) for e in (0, 3)
            ]
            got.append(lax.ppermute(piece, ("y", "c", "zl"), pairs))
        else:
            pairs = []
            for z in range(4):
                c = z % 2
                src = (z + k) % 4
                pairs.append(
                    ((src // 2) * 4 + c * 2 + src % 2, (z // 2) * 4 + c * 2 + z % 2)
                )
            got.append(lax.ppermute(piece, ("zh", "c", "zl"), pairs))
    return got


def pieces_kernel(pos, kept, far, *outs):
    for k in range(4):
        block = lax.rem(pos[0] + k, 4)
        outs[k][...] = (kept[block].astype(f32) + far[block].astype(f32)).astype(bf16)


def sum_pieces(index, kept, far):
    outs = [shaped(kept.shape[1:], bf16)] * 4
    return call(pieces_kernel, outs, kept, far, pos=index)


def last_piece_kernel(pos, *refs):
    late, out = refs[-2:]
    total = sum(ref[...].astype(f32) for ref in refs[:4])
    out[:CW] = total[:CW].astype(bf16)
    rows = late[jnp.minimum(pos[0], 1)]
    out[CW:] = (total[CW:] + jnp.where(pos[0] < 2, rows, 0.0)).astype(bf16)


def total_kernel(*refs):
    refs[-1][...] = sum(ref[...].astype(f32) for ref in refs[:-1]).astype(bf16)


def sum_parts(*parts):
    return call(total_kernel, [shaped(parts[0].shape, bf16)], *parts)[0]


def blocks_kernel(pos, *refs):
    for k in range(4):
        refs[4][lax.rem(pos[0] + k, 4)] = refs[k][...]


def place_blocks(index, parts):
    return call(blocks_kernel, [shaped((4, *parts[0].shape), bf16)], *parts, pos=index)[0]


def sum_ring(value, axis):
    return value + sum(shift(value, axis, k) for k in range(1, SIZES[axis]))


def local(
    inputs,
    picture_ids,
    cotangent,
    norm_gain,
    norm_bias,
    w_qkv,
    q_bias,
    v_bias,
    w_out,
    out_bias,
    w_up,
    up_bias,
    w_down,
    down_bias,
):
    layers = w_qkv.shape[0]
    zl, c, x, y = (lax.axis_index(name) for name in ("zl", "c", "x", "y"))
    pos = jnp.stack([zl, x, jnp.where(zl == c, 0, 1)]).astype(jnp.int32)

    z_index = (lax.axis_index("zh") * 2 + zl)[None]
    here = picture_ids[0, 0] > -2

    def apart(work):
        shapes = jax.eval_shape(work)
        return lax.cond(
            here, work, lambda: jax.tree.map(lambda s: jnp.zeros(s.shape, s.dtype), shapes)
        )

    wq_t = jnp.swapaxes(w_qkv, 2, 3).reshape(layers, 3 * CW, D)
    half = 3 * CW // 2

    wq_far = [(shift(wq_t[0, :half], Z, 1), shift(wq_t[0, half:], Z, -1))]
    normed, stream = call(
        first_kernel, [shaped((NT, D), bf16), shaped((CHUNK, D), f32)],
        inputs, norm_gain, norm_bias, pos=pos,
    )
    w_out, w_up, w_down, q_bias, v_bias, up_bias = after(
        (w_out, w_up, w_down, q_bias, v_bias, up_bias), normed
    )
    bias = jnp.concatenate(
        [
            jnp.pad(part, ((0, 0), (0, size - part.shape[1])))
            for part, size in ((q_bias, V_AT), (v_bias, UP_AT - V_AT), (up_bias, FP))
        ],
        axis=1,
    )
    biases = (bias, shift(bias, "zl", 1))
    ids_far = shift(picture_ids, "c", 1)
    pad = ((0, FP - FW), (0, 0))
    wide_weights = [
        (jnp.pad(w_up[layer].T, pad), jnp.pad(w_down[layer], pad)) for layer in range(layers)
    ]
    out_far = [(shift(w_out[0], Z, 1),)]
    ids = arrange_ids(pos, picture_ids, ids_far)

    def far_wide(layer, anchor):
        up_rows, down_rows = after(wide_weights[layer], anchor)
        return shift(up_rows, Z, 1), shift(down_rows, Z, -1)

    def keys_step(layer, chunks):
        q, kv, part, normed = project(layer, chunks, Layer(wq_t, layer), wq_far[layer], biases)
        kvo = shift(kv, "c", 1)
        kvz = shift(part, "zl", 1)
        kvd = shift(kvz, "c", 1)
        wo = (Layer(w_out, layer), *out_far[layer])
        mixed_a, total_a = attend_row(q, (kv, kvo), ((0, NA), (0, NA)), ids[0], ids[1], wo)
        return q, kv, kvo, kvz, kvd, normed, wo, mixed_a, total_a

    def attention_step(layer, q, kv, kvo, kvz, kvd, wo, total_a, stream):
        mixed_b, *sends = attend_quarter(
            q, (kv, kvo, kvz, kvd), ((NA, NB), (NA, NB), (0, NB), (0, NB)),
            ids[2], ids[3], wo, total_a,
        )
        got = scatter_x(sends)
        middle, low = norm_step(layer, (layer, 1), stream, got, out_bias, norm_gain, norm_bias)
        return mixed_b, middle, gather_x(low)

    normed = after(normed, (wide_weights, ids))
    q, kv, kvo, kvz, kvd, normed, wo, mixed_a, total_a = keys_step(0, [normed])
    wide_far = [far_wide(0, (kvz, *out_far[0]))]
    def first_attention():
        split = (3 * CW + CW) // 2 - half
        sends = (
            jnp.concatenate([wq_t[1, :half], w_out[1, :split]], axis=0),
            jnp.concatenate([wq_t[1, half:], w_out[1, split:]], axis=0),
        )
        done = attention_step(0, q, kv, kvo, kvz, kvd, wo, total_a, stream)
        return done, sends

    (mixed_b, middle, chunks), next_sends = apart(first_attention)
    own = (Layer(wq_t, 0), Layer(w_out, 0), *wide_weights[0])
    weights = [(own, (wq_far[0], out_far[0], *wide_far[0]))]
    sent_up, sent_down = shift(next_sends[0], Z, 1), shift(next_sends[1], Z, -1)
    wq_far.append((sent_up, sent_down))
    out_far.append((sent_up, sent_down))

    def first_mlp():
        normed_two, up, act, *sends = mlp(0, chunks, *weights[0], biases)
        got = scatter_x(sends)
        stream, low = norm_step(0, (1, 0), middle, got, down_bias, norm_gain, norm_bias)
        return normed_two, up, act, stream, gather_x(low)

    normed_two, up, act, stream1, chunks1 = apart(first_mlp)
    kept = [(stream, normed, q, kv, kvo, kvz, kvd, mixed_a, mixed_b, middle, normed_two, up, act)]

    chunks1 = after(chunks1, wq_far[1])
    q1, kv1, kvo1, kvz1, kvd1, normed1, wo1, mixed_a1, total_a1 = keys_step(1, chunks1)
    wide_far.append(far_wide(1, (kvz1, total_a1)))

    def second_attention():
        low = call(
            cotangent_kernel,
            [shaped((NT, D), bf16), shaped((CHUNK, D), f32), shaped((1, D), f32)],
            cotangent, ids[0], ids[2], pos=pos,
        )
        return attention_step(1, q1, kv1, kvo1, kvz1, kvd1, wo1, total_a1, stream1), low

    (mixed_b1, middle1, chunks), (low_in, grad_flow, d_down_bias) = apart(second_attention)
    own = (Layer(wq_t, 1), Layer(w_out, 1), *wide_weights[1])
    weights.append((own, (wq_far[1], out_far[1], *wide_far[1])))
    normed_two, up, act, *last_sends = mlp(1, chunks, *weights[1], biases)
    kept.append(
        (stream1, normed1, q1, kv1, kvo1, kvz1, kvd1, mixed_a1, mixed_b1, middle1, normed_two, up, act)
    )

    def feed_forward_back(layer, chunks, grad_flow):
        own, oth = weights[layer]
        middle, normed_two, up, act = kept[layer][-4:]
        d_up, d_up_bias, sends, grad_low = mlp_back(chunks, up, own, oth)
        got = scatter_x(sends)
        kept_m, sent_m = call(
            mlp_weights_kernel, [shaped((4, HF, D), bf16)] * 2,
            d_up, act, normed_two, grad_low, pos=pos,
        )
        grad_mid, mid_low, norm_two = norm_back((layer, 1), middle, got, grad_flow, norm_gain)
        return grad_mid, mid_low, norm_two, d_up_bias, (kept_m, sent_m)

    def gather_mid(mid_low, *kept_and_sent):
        sums = [sum_parts(kept, shift(sent, "c", 1)) for kept, sent in kept_and_sent]
        return gather_x(mid_low), sums

    def attention_back(layer, mid_chunks, last_result=None):
        own, oth = weights[layer]
        q, kv, kvo, kvz, kvd = kept[layer][2:7]
        mid, dq, d_own, d_far, d_z = attend_back(
            mid_chunks, q, kv, kvo, kvz, kvd, ids, (own[1], *oth[1])
        )
        d_far = shift(d_far, "c", 1)
        d_z = shift((d_z + d_far[..., NT:].astype(f32)).astype(bf16), "zl", 1)
        result = None
        if last_result is not None:
            result = last_result()
            d_z = after(d_z, result)
        stacked, d_qv_bias, *sends = project_back(dq, d_own, d_far, d_z, own[0], oth[0])
        return mid, stacked, d_qv_bias, scatter_x(sends), result

    def last_result():
        return call(
            functools.partial(result_kernel, layers - 1), [shaped((CHUNK, D), bf16)],
            middle1, *scatter_x(last_sends), down_bias,
        )[0]

    grad_mid1, mid_low1, norm_two1, d_up_bias1, part_m1 = feed_forward_back(
        1, [low_in], grad_flow
    )
    mid_chunks1, (feed_m1,) = apart(lambda: gather_mid(mid_low1, part_m1))
    sum_m1 = lax.psum(feed_m1, ("y", "zh", "zl"))

    def first_block():
        stream_in, normed = kept[1][:2]
        mid, stacked, d_qv_bias, got, _ = attention_back(1, mid_chunks1)
        part_a = call(
            plain_weights_kernel, [shaped((4, CW, D), bf16)] * 2,
            stacked, *kept[1][7:9], normed, mid, pos=pos,
        )
        grad_flow, low, norm_one = norm_back((1, 0), stream_in, got, grad_mid1, norm_gain)
        chunks = gather_x(low)
        back = feed_forward_back(0, chunks, grad_flow)
        return d_qv_bias, norm_one, part_a, back

    d_qv_bias1, norm_one1, part_a1, back = apart(first_block)
    grad_mid0, mid_low0, norm_two0, d_up_bias0, part_m0 = back
    mid_chunks0, (feed_a1, feed_m0) = apart(lambda: gather_mid(mid_low0, part_a1, part_m0))
    sum_a1, sum_m0 = lax.psum((feed_a1, feed_m0), ("zh", "zl", "y"))

    def second_block():
        stream_in, normed = kept[0][:2]
        mid, stacked, d_qv_bias0, got, result = attention_back(0, mid_chunks0, last_result)
        part_a = call(
            attend_weights_kernel, [shaped((4, CW + EXTRA, D), bf16)] * 2,
            stacked, *kept[0][7:9], normed, mid, d_qv_bias0, d_qv_bias1, d_up_bias0, d_up_bias1,
            pos=pos, scratch=[pltpu.VMEM((EXTRA, D), f32)],
        )
        _, low, norm_one = norm_back((0, 0), stream_in, got, grad_mid0, norm_gain)
        pieces = sum_pieces(z_index, part_a[0], shift(part_a[1], "c", 1))
        return low, norm_one, pieces, result

    low, norm_one0, pieces, result = apart(second_block)

    def first_sums():
        parts = scatter_ring(pieces, Z)
        both = jnp.stack([low, shift(low, "zl", 1)])
        in_slots = gather_x(both)
        late = call(
            wide_kernel, [shaped((2, EXTRA, D), f32)],
            norm_one0, norm_two0, norm_one1, norm_two1, d_down_bias,
        )[0]
        late = sum_ring(late + shift(late, "c", 1), "x")
        late = sum_ring(after(late, parts), Z)
        piece = call(
            last_piece_kernel, [shaped((CW + EXTRA, D), bf16)], *parts, late, pos=z_index
        )[0]
        return in_slots, piece, jnp.stack([result, shift(result, "zl", 1)])

    in_slots, piece, results = apart(first_sums)

    def second_sums():
        parts = [piece] + [shift(piece, "y", k) for k in (1, 2, 3)]
        out_slots = gather_x(results)
        return sum_parts(*parts), out_slots

    total, out_slots = apart(second_sums)

    def last_sums():
        parts = gather_ring(total, Z, True)
        sums = [(part, shift(part, "c", 1)) for part in (sum_m0, sum_m1)]
        weight_grads = mlp_final(pos, sums)
        parts = after(parts, weight_grads)
        full = place_blocks(z_index, parts)
        input_grad = placed_rows(pos, in_slots, f32)
        outputs = placed_rows(pos, out_slots, bf16)
        other_a1 = shift(after(sum_a1, parts[1]), "c", 1)
        return input_grad, outputs, (full, shift(full, "c", 1)), (sum_a1, other_a1), weight_grads

    input_grad, outputs, sum_a0, sum_a1, (d_up, d_down) = apart(last_sums)
    d_qkv, d_out, d_gain, d_bias, d_q, d_v, d_out_bias, d_up_bias, d_down_bias = attend_final(
        pos, (sum_a0, sum_a1)
    )
    return (
        outputs,
        input_grad,
        d_gain,
        d_bias,
        jnp.swapaxes(d_qkv, 2, 3),
        d_q,
        d_v,
        d_out,
        d_out_bias,
        jnp.transpose(d_up, (1, 2, 0)),
        d_up_bias,
        jnp.transpose(d_down, (1, 0, 2)),
        d_down_bias,
    )


def solution(mesh):
    cut = Mesh(mesh.devices.reshape(4, 2, 2, 2, 4), ("y", "zh", "c", "zl", "x"))
    dp, tensor = ("y", "zh"), ("zl", "x")
    weight_specs = (
        P(),
        P(),
        P(None, None, None, tensor),
        P(None, tensor),
        P(None, tensor),
        P(None, tensor, None),
        P(),
        P(None, None, tensor),
        P(None, tensor),
        P(None, tensor, None),
        P(),
    )
    return jax.shard_map(
        local,
        mesh=cut,
        in_specs=(P(dp, "c", None), P(dp, "c"), P(dp, "c", None), *weight_specs),
        out_specs=(P(dp, "c", None), P(dp, "c", None), *weight_specs),
        check_vma=False,
    )
```
